32 devices in a mesh: batch: 16 (over z, x, core), seq: 2 (over y).
Axes of the slice: x: 2, y: 2, z: 4, core: 2. Of those that a mesh axis runs over, the one named last changes fastest.
Arguments:
- inputs: bfloat16 [16, 4096, 512], P('batch', 'seq'), may hold values from -6 to 6
- window_lengths: int32 [16, 9], P('batch'), may hold values from 0 to 1024, as said below
- conv_weight: bfloat16 [9, 512, 512], P(None, 'seq', 'batch'), may hold values from -0.09375 to 0.09375
- conv_bias: bfloat16 [512], P(('batch', 'seq')), may hold values from -3 to 3
- norm1_gain: bfloat16 [512], P(('batch', 'seq')), may hold values from 0.25 to 1.75
- norm1_bias: bfloat16 [512], P(('batch', 'seq')), may hold values from -2 to 2
- up_weight: bfloat16 [512, 2048], P('seq', 'batch'), may hold values from -0.25 to 0.25
- up_bias: bfloat16 [2048], P(('batch', 'seq')), may hold values from -3 to 3
- down_weight: bfloat16 [2048, 512], P('batch', 'seq'), may hold values from -0.125 to 0.125
- down_bias: bfloat16 [512], P(('batch', 'seq')), may hold values from -3 to 3
- norm2_gain: bfloat16 [512], P(('batch', 'seq')), may hold values from 0.25 to 1.75
- norm2_bias: bfloat16 [512], P(('batch', 'seq')), may hold values from -2 to 2
- out_grad: bfloat16 [16, 4096, 512], P('batch', 'seq'), may hold values from -6 to 6
Outputs:
- block_output: bfloat16 [16, 4096, 512], P('batch', 'seq')
- input_grad: float32 [16, 4096, 512], P('batch', 'seq')
- conv_weight_grad: float32 [9, 512, 512], P(None, 'seq', 'batch')
- conv_bias_grad: float32 [512], P(('batch', 'seq'))
- norm1_gain_grad: float32 [512], P(('batch', 'seq'))
- norm1_bias_grad: float32 [512], P(('batch', 'seq'))
- up_weight_grad: float32 [512, 2048], P('seq', 'batch')
- up_bias_grad: float32 [2048], P(('batch', 'seq'))
- down_weight_grad: float32 [2048, 512], P('batch', 'seq')
- down_bias_grad: float32 [512], P(('batch', 'seq'))
- norm2_gain_grad: float32 [512], P(('batch', 'seq'))
- norm2_bias_grad: float32 [512], P(('batch', 'seq'))
The draws below stay inside these ranges and needn't reach their ends.
Inputs may be any that keep to these rules, and one draw needn't show every extreme that they name: `window_lengths`: windows are 256, 512 or 1024 bases long. Each row begins with windows that fill one to three quarters of 1024, continues with whole windows of 1024 bases, and ends with zero or more shorter windows followed by at most 256 bases of padding; unused slots are 0 and come last.
All inputs are finite; a program needn't handle non-finite values.
Results may differ from the reference program's by a relative error of at most 0.008.
Values may be sent and summed in bfloat16 or wider, within the bound.
No kernel may reach another device: no remote copies, remote signals or barrier semaphores. Data moves between devices by JAX's collectives and lax.ppermute only.
A program may use at most 192 MiB of HBM per device.

```python
import math
import jax
import jax.numpy as jnp
from jax import lax

D = 512
FF = 2048
KERNEL_TAPS = 9
DILATION_STEP = 32
WIN = 1024
LENGTH = 4096
SLOTS = 9
ROWS = 16


LEAD_TAIL = [[1, 0, 0, 1, 2, 0], [1, 0, 0, 2, 1, 0], [1, 0, 0, 1, 1, 1], [1, 0, 0, 2, 0, 0], [1, 0, 0, 1, 1, 0], [2, 0, 0, 2, 0, 0], [2, 0, 0, 1, 1, 0], [2, 0, 0, 1, 0, 0], [1, 1, 0, 2, 0, 0], [1, 1, 0, 1, 1, 0], [1, 1, 0, 1, 0, 0], [1, 2, 0, 1, 0, 0], [1, 2, 0, 0, 0, 0], [2, 1, 0, 1, 0, 0], [2, 1, 0, 0, 0, 0], [1, 1, 1, 1, 0, 0], [1, 1, 1, 0, 0, 0]]


def draw_window_lengths(key, part):
    key = jax.random.fold_in(key, 7)
    table = jnp.array(LEAD_TAIL, dtype=jnp.int32)
    pick = jax.random.randint(key, (ROWS,), 0, table.shape[0])
    chosen = table[pick]
    whole_count = LENGTH // WIN - 1
    middle = jnp.full((ROWS, whole_count), 4, jnp.int32)
    row_slots = jnp.concatenate([chosen[:, :3], middle, chosen[:, 3:]], 1)
    order = jnp.argsort((row_slots == 0).astype(jnp.int32), axis=1, stable=True)
    row_slots = jnp.take_along_axis(row_slots, order, 1)
    return row_slots * (WIN // 4)


def with_spikes(entries, key, source, target, blocks, factor):
    owner, partner = [(jnp.arange(entries.shape[position]) // (entries.shape[position] // blocks)).reshape([-1 if axis == position else 1 for axis in range(entries.ndim)]) for position in (source, target)]
    chosen = jax.random.permutation(key, blocks)[partner]
    strong = (owner == chosen) | (owner == (partner + blocks // 2) % blocks)
    return jnp.where(strong, factor * entries, entries)


def levels(own_key, dims, cuts, least, high):
    def one(dim, shards_of):
        heights = jax.random.uniform(jax.random.fold_in(jax.random.fold_in(own_key, 6), dim), (shards_of,), jnp.float32, least / len(cuts), high / len(cuts))
        return jnp.repeat(jnp.exp(heights), dims[dim] // shards_of).reshape((-1,) + (1,) * (len(dims) - dim - 1))

    loudness = one(*cuts[0])
    for cut in cuts[1:]:
        loudness = loudness * one(*cut)
    return loudness


def noise(key, shape, width, reach, split=(), kind=jnp.bfloat16):
    values = jax.random.normal(key, shape, jnp.float32) * width
    if len(split) > 0:
        values = levels(key, shape, split, -0.22, 0.18) * values
    return jnp.clip(values, min=-reach, max=reach).astype(kind)


def heavy_noise(rng, dims, scale, most, cuts, heavy, kind=jnp.bfloat16):
    values = scale * jax.random.normal(rng, dims, jnp.float32)
    if cuts:
        values = values * levels(rng, dims, cuts, -0.22, 0.18)
    return jnp.clip(with_spikes(values, jax.random.fold_in(rng, 3), *heavy), -most, most).astype(kind)


def setup_inputs(seed: int = 0) -> dict:
    streams_of = jax.random.split(jax.random.key(seed), 14)
    inputs = noise(streams_of[0], (ROWS, LENGTH, D), 1.0, 6.0, ((0, 16), (1, 2)))
    window_lengths = draw_window_lengths(jax.random.fold_in(streams_of[13], 71), 0)
    conv_weight = noise(streams_of[2], (KERNEL_TAPS, D, D), (KERNEL_TAPS * D) ** -0.5, 0.09375, ((1, 2), (2, 16)))
    conv_bias = noise(streams_of[3], (D,), 0.5, 3.0, ((0, 32),))
    norm1_gain = jnp.clip(1.0 + 0.15 * jax.random.normal(streams_of[4], (D,), jnp.float32), 0.25, 1.75).astype(jnp.bfloat16)
    norm1_bias = noise(streams_of[5], (D,), 0.3, 2.0, ((0, 32),))
    up_weight = noise(streams_of[6], (D, FF), D ** -0.5, 0.25, ((0, 2), (1, 16)))
    up_bias = noise(streams_of[7], (FF,), 0.5, 3.0, ((0, 32),))
    down_weight = noise(streams_of[8], (FF, D), FF ** -0.5, 0.125, ((0, 16), (1, 2)))
    down_bias = noise(streams_of[9], (D,), 0.5, 3.0, ((0, 32),))
    norm2_gain = jnp.clip(1.0 + 0.15 * jax.random.normal(streams_of[10], (D,), jnp.float32), 0.25, 1.75).astype(jnp.bfloat16)
    norm2_bias = noise(streams_of[11], (D,), 0.3, 2.0, ((0, 32),))
    out_grad = heavy_noise(streams_of[12], (ROWS, LENGTH, D), 1.0, 6.0, ((0, 16), (1, 2)), (0, 2, 16, 2.0))
    return dict(inputs=inputs, window_lengths=window_lengths, conv_weight=conv_weight, conv_bias=conv_bias, norm1_gain=norm1_gain, norm1_bias=norm1_bias, up_weight=up_weight, up_bias=up_bias, down_weight=down_weight, down_bias=down_bias, norm2_gain=norm2_gain, norm2_bias=norm2_bias, out_grad=out_grad)


@jax.custom_vjp
def low(v):
    return lax.optimization_barrier(v.astype(jnp.bfloat16)).astype(jnp.float32)

@jax.custom_vjp
def low_back(v):
    return v

def low_keep(v):
    return (low(v), None)

def low_pass(kept, grad):
    return (grad,)

def back_keep(v):
    return (v, None)

def back_low(kept, grad):
    return (low(grad),)
low.defvjp(low_keep, low_pass)
low_back.defvjp(back_keep, back_low)
EPSILON = 1e-05
HIGHEST = lax.Precision.HIGHEST

def gelu_exact(values):
    return jax.nn.gelu(values, approximate=False)

def layer_norm(values, gain_vec, bias_vec):
    average = lax.optimization_barrier(jnp.mean(values, -1, keepdims=True))
    centered = values - average
    variance = lax.optimization_barrier(jnp.mean(centered * centered, -1, keepdims=True))
    return centered * lax.rsqrt(variance + EPSILON) * gain_vec + bias_vec

def window_layout(lengths_part):
    window_end = jnp.cumsum(lengths_part, axis=-1)
    positions = jnp.arange(LENGTH, dtype=jnp.int32)
    window_id = lax.optimization_barrier(jnp.sum((positions[None, :, None] >= window_end[:, None, :]).astype(jnp.int32), -1))
    valid_mask = (positions[None, :] < window_end[:, -1:]).astype(jnp.float32)
    return (window_id, valid_mask)

def block_forward(rows_in, lengths_part, conv_weight, conv_bias, norm1_gain, norm1_bias, up_weight, up_bias, down_weight, down_bias, norm2_gain, norm2_bias):
    window_id, valid_mask = window_layout(lengths_part)
    masked = rows_in * valid_mask[..., None]
    border_width = KERNEL_TAPS // 2 * DILATION_STEP
    padded = jnp.pad(masked, ((0, 0), (border_width, border_width), (0, 0)))
    padded_id = jnp.pad(window_id, ((0, 0), (border_width, border_width)), constant_values=-1)
    pieces = []
    for kernel_tap_index in range(KERNEL_TAPS):
        start_offset = kernel_tap_index * DILATION_STEP
        same_window = (padded_id[:, start_offset:start_offset + LENGTH] == window_id).astype(jnp.float32)
        pieces.append(padded[:, start_offset:start_offset + LENGTH] * same_window[..., None])
    stacked = jnp.stack(pieces, 2)
    conv_out = jnp.einsum('rtki,kio->rto', stacked, conv_weight, precision=HIGHEST) + conv_bias
    conv_out = low_back(conv_out)
    hidden_one = rows_in + layer_norm(gelu_exact(conv_out), norm1_gain, norm1_bias)
    up_out = jnp.einsum('rti,if->rtf', low(hidden_one), up_weight, precision=HIGHEST) + up_bias
    up_out = low_back(up_out)
    activated = low(gelu_exact(up_out))
    down_out = jnp.einsum('rtf,fo->rto', activated, down_weight, precision=HIGHEST) + down_bias
    down_out = low_back(down_out)
    return hidden_one + layer_norm(down_out, norm2_gain, norm2_bias)

def reference(inputs, window_lengths, conv_weight, conv_bias, norm1_gain, norm1_bias, up_weight, up_bias, down_weight, down_bias, norm2_gain, norm2_bias, out_grad):
    params = tuple((p.astype(jnp.float32) for p in (conv_weight, conv_bias, norm1_gain, norm1_bias, up_weight, up_bias, down_weight, down_bias, norm2_gain, norm2_bias)))
    group_rows = math.gcd(ROWS, max(1, 4096 // LENGTH))
    group_count = ROWS // group_rows

    def one_group(totals, pieces):
        rows_in, lengths_part, grad_in = pieces

        def forward(rows_f, *weights):
            return block_forward(rows_f, lengths_part, *weights)
        result, pullback = jax.vjp(forward, rows_in.astype(jnp.float32), *params)
        grads = pullback(grad_in.astype(jnp.float32))
        totals = tuple((a + b for a, b in zip(totals, grads[1:])))
        return (totals, (result.astype(jnp.bfloat16), grads[0]))
    initial = tuple((jnp.zeros(p.shape, jnp.float32) for p in params))
    totals, (outputs, input_grads) = lax.scan(one_group, initial, (inputs.reshape(group_count, group_rows, LENGTH, D), window_lengths.reshape(group_count, group_rows, SLOTS), out_grad.reshape(group_count, group_rows, LENGTH, D)))
    return (outputs.reshape(ROWS, LENGTH, D), input_grads.reshape(ROWS, LENGTH, D), totals[0], totals[1], totals[2], totals[3], totals[4], totals[5], totals[6], totals[7], totals[8], totals[9])
```

```python
import functools
import jax
import jax.numpy as jnp
from jax import lax
from jax.experimental import pallas as pl
from jax.experimental.pallas import tpu as pltpu
from jax.sharding import PartitionSpec as P

KERNEL_TAPS = 9
DILATION_STEP = 32
EPSILON = 1e-05
SUB = 256
BF = jnp.bfloat16
F32 = jnp.float32
NN = (((1,), (0,)), ((), ()))
NT = (((1,), (1,)), ((), ()))
TN = (((0,), (0,)), ((), ()))


def dot(a, b, dims):
    return lax.dot_general(a, b, dims, preferred_element_type=F32)


def conv_cost(count, width):
    return pl.CostEstimate(flops=2 * count * KERNEL_TAPS * width * width, bytes_accessed=2**24, transcendentals=0)


def gelu_pair(v):
    size = jnp.abs(v)
    t = pl.reciprocal(1.0 + 0.23164189 * size, approx=True)
    poly = t * (0.127414796 + t * (-0.142248368 + t * (0.710706871 + t * (-0.726576013 + t * 0.530702714))))
    bell = jnp.exp2(-0.72134752 * (size * size))
    value = jnp.maximum(v, 0.0) - size * (poly * bell)
    low_side = bell * (poly - 0.39894228 * size)
    return value, jnp.where(v >= 0.0, 1.0 - low_side, low_side)


def row_mean(v):
    return jnp.sum(v, -1, keepdims=True) * (1.0 / v.shape[-1])


def fold(v):
    total = v[0:8]
    for r in range(8, v.shape[0], 8):
        total = total + v[r : r + 8]
    return total


def fill_columns(col, load, flags, block, subs, width):
    for r in range(subs):
        j = block * subs + r
        base = j * SUB
        own = flags[2, j].astype(F32).astype(BF)
        before = flags[0, j].astype(F32).astype(BF)
        after = flags[1, j].astype(F32).astype(BF)
        for k in range(KERNEL_TAPS):
            o = (k - KERNEL_TAPS // 2) * DILATION_STEP
            columns = slice(k * width, (k + 1) * width)
            first = r * SUB
            if o < 0:
                col[first : first - o, columns] = load(base + o, -o) * before
                col[first - o : first + SUB, columns] = load(base, SUB + o) * own
            elif o == 0:
                col[first : first + SUB, columns] = load(base, SUB) * own
            else:
                col[first : first + SUB - o, columns] = load(base + o, SUB - o) * own
                col[first + SUB - o : first + SUB, columns] = load(base + SUB, o) * after


def conv_kernel(subs, flags, prev, x, nxt, w, bias, xhat_out, scale_out, ext, col):
    block = pl.program_id(0)
    width = x.shape[1]
    border = prev.shape[0]

    @pl.when(block == 0)
    def _():
        ext[0:border] = prev[...]
        ext[border : border + x.shape[0]] = x[...]
        ext[border + x.shape[0] :] = nxt[...]

    def load(start, count):
        return ext[pl.ds(pl.multiple_of(start + border, DILATION_STEP), count), :]

    fill_columns(col, load, flags, block, subs, width)
    total = None
    for k in range(KERNEL_TAPS):
        part = dot(col[:, k * width : (k + 1) * width], w[k], NT)
        total = part if total is None else total + part
    value, slope = gelu_pair(total + bias[...])
    centered = value - row_mean(value)
    rstd = lax.rsqrt(row_mean(centered * centered) + EPSILON)
    xhat_out[...] = centered * rstd
    scale_out[...] = slope * rstd


def conv_forward(flags, prev, x, nxt, w, bias, subs):
    count, width = x.shape
    rows = subs * SUB
    whole = lambda shape: pl.BlockSpec(shape, lambda j, f: (0,) * len(shape), pipeline_mode=pl.Buffered(1))
    return pl.pallas_call(
        functools.partial(conv_kernel, subs),
        grid_spec=pltpu.PrefetchScalarGridSpec(
            num_scalar_prefetch=1,
            grid=(count // rows,),
            in_specs=[whole(prev.shape), whole(x.shape), whole(nxt.shape), whole(w.shape), whole(bias.shape)],
            out_specs=[pl.BlockSpec((rows, width), lambda j, f: (j, 0))] * 2,
            scratch_shapes=[
                pltpu.VMEM((count + 2 * prev.shape[0], width), BF),
                pltpu.VMEM((rows, KERNEL_TAPS * width), BF),
            ],
        ),
        out_shape=[jax.ShapeDtypeStruct((count, width), F32)] * 2,
        compiler_params=pltpu.CompilerParams(vmem_limit_bytes=56 * 2**20),
        cost_estimate=conv_cost(count, width),
        name="conv_forward",
    )(flags, prev, x, nxt, w, bias)


def ffn_kernel(chunk, fast, core, x, xhat, scale, og, pair, ub, vec, out, gh_out, gc_out, *rest):
    act, slope, dup, ddown, sums, ub_sums = rest[-6:]
    step = pl.program_id(0)
    last = pl.num_programs(0) - 1
    _, hidden, width = pair.shape
    chunks = hidden // chunk
    gain1, shift1, db, gain2, shift2 = (vec[i : i + 1, :] for i in range(5))

    @pl.when(step == 0)
    def _():
        dup[...] = jnp.zeros_like(dup)
        ddown[...] = jnp.zeros_like(ddown)
        sums[...] = jnp.zeros_like(sums)
        ub_sums[...] = jnp.zeros_like(ub_sums)

    one = x[...].astype(F32) + (xhat[...] * gain1 + shift1)
    low = one.astype(BF)
    total = None
    for f in range(chunks):
        cols = slice(f * chunk, (f + 1) * chunk)
        value, s = gelu_pair(dot(low, pair[0, cols, :], NT) + ub[:, cols])
        a = value.astype(BF)
        act[:, cols] = a
        slope[:, cols] = s
        part = dot(a, pair[1, cols, :], NN)
        total = part if total is None else total + part
    d = total + db
    centered = d - row_mean(d)
    rstd = lax.rsqrt(row_mean(centered * centered) + EPSILON)
    hat = centered * rstd
    out[...] = (one + (hat * gain2 + shift2)).astype(BF)
    g = og[...].astype(F32)
    e = g * gain2
    gd = (rstd * (e - row_mean(e) - hat * row_mean(e * hat))).astype(BF)
    sums[0] += fold(g * hat)
    sums[1] += fold(g)
    sums[2] += fold(gd.astype(F32))
    gh = g
    for f in range(chunks):
        cols = slice(f * chunk, (f + 1) * chunk)
        ddown[:, cols] += dot(gd, act[:, cols], TN)
        gu = dot(gd, pair[1, cols, :], NT) * slope[:, cols]
        gul = gu.astype(BF)
        ub_sums[:, cols] += fold(gul.astype(F32))
        dup[:, cols] += dot(low, gul, TN)
        gh = gh + dot(gul, pair[0, cols, :], NN)
    gh_out[...] = gh
    sums[3] += fold(gh * xhat[...])
    sums[4] += fold(gh)
    e = gh * gain1
    gc = (scale[...] * (e - row_mean(e) - xhat[...] * row_mean(e * xhat[...]))).astype(BF)
    gc_out[...] = gc
    sums[5] += fold(gc.astype(F32))

    @pl.when(step == last)
    def _():
        if not fast:
            up_out, down_out, sums_out, ub_out = rest[:4]
            up_out[...] = dup[...]
            down_out[...] = ddown[...]
            sums_out[...] = jnp.sum(sums[...], 1)
            ub_out[...] = jnp.sum(ub_sums[...], 0, keepdims=True)
            return
        up_send, up_keep, down_send, down_keep = rest[:4]
        mine = core[0] == 0
        block = up_send.shape[3]
        half = width // 2
        devices = 2 * (hidden // block)

        def own(length):
            each = length // devices
            place = lax.broadcasted_iota(jnp.int32, (devices, length), 1) // each
            return place == lax.broadcasted_iota(jnp.int32, (devices, length), 0)

        def pick(length, start):
            each = length // devices
            place = lax.broadcasted_iota(jnp.int32, (length, 128), 0) % each + start
            return (place == lax.broadcasted_iota(jnp.int32, (length, 128), 1)).astype(BF)

        first = None
        for v in range(6):
            line = jnp.sum(sums[v], 0, keepdims=True)
            part = dot(jnp.where(own(width), line, 0.0).astype(BF), pick(width, v * (width // devices)), NN)
            first = part if first is None else first + part
        line = jnp.sum(ub_sums[...], 0, keepdims=True)
        second = dot(jnp.where(own(hidden), line, 0.0).astype(BF), pick(hidden, 0), NN)
        index = lax.broadcasted_iota(jnp.int32, (16, 128), 0)

        def tail(b, s):
            at = 2 * b + s
            return jnp.where(index == 0, first[at : at + 1], jnp.where(index == 1, second[at : at + 1], 0.0)).astype(BF)

        for z in range(up_send.shape[0]):
            for s in range(2):
                take = slice(s * half, (s + 1) * half)
                for acc, send, keep in ((dup, up_send, up_keep), (ddown, down_send, down_keep)):
                    lo = acc[take, 2 * z * block : (2 * z + 1) * block].astype(BF)
                    hi = acc[take, (2 * z + 1) * block : (2 * z + 2) * block].astype(BF)
                    send[z, s, 0:half] = jnp.where(mine, hi, lo)
                    keep[z, s, 0:half] = jnp.where(mine, lo, hi)
                lo, hi = tail(2 * z, s), tail(2 * z + 1, s)
                up_send[z, s, half:] = jnp.where(mine, hi, lo)
                up_keep[z, s, half:] = jnp.where(mine, lo, hi)


def ffn(core, x, xhat, scale, og, pair, ub, vec, rows, chunk, batch, fast):
    count, width = x.shape
    hidden = pair.shape[1]
    whole = lambda shape: pl.BlockSpec(shape, lambda j, f: (0,) * len(shape), pipeline_mode=pl.Buffered(1))
    tile = pl.BlockSpec((rows, width), lambda j, f: (j, 0))
    sds = jax.ShapeDtypeStruct
    if fast:
        shapes = [sds((batch // 2, 2, width // 2 + extra, hidden // batch), BF) for extra in (16, 16, 0, 0)]
    else:
        shapes = [sds(s, F32) for s in ((width, hidden), (width, hidden), (6, width), (1, hidden))]
    return pl.pallas_call(
        functools.partial(ffn_kernel, chunk, fast),
        grid_spec=pltpu.PrefetchScalarGridSpec(
            num_scalar_prefetch=1,
            grid=(count // rows,),
            in_specs=[tile, tile, tile, tile, whole(pair.shape), whole(ub.shape), whole(vec.shape)],
            out_specs=[tile, tile, tile] + [whole(s.shape) for s in shapes],
            scratch_shapes=[
                pltpu.VMEM((rows, hidden), BF),
                pltpu.VMEM((rows, hidden), F32),
                pltpu.VMEM((width, hidden), F32),
                pltpu.VMEM((width, hidden), F32),
                pltpu.VMEM((6, 8, width), F32),
                pltpu.VMEM((8, hidden), F32),
            ],
        ),
        out_shape=[sds((count, width), BF), sds((count, width), F32), sds((count, width), BF)] + shapes,
        compiler_params=pltpu.CompilerParams(vmem_limit_bytes=60 * 2**20),
        cost_estimate=pl.CostEstimate(flops=12 * count * width * hidden, bytes_accessed=2**25, transcendentals=0),
        name="feed_forward",
    )(core, x, xhat, scale, og, pair, ub, vec)


def conv_weight_kernel(fast, flags, prev, x, nxt, g, *rest):
    ext, col = rest[-2:]
    tap = pl.program_id(0)
    count, width = x.shape
    border = prev.shape[0]
    subs = count // SUB

    @pl.when(tap == 0)
    def _():
        ext[0:border] = prev[...]
        ext[border : border + count] = x[...]
        ext[border + count :] = nxt[...]

    o = (tap - KERNEL_TAPS // 2) * DILATION_STEP
    place = lax.broadcasted_iota(jnp.int32, (SUB, 1), 0) + o
    for r in range(subs):
        own = flags[2, r].astype(F32)
        before = flags[0, r].astype(F32)
        after = flags[1, r].astype(F32)
        mask = jnp.where(place < 0, before, jnp.where(place >= SUB, after, own)).astype(BF)
        rows = ext[pl.ds(pl.multiple_of(r * SUB + o + border, DILATION_STEP), SUB), :]
        col[r * SUB : (r + 1) * SUB, :] = rows * mask
    grad = dot(g[...], col[...], TN)
    if not fast:
        rest[0][0] = grad
        return
    send, keep = rest[:2]
    mine = flags[3, 0] == 0
    block = send.shape[3]
    half = width // 2
    for s in range(2):
        for z in range(send.shape[2]):
            lo = grad[2 * z * block : (2 * z + 1) * block, s * half : (s + 1) * half].astype(BF)
            hi = grad[(2 * z + 1) * block : (2 * z + 2) * block, s * half : (s + 1) * half].astype(BF)
            send[s, 0, z] = jnp.where(mine, hi, lo)
            keep[s, 0, z] = jnp.where(mine, lo, hi)


def conv_weight_backward(flags, prev, x, nxt, g, batch, fast):
    count, width = x.shape
    whole = lambda shape: pl.BlockSpec(shape, lambda j, f: (0,) * len(shape), pipeline_mode=pl.Buffered(1))
    if fast:
        part = (2, KERNEL_TAPS, batch // 2, width // batch, width // 2)
        specs = [pl.BlockSpec((2, 1) + part[2:], lambda k, f: (0, k, 0, 0, 0))] * 2
        shapes = [jax.ShapeDtypeStruct(part, BF)] * 2
    else:
        specs = [pl.BlockSpec((1, width, width), lambda k, f: (k, 0, 0))]
        shapes = [jax.ShapeDtypeStruct((KERNEL_TAPS, width, width), F32)]
    return pl.pallas_call(
        functools.partial(conv_weight_kernel, fast),
        grid_spec=pltpu.PrefetchScalarGridSpec(
            num_scalar_prefetch=1,
            grid=(KERNEL_TAPS,),
            in_specs=[whole(prev.shape), whole(x.shape), whole(nxt.shape), whole(g.shape)],
            out_specs=specs,
            scratch_shapes=[pltpu.VMEM((count + 2 * prev.shape[0], width), BF), pltpu.VMEM((count, width), BF)],
        ),
        out_shape=shapes,
        compiler_params=pltpu.CompilerParams(vmem_limit_bytes=56 * 2**20),
        cost_estimate=conv_cost(count, width),
        name="conv_weight_backward",
    )(flags, prev, x, nxt, g)


def conv_input_kernel(subs, flags, prev, g, nxt, w, gh, out, ext, col):
    block = pl.program_id(0)
    count, width = g.shape
    border = prev.shape[0]

    @pl.when(block == 0)
    def _():
        ext[0:border] = prev[...]
        ext[border : border + count] = g[...]
        ext[border + count :] = nxt[...]

    def load(start, size):
        return ext[pl.ds(pl.multiple_of(start + border, DILATION_STEP), size), :]

    fill_columns(col, load, flags, block, subs, width)
    total = gh[...]
    for k in range(KERNEL_TAPS):
        total = total + dot(col[:, k * width : (k + 1) * width], w[KERNEL_TAPS - 1 - k], NN)
    out[...] = total


def conv_input_backward(flags, prev, g, nxt, w, gh, subs):
    count, width = g.shape
    rows = subs * SUB
    whole = lambda shape: pl.BlockSpec(shape, lambda j, f: (0,) * len(shape), pipeline_mode=pl.Buffered(1))
    tile = pl.BlockSpec((rows, width), lambda j, f: (j, 0))
    return pl.pallas_call(
        functools.partial(conv_input_kernel, subs),
        grid_spec=pltpu.PrefetchScalarGridSpec(
            num_scalar_prefetch=1,
            grid=(count // rows,),
            in_specs=[whole(prev.shape), whole(g.shape), whole(nxt.shape), whole(w.shape), tile],
            out_specs=tile,
            scratch_shapes=[
                pltpu.VMEM((count + 2 * prev.shape[0], width), BF),
                pltpu.VMEM((rows, KERNEL_TAPS * width), BF),
            ],
        ),
        out_shape=jax.ShapeDtypeStruct((count, width), F32),
        compiler_params=pltpu.CompilerParams(vmem_limit_bytes=56 * 2**20),
        cost_estimate=conv_cost(count, width),
        name="conv_input_backward",
    )(flags, prev, g, nxt, w, gh)


def swap(value, axis, bit):
    count = lax.axis_size(axis)
    return lax.ppermute(value, axis, [(i, i ^ bit) for i in range(count)])


def half_of(axis, bit):
    return (lax.axis_index(axis) // bit) % 2


def exchange(value, axis, bit, dim):
    mine = half_of(axis, bit)
    give = lax.dynamic_index_in_dim(value, 1 - mine, dim, keepdims=False).astype(BF)
    keep = lax.dynamic_index_in_dim(value, mine, dim, keepdims=False).astype(F32)
    return keep + swap(give, axis, bit).astype(F32)


def gather_pieces(own, batch, seq):
    offsets = [(0, 0)]
    bit = batch // 2
    while bit >= 4:
        own = jnp.concatenate([own, swap(own, "batch", bit)], 0)
        offsets += [(b ^ bit, s) for b, s in offsets]
        bit //= 2
    cut = own.shape[1] // 32 * 16
    over_x = swap(own, "batch", 2)
    over_y = swap(own, "seq", 1)
    top = swap(over_x[:, :cut], "seq", 1)
    bottom = swap(over_y[:, cut:], "batch", 2)
    return [own, over_x, over_y, top, bottom], offsets, cut


def assemble_kernel(pieces, taps, rows, small, where, *refs):
    count = len(pieces)
    sources, targets, stash = refs[:count], refs[count : count + 1 + bool(small)], refs[count + 1 + bool(small) :]
    whole = targets[0]
    wide = sources[0].shape[2]
    if small:
        stash[0][...] = jnp.zeros_like(stash[0])
    for source, (offsets, first) in zip(sources, pieces):
        size = source.shape[1]
        for n, (db, ds) in enumerate(offsets):
            b = where[0] ^ db
            s = where[1] ^ ds
            columns = pl.ds(pl.multiple_of(s * wide, wide), wide)
            at = first
            while at < first + size:
                if at >= taps * rows:
                    row = source[n, at - first : at - first + 1, :].astype(F32) if at == taps * rows else None
                    if row is not None:
                        stash[0][pl.ds(2 * b + s, 1), :] = row
                    break
                tap = at // rows
                upto = min(first + size, (tap + 1) * rows)
                inside = at - tap * rows
                whole[tap, pl.ds(pl.multiple_of(b * rows + inside, 16), upto - at), columns] = source[n, at - first : upto - first, :]
                at = upto
    if small:
        table = stash[0][...]
        out = targets[1]
        devices = table.shape[0]
        for v, (start, each, row) in enumerate(small):
            length = devices * each
            pick = (
                lax.broadcasted_iota(jnp.int32, (wide, length), 1) % each + start
                == lax.broadcasted_iota(jnp.int32, (wide, length), 0)
            ).astype(BF)
            spread = dot(table.astype(BF), pick, NN)
            own = lax.broadcasted_iota(jnp.int32, (devices, length), 1) // each == lax.broadcasted_iota(
                jnp.int32, (devices, length), 0
            )
            out[row : row + 1, :length] = jnp.sum(jnp.where(own, spread, 0.0), 0, keepdims=True)


def assemble(where, arrays, pieces, taps, rows, batch, small, width):
    shape = (taps, rows * batch, arrays[0].shape[2] * 2)
    out_shape = [jax.ShapeDtypeStruct(shape, BF)]
    scratch = []
    if small:
        out_shape.append(jax.ShapeDtypeStruct((8, width), F32))
        scratch.append(pltpu.VMEM((2 * batch, arrays[0].shape[2]), F32))
    return pl.pallas_call(
        functools.partial(assemble_kernel, pieces, taps, rows, small),
        grid_spec=pltpu.PrefetchScalarGridSpec(
            num_scalar_prefetch=1,
            grid=(1,),
            in_specs=[pl.BlockSpec(a.shape, lambda i, f: (0, 0, 0)) for a in arrays],
            out_specs=[pl.BlockSpec(o.shape, lambda i, f, n=len(o.shape): (0,) * n) for o in out_shape],
            scratch_shapes=scratch,
        ),
        out_shape=out_shape,
        compiler_params=pltpu.CompilerParams(vmem_limit_bytes=56 * 2**20),
        name="assemble",
    )(where, *arrays)


def gather_whole(where, own, taps, rows, batch, seq, small, width):
    arrays, offsets, cut = gather_pieces(own, batch, seq)
    shift = lambda b, s: tuple((ob ^ b, os ^ s) for ob, os in offsets)
    plans = [(shift(0, 0), 0), (shift(2, 0), 0), (shift(0, 1), 0), (shift(2, 1), 0), (shift(2, 1), cut)]
    others = [swap(a, "batch", 1) for a in arrays]
    plans = plans + [(tuple((b ^ 1, s) for b, s in o), first) for o, first in plans]
    return assemble(where, arrays + others, tuple(plans), taps, rows, batch, small, width)


def local(inputs, window_lengths, conv_weight, conv_bias, norm1_gain, norm1_bias, up_weight, up_bias, down_weight,
          down_bias, norm2_gain, norm2_bias, out_grad):
    _, count, width = inputs.shape
    batch, seq = lax.axis_size("batch"), lax.axis_size("seq")
    hidden = up_weight.shape[1] * batch
    border = KERNEL_TAPS // 2 * DILATION_STEP
    my_batch, my_seq = lax.axis_index("batch"), lax.axis_index("seq")
    x, og = inputs[0], out_grad[0]

    def ends(value):
        first, final = value[:border], value[count - border :]
        if seq == 2:
            other = swap(jnp.where(my_seq == 0, final, first), "seq", 1)
            return other, other
        up = [(i, i + 1) for i in range(seq - 1)]
        return lax.ppermute(final, "seq", up), lax.ppermute(first, "seq", [(j, i) for i, j in up])

    lengths = window_lengths[0]
    slots = lengths.shape[0]
    window_end = jnp.sum(jnp.where(jnp.arange(slots)[:, None] >= jnp.arange(slots)[None, :], lengths[None, :], 0), 1)
    subs = count // SUB
    starts = my_seq * count + (jnp.arange(subs + 2, dtype=jnp.int32) - 1) * SUB
    ids = jnp.sum((starts[:, None] >= window_end[None, :]).astype(jnp.int32), 1)
    inside = (ids < slots).astype(jnp.int32)[1:-1]
    same = ((ids[1:] == ids[:-1]) & (starts[:-1] >= 0)).astype(jnp.int32)
    core = jnp.full((subs,), my_batch % 2, jnp.int32)
    flags = jnp.stack([same[:-1] * inside, same[1:] * inside, inside, core])

    prev, nxt = ends(x)
    vectors = [conv_bias, norm1_gain, norm1_bias, down_bias, norm2_gain, norm2_bias, up_bias]
    rows = width // batch
    hidden_rows = hidden // batch
    conv_own = conv_weight.transpose(0, 2, 1)
    pair_own = jnp.stack([up_weight.T, down_weight])
    if seq == 2:
        where = jnp.stack([my_batch, my_seq]).astype(jnp.int32)
        wide = conv_own.shape[2]
        each = [v.shape[0] for v in vectors]
        tail = jnp.concatenate(vectors + [jnp.zeros((16 * wide - sum(each),), BF)]).reshape(16, wide)
        conv_block = jnp.concatenate([conv_own.reshape(-1, wide), tail], 0)[None]
        small = []
        for i, n in enumerate(each):
            small.append((sum(each[:i]), n, i))
        conv_full, table = gather_whole(where, conv_block, KERNEL_TAPS, rows, batch, seq, tuple(small), hidden)
        (pair_full,) = gather_whole(
            where, pair_own.reshape(1, -1, wide), 2, hidden_rows, batch, seq, (), hidden
        )
        conv_bias_row = table[0:1, :width]
        vec = jnp.concatenate([table[1:6, :width], jnp.zeros((3, width), F32)])
        up_bias_row = table[6:7]
    else:
        def every(value, dims):
            value = lax.all_gather(value, "seq", axis=dims[0], tiled=True)
            return lax.all_gather(value, "batch", axis=dims[1], tiled=True)
        conv_full = every(conv_own, (2, 1))
        pair_full = every(pair_own, (2, 1))
        full = [lax.all_gather(v, ("batch", "seq"), axis=0, tiled=True).astype(F32) for v in vectors]
        conv_bias_row = full[0][None]
        vec = jnp.stack(full[1:6] + [jnp.zeros((width,), F32)] * 3)
        up_bias_row = full[6][None]

    xhat, scale = conv_forward(flags, prev, x, nxt, conv_full, conv_bias_row, 2)
    fast = seq == 2
    block_output, grad_hidden, grad_conv, *ffn_grads = ffn(
        flags[3, :1], x, xhat, scale, og, pair_full, up_bias_row, vec, 2 * SUB, min(1024, hidden), batch, fast
    )
    grad_prev, grad_next = ends(grad_conv)
    conv_grads = conv_weight_backward(flags, prev, x, nxt, grad_conv, batch, fast)
    input_grad = conv_input_backward(flags, grad_prev, grad_conv, grad_next, conv_full, grad_hidden, 2)
    sums = whole_sums if not fast else pair_sums
    weight_grads = sums(conv_grads, ffn_grads, batch, seq, width, hidden)
    conv_grad, cb, g1, s1, up_grad, ub_grad, down_grad, db, g2, s2 = weight_grads
    return (block_output[None], input_grad[None], conv_grad, cb, g1, s1, up_grad, ub_grad, down_grad, db, g2, s2)


def whole_sums(conv_grads, ffn_grads, batch, seq, width, hidden):
    def total(value, dims):
        value = lax.psum_scatter(value, "batch", scatter_dimension=dims[1], tiled=True)
        return lax.psum_scatter(value, "seq", scatter_dimension=dims[0], tiled=True)

    conv_grad = total(conv_grads[0], (2, 1)).transpose(0, 2, 1)
    up_grad = total(ffn_grads[0], (0, 1))
    down_grad = total(ffn_grads[1], (0, 1)).T
    vec_grads = total(ffn_grads[2].reshape(6, batch, seq, -1), (2, 1)).reshape(6, -1)
    ub_grad = total(ffn_grads[3].reshape(batch, seq, -1), (1, 0)).reshape(-1)
    g2, s2, db, g1, s1, cb = (vec_grads[i] for i in range(6))
    return conv_grad, cb, g1, s1, up_grad, ub_grad, down_grad, db, g2, s2


def pair_sums(conv_grads, ffn_grads, batch, seq, width, hidden):
    z_count = batch // 4

    def finish(value, dim):
        bit, left = 4, z_count
        while left > 1:
            shape = value.shape
            value = exchange(value.reshape(shape[:dim] + (left // 2, 2) + shape[dim + 1 :]), "batch", bit, dim + 1)
            bit, left = bit * 2, left // 2
        return value

    def chip(send, keep):
        return keep.astype(F32) + swap(send, "batch", 1).astype(F32)

    up_send, up_keep, down_send, down_keep = ffn_grads
    block = hidden // batch
    up_sum = chip(up_send, up_keep).reshape(z_count, 2, 2, -1, block)
    down_sum = chip(down_send, down_keep).reshape(z_count, 2, 2, -1, block)
    up_sum = exchange(exchange(up_sum, "batch", 2, 1), "seq", 1, 1)
    down_sum = exchange(exchange(down_sum, "seq", 1, 2), "batch", 2, 1)
    pair_sum = finish(jnp.concatenate([up_sum, down_sum], 1), 0)[0]
    rows = width // batch
    conv_sum = chip(*conv_grads).reshape(2, KERNEL_TAPS, z_count, 2, rows, width // 2)
    upper = exchange(exchange(conv_sum[..., : rows // 2, :], "batch", 2, 3), "seq", 1, 0)
    lower = exchange(exchange(conv_sum[..., rows // 2 :, :], "seq", 1, 0), "batch", 2, 2)
    conv_grad = finish(jnp.concatenate([upper, lower], 2), 1)[:, 0].transpose(0, 2, 1)
    up_rows = up_sum.shape[1]
    head = width // 2
    up_grad = pair_sum[:head]
    down_grad = pair_sum[up_rows : up_rows + head].T
    each = width // (batch * seq)
    g2, s2, db, g1, s1, cb = (pair_sum[head, i * each : (i + 1) * each] for i in range(6))
    ub_grad = pair_sum[head + 1, : hidden // (batch * seq)]
    return conv_grad, cb, g1, s1, up_grad, ub_grad, down_grad, db, g2, s2


def solution(mesh):
    in_specs = (
        P("batch", "seq", None),
        P("batch", None),
        P(None, "seq", "batch"),
        P(("batch", "seq")),
        P(("batch", "seq")),
        P(("batch", "seq")),
        P("seq", "batch"),
        P(("batch", "seq")),
        P("batch", "seq"),
        P(("batch", "seq")),
        P(("batch", "seq")),
        P(("batch", "seq")),
        P("batch", "seq", None),
    )
    out_specs = (
        P("batch", "seq", None),
        P("batch", "seq", None),
        P(None, "seq", "batch"),
        P(("batch", "seq")),
        P(("batch", "seq")),
        P(("batch", "seq")),
        P("seq", "batch"),
        P(("batch", "seq")),
        P("batch", "seq"),
        P(("batch", "seq")),
        P(("batch", "seq")),
        P(("batch", "seq")),
    )
    return jax.shard_map(local, mesh=mesh, in_specs=in_specs, out_specs=out_specs, check_vma=False)
```

```python
import functools
import jax
import jax.numpy as jnp
from jax import lax
from jax.experimental import pallas as pl
from jax.experimental.pallas import tpu as pltpu
from jax.sharding import Mesh, PartitionSpec as P

KERNEL_TAPS = 9
DILATION_STEP = 32
EPSILON = 1e-05
SUB = 256
BF = jnp.bfloat16
F32 = jnp.float32
VMEM_CONV = 28 * 2**20
VMEM_FFN = 46 * 2**20
VMEM_FIRST = 30 * 2**20
VMEM_PACK = 60 * 2**20
VMEM_SUM = 24 * 2**20
COST = 1
BATCH = ("z", "x", "core")
X, Y, Z0, Z1, CORE = ("x", 1), ("seq", 1), ("z", 1), ("z", 2), ("core", 1)
NN = (((1,), (0,)), ((), ()))
NT = (((1,), (1,)), ((), ()))
TN = (((0,), (0,)), ((), ()))


def dot(a, b, dims):
    return lax.dot_general(a, b, dims, preferred_element_type=F32)


def conv_cost(count, width):
    return pl.CostEstimate(flops=2 * count * KERNEL_TAPS * width * width // COST, bytes_accessed=2**20, transcendentals=0)


def gelu_pair(v):
    size = jnp.abs(v)
    t = pl.reciprocal(1.0 + 0.23164189 * size, approx=True)
    poly = t * (0.127414796 + t * (-0.142248368 + t * (0.710706871 + t * (-0.726576013 + t * 0.530702714))))
    bell = jnp.exp2(-0.72134752 * (size * size))
    value = jnp.maximum(v, 0.0) - size * (poly * bell)
    low_side = bell * (poly - 0.39894228 * size)
    return value, jnp.where(v >= 0.0, 1.0 - low_side, low_side)


def row_mean(v):
    return jnp.sum(v, -1, keepdims=True) * (1.0 / v.shape[-1])


def fold(v):
    total = v[0:8]
    for r in range(8, v.shape[0], 8):
        total = total + v[r : r + 8]
    return total


def fill_columns(col, load, flags, block, subs, width):
    for r in range(subs):
        j = block * subs + r
        base = j * SUB
        own = flags[2, j].astype(F32).astype(BF)
        before = flags[0, j].astype(F32).astype(BF)
        after = flags[1, j].astype(F32).astype(BF)
        for k in range(KERNEL_TAPS):
            o = (k - KERNEL_TAPS // 2) * DILATION_STEP
            columns = slice(k * width, (k + 1) * width)
            first = r * SUB
            if o < 0:
                col[first : first - o, columns] = load(base + o, -o) * before
                col[first - o : first + SUB, columns] = load(base, SUB + o) * own
            elif o == 0:
                col[first : first + SUB, columns] = load(base, SUB) * own
            else:
                col[first : first + SUB - o, columns] = load(base + o, SUB - o) * own
                col[first + SUB - o : first + SUB, columns] = load(base + SUB, o) * after


def place(plan, batch_index, seq_index, sources, whole, sems):
    copies = []
    taps = whole.shape[0]
    for source, (offsets, first) in zip(sources, plan):
        if offsets is None:
            copies.append(pltpu.make_async_copy(source, whole, sems.at[len(copies)]))
            continue
        _, span, rows, wide = source.shape
        span = min(span, taps - max(first, 0))
        for n, (db, ds) in enumerate(offsets):
            b, s = (db, ds) if first < 0 else (batch_index ^ db, seq_index ^ ds)
            at_rows = pl.ds(pl.multiple_of(b * rows, rows), rows)
            at_columns = pl.ds(pl.multiple_of(s * wide, wide), wide)
            target = whole.at[pl.ds(max(first, 0), span), at_rows, at_columns]
            copies.append(pltpu.make_async_copy(source.at[n, pl.ds(0, span)], target, sems.at[len(copies)]))
    return copies


def count_copies(plan):
    return sum(1 if offsets is None else len(offsets) for offsets, _ in plan)


def spread_table(small, rows, out):
    devices, wide = rows.shape
    for v, (start, each) in enumerate(small):
        length = devices * each
        place_of = lax.broadcasted_iota(jnp.int32, (wide, length), 1) % each + start
        pick = (place_of == lax.broadcasted_iota(jnp.int32, (wide, length), 0)).astype(BF)
        values = dot(rows, pick, NN)
        owner = lax.broadcasted_iota(jnp.int32, (devices, length), 1) // each
        own = owner == lax.broadcasted_iota(jnp.int32, (devices, length), 0)
        out[v : v + 1, :length] = jnp.sum(jnp.where(own, values, 0.0), 0, keepdims=True)


def conv_kernel(subs, plan, small, taps, flags, prev, x, nxt, *rest):
    block = pl.program_id(0)
    width = x.shape[1]
    border = prev.shape[0]
    sources = rest[: len(plan)]
    if small:
        xhat_out, scale_out, w_out, table, ext, col, w, sems, out_sem, tails, tail_sems = rest[len(plan) :]
    else:
        table, xhat_out, scale_out, w_out, ext, col, w, sems, out_sem = rest[len(plan) :]

    def copies_in():
        copies = place(plan, flags[4, 0], flags[4, 1], sources, w, sems)
        if small:
            for source, (offsets, first) in zip(sources, plan):
                if first + source.shape[1] <= taps:
                    continue
                for db, ds in offsets:
                    n = offsets.index((db, ds))
                    device = 2 * (flags[4, 0] ^ db) + (flags[4, 1] ^ ds)
                    k = len(copies) - count_copies(plan)
                    copies.append(
                        pltpu.make_async_copy(
                            source.at[n, taps - first, pl.ds(0, 16)], tails.at[device], tail_sems.at[k]
                        )
                    )
        return copies

    @pl.when(block == 0)
    def _():
        for copy in copies_in():
            copy.start()
        ext[0:border] = prev[...]
        ext[border : border + x.shape[0]] = x[...]
        ext[border + x.shape[0] :] = nxt[...]

        for copy in copies_in():
            copy.wait()
        pltpu.make_async_copy(w, w_out, out_sem).start()
        if small:
            devices, high, wide = tails.shape
            first_row = lax.broadcasted_iota(jnp.int32, (devices, devices * high), 0) * high
            pick = (first_row == lax.broadcasted_iota(jnp.int32, (devices, devices * high), 1)).astype(BF)
            rows = dot(pick, tails[...].reshape(devices * high, wide), NN).astype(BF)
            spread_table(small, rows, table)

    @pl.when(block == pl.num_programs(0) - 1)
    def _():
        pltpu.make_async_copy(w, w_out, out_sem).wait()

    def load(start, count):
        return ext[pl.ds(pl.multiple_of(start + border, DILATION_STEP), count), :]

    fill_columns(col, load, flags, block, subs, width)
    total = None
    for k in range(KERNEL_TAPS):
        part = dot(col[:, k * width : (k + 1) * width], w[k], NT)
        total = part if total is None else total + part
    value, slope = gelu_pair(total + table[0:1, :width])
    centered = value - row_mean(value)
    rstd = lax.rsqrt(row_mean(centered * centered) + EPSILON)
    xhat_out[...] = centered * rstd
    scale_out[...] = slope * rstd


def whole_block(shape):
    return pl.BlockSpec(shape, lambda *_: (0,) * len(shape), pipeline_mode=pl.Buffered(1))


def conv_forward(flags, prev, x, nxt, sources, plan, small, table, subs, hidden):
    count, width = x.shape
    rows = subs * SUB
    anywhere = [pl.BlockSpec(memory_space=pl.ANY)] * len(sources)
    out_specs = [pl.BlockSpec((rows, width), lambda j, f: (j, 0))] * 2 + [pl.BlockSpec(memory_space=pltpu.HBM)]
    out_shape = [pltpu.HBM((count, width), F32)] * 2 + [pltpu.HBM((KERNEL_TAPS, width, width), BF)]
    scratch = [
        pltpu.VMEM((count + 2 * prev.shape[0], width), BF),
        pltpu.VMEM((rows, KERNEL_TAPS * width), BF),
        pltpu.VMEM((KERNEL_TAPS, width, width), BF),
        pltpu.SemaphoreType.DMA((count_copies(plan),)),
        pltpu.SemaphoreType.DMA,
    ]
    extra_specs, extra = [], []
    if small:
        out_specs = out_specs + [whole_block((8, hidden))]
        out_shape = out_shape + [jax.ShapeDtypeStruct((8, hidden), F32)]
        devices = width // small[0][1]
        scratch += [pltpu.VMEM((devices, 16, width // 2), BF), pltpu.SemaphoreType.DMA((devices,))]
    else:
        extra_specs, extra = [whole_block(table.shape)], [table]
    outs = pl.pallas_call(
        functools.partial(conv_kernel, subs, plan, small, KERNEL_TAPS),
        grid_spec=pltpu.PrefetchScalarGridSpec(
            num_scalar_prefetch=1,
            grid=(count // rows,),
            in_specs=[whole_block(prev.shape), whole_block(x.shape), whole_block(nxt.shape)] + anywhere + extra_specs,
            out_specs=out_specs,
            scratch_shapes=scratch,
        ),
        out_shape=out_shape,
        compiler_params=pltpu.CompilerParams(vmem_limit_bytes=VMEM_FIRST),
        cost_estimate=conv_cost(count, width),
        name="conv_forward",
    )(flags, prev, x, nxt, *sources, *extra)
    return outs if small else (*outs, table)


def ffn_kernel(chunk, fast, plan, flags, x, xhat, scale, og, table, *rest):
    sources, rest = rest[: len(plan)], rest[len(plan) :]
    out, gh_out, gc_out, *rest = rest
    act, slope, dup, ddown, sums, ub_sums, pair, sems = rest[-8:]
    step = pl.program_id(0)
    last = pl.num_programs(0) - 1
    _, hidden, width = pair.shape
    chunks = hidden // chunk
    gain1, shift1, db, gain2, shift2 = (table[i : i + 1, :width] for i in range(1, 6))
    ub = table[6:7, :]

    @pl.when(step == 0)
    def _():
        copies = place(plan, flags[4, 0], flags[4, 1], sources, pair, sems)
        for copy in copies:
            copy.start()
        dup[...] = jnp.zeros_like(dup)
        ddown[...] = jnp.zeros_like(ddown)
        sums[...] = jnp.zeros_like(sums)
        ub_sums[...] = jnp.zeros_like(ub_sums)
        for copy in copies:
            copy.wait()

    one = x[...].astype(F32) + (xhat[...] * gain1 + shift1)
    low = one.astype(BF)
    total = None
    for f in range(chunks):
        cols = slice(f * chunk, (f + 1) * chunk)
        value, s = gelu_pair(dot(low, pair[0, cols, :], NT) + ub[:, cols])
        a = value.astype(BF)
        act[:, cols] = a
        slope[:, cols] = s
        part = dot(a, pair[1, cols, :], NN)
        total = part if total is None else total + part
    d = total + db
    centered = d - row_mean(d)
    rstd = lax.rsqrt(row_mean(centered * centered) + EPSILON)
    hat = centered * rstd
    out[...] = (one + (hat * gain2 + shift2)).astype(BF)
    g = og[...].astype(F32)
    e = g * gain2
    gd = (rstd * (e - row_mean(e) - hat * row_mean(e * hat))).astype(BF)
    sums[0] += fold(g * hat)
    sums[1] += fold(g)
    sums[2] += fold(gd.astype(F32))
    gh = g
    for f in range(chunks):
        cols = slice(f * chunk, (f + 1) * chunk)
        ddown[:, cols] += dot(gd, act[:, cols], TN)
        gu = dot(gd, pair[1, cols, :], NT) * slope[:, cols]
        gul = gu.astype(BF)
        ub_sums[:, cols] += fold(gul.astype(F32))
        dup[:, cols] += dot(low, gul, TN)
        gh = gh + dot(gul, pair[0, cols, :], NN)
    gh_out[...] = gh
    sums[3] += fold(gh * xhat[...])
    sums[4] += fold(gh)
    e = gh * gain1
    gc = (scale[...] * (e - row_mean(e) - xhat[...] * row_mean(e * xhat[...]))).astype(BF)
    gc_out[...] = gc
    sums[5] += fold(gc.astype(F32))

    @pl.when(step == last)
    def _():
        if not fast:
            up_out, down_out, sums_out, ub_out = rest[:4]
            up_out[...] = dup[...]
            down_out[...] = ddown[...]
            sums_out[...] = jnp.sum(sums[...], 1)
            ub_out[...] = jnp.sum(ub_sums[...], 0, keepdims=True)
            return
        send, keep = rest[:2]
        mine = flags[3, 0] == 0
        block = send.shape[-1]
        half = width // 2
        devices = 2 * (hidden // block)

        def own(length):
            each = length // devices
            place = lax.broadcasted_iota(jnp.int32, (devices, length), 1) // each
            return place == lax.broadcasted_iota(jnp.int32, (devices, length), 0)

        def pick(length, start):
            each = length // devices
            place = lax.broadcasted_iota(jnp.int32, (length, 128), 0) % each + start
            return (place == lax.broadcasted_iota(jnp.int32, (length, 128), 1)).astype(BF)

        first = None
        for v in range(6):
            line = jnp.sum(sums[v], 0, keepdims=True)
            part = dot(jnp.where(own(width), line, 0.0).astype(BF), pick(width, v * (width // devices)), NN)
            first = part if first is None else first + part
        line = jnp.sum(ub_sums[...], 0, keepdims=True)
        second = dot(jnp.where(own(hidden), line, 0.0).astype(BF), pick(hidden, 0), NN)
        index = lax.broadcasted_iota(jnp.int32, (16, 128), 0)

        def tail(b, s):
            at = 2 * b + s
            return jnp.where(index == 0, first[at : at + 1], jnp.where(index == 1, second[at : at + 1], 0.0)).astype(BF)

        for b in range(0, hidden // block, 2):
            for s in range(2):
                take = slice(s * half, (s + 1) * half)
                x_bit, z = b // 2 % 2, (b // 4 % 2, b // 8)
                up_at, down_at = (2 * x_bit + s, *z), (2 * s + x_bit, *z)
                for acc, at, start in ((dup, up_at, 0), (ddown, down_at, half + 16)):
                    lo = acc[take, b * block : (b + 1) * block].astype(BF)
                    hi = acc[take, (b + 1) * block : (b + 2) * block].astype(BF)
                    send[(*at, slice(start, start + half))] = jnp.where(mine, hi, lo)
                    keep[(*at, slice(start, start + half))] = jnp.where(mine, lo, hi)
                lo, hi = tail(b, s), tail(b + 1, s)
                send[(*up_at, slice(half, half + 16))] = jnp.where(mine, hi, lo)
                keep[(*up_at, slice(half, half + 16))] = jnp.where(mine, lo, hi)


def ffn(flags, x, xhat, scale, og, table, sources, plan, rows, chunk, batch, fast):
    count, width = x.shape
    hidden = table.shape[1]
    tile = pl.BlockSpec((rows, width), lambda j, f: (j, 0))
    sds = jax.ShapeDtypeStruct
    if fast:
        shapes = [sds((4, 2, 2, width + 16, hidden // batch), BF)] * 2
    else:
        shapes = [sds(s, F32) for s in ((width, hidden), (width, hidden), (6, width), (1, hidden))]
    anywhere = [pl.BlockSpec(memory_space=pl.ANY)] * len(sources)
    return pl.pallas_call(
        functools.partial(ffn_kernel, chunk, fast, plan),
        grid_spec=pltpu.PrefetchScalarGridSpec(
            num_scalar_prefetch=1,
            grid=(count // rows,),
            in_specs=[tile, tile, tile, tile, whole_block(table.shape)] + anywhere,
            out_specs=[tile, tile, tile] + [whole_block(s.shape) for s in shapes],
            scratch_shapes=[
                pltpu.VMEM((rows, hidden), BF),
                pltpu.VMEM((rows, hidden), F32),
                pltpu.VMEM((width, hidden), F32),
                pltpu.VMEM((width, hidden), F32),
                pltpu.VMEM((6, 8, width), F32),
                pltpu.VMEM((8, hidden), F32),
                pltpu.VMEM((2, hidden, width), BF),
                pltpu.SemaphoreType.DMA((count_copies(plan),)),
            ],
        ),
        out_shape=[sds((count, width), BF), sds((count, width), F32), sds((count, width), BF)] + shapes,
        compiler_params=pltpu.CompilerParams(vmem_limit_bytes=VMEM_FFN if fast else VMEM_PACK),
        cost_estimate=pl.CostEstimate(flops=12 * count * width * hidden // COST, bytes_accessed=2**20, transcendentals=0),
        name="feed_forward",
    )(flags, x, xhat, scale, og, table, *sources)


def conv_weight_kernel(fast, flags, prev, x, nxt, g, *rest):
    ext, col = rest[-2:]
    tap = pl.program_id(0)
    count, width = g.shape
    border = prev.shape[0]
    subs = count // SUB

    @pl.when(tap == 0)
    def _():
        ext[0:border] = prev[...]
        ext[border : border + count] = x[...]
        ext[border + count :] = nxt[...]

    o = (tap - KERNEL_TAPS // 2) * DILATION_STEP
    offset = lax.broadcasted_iota(jnp.int32, (SUB, 1), 0) + o
    for r in range(subs):
        own = flags[2, r].astype(F32)
        before = flags[0, r].astype(F32)
        after = flags[1, r].astype(F32)
        mask = jnp.where(offset < 0, before, jnp.where(offset >= SUB, after, own)).astype(BF)
        rows = ext[pl.ds(pl.multiple_of(r * SUB + o + border, DILATION_STEP), SUB), :]
        col[r * SUB : (r + 1) * SUB, :] = rows * mask

    grad = dot(g[...], col[...], TN)
    if not fast:
        rest[0][0] = grad
        return
    mine = flags[3, 0] == 0
    half = width // 2

    send, keep = rest[:2]
    block = send.shape[4]
    early = (tap < (KERNEL_TAPS + 1) // 2).astype(jnp.int32)
    for s in range(2):
        columns = slice(s * half, (s + 1) * half)
        for b in range(0, width // block, 2):
            bit = b // 2 % 2
            at = (early * (2 * bit + s) + (1 - early) * (2 * s + bit), b // 4 % 2, b // 8, 0)
            lo = grad[b * block : (b + 1) * block, columns].astype(BF)
            hi = grad[(b + 1) * block : (b + 2) * block, columns].astype(BF)
            send[at] = jnp.where(mine, hi, lo)
            keep[at] = jnp.where(mine, lo, hi)


def conv_weight_backward(flags, prev, x, nxt, g, batch, fast):
    count, width = x.shape
    if fast:
        block = (4, 2, 2, 1, width // batch, width // 2)
        specs = [pl.BlockSpec(block, lambda k, f: (0, 0, 0, k, 0, 0))] * 2
        shapes = [jax.ShapeDtypeStruct(block[:3] + (KERNEL_TAPS,) + block[4:], BF)] * 2
    else:
        specs = [pl.BlockSpec((1, width, width), lambda k, f: (k, 0, 0))]
        shapes = [jax.ShapeDtypeStruct((KERNEL_TAPS, width, width), F32)]
    return pl.pallas_call(
        functools.partial(conv_weight_kernel, fast),
        grid_spec=pltpu.PrefetchScalarGridSpec(
            num_scalar_prefetch=1,
            grid=(KERNEL_TAPS,),
            in_specs=[whole_block(a.shape) for a in (prev, x, nxt, g)],
            out_specs=specs,
            scratch_shapes=[
                pltpu.VMEM((count + 2 * prev.shape[0], width), BF),
                pltpu.VMEM((count, width), BF),
            ],
        ),
        out_shape=shapes,
        compiler_params=pltpu.CompilerParams(vmem_limit_bytes=VMEM_CONV),
        cost_estimate=conv_cost(count, width),
        name="conv_weight_backward",
    )(flags, prev, x, nxt, g)


def conv_input_kernel(subs, flags, prev, g, nxt, gh, w, out, ext, col):
    step = pl.program_id(0)
    count, width = g.shape
    border = prev.shape[0]

    @pl.when(step == 0)
    def _():
        ext[0:border] = prev[...]
        ext[border : border + count] = g[...]
        ext[border + count :] = nxt[...]

    def load(start, size):
        return ext[pl.ds(pl.multiple_of(start + border, DILATION_STEP), size), :]

    fill_columns(col, load, flags, step, subs, width)
    total = gh[...]
    for k in range(KERNEL_TAPS):
        total = total + dot(col[:, k * width : (k + 1) * width], w[KERNEL_TAPS - 1 - k], NN)
    out[...] = total


def conv_input_backward(flags, prev, g, nxt, gh, weights, subs):
    count, width = g.shape
    rows = subs * SUB
    tile = pl.BlockSpec((rows, width), lambda j, f: (j, 0))
    return pl.pallas_call(
        functools.partial(conv_input_kernel, subs),
        grid_spec=pltpu.PrefetchScalarGridSpec(
            num_scalar_prefetch=1,
            grid=(count // rows,),
            in_specs=[whole_block(a.shape) for a in (prev, g, nxt)] + [tile, whole_block(weights.shape)],
            out_specs=tile,
            scratch_shapes=[
                pltpu.VMEM((count + 2 * prev.shape[0], width), BF),
                pltpu.VMEM((rows, KERNEL_TAPS * width), BF),
            ],
        ),
        out_shape=jax.ShapeDtypeStruct((count, width), F32),
        compiler_params=pltpu.CompilerParams(vmem_limit_bytes=VMEM_CONV),
        cost_estimate=conv_cost(count, width),
        name="conv_input_backward",
    )(flags, prev, g, nxt, gh, weights)


def pack_kernel(small, slots, count, lengths, first, final, conv, up, down, *rest):
    vectors, (flags, halo, conv_out, pair_out) = rest[: len(small)], rest[len(small) :]
    batch_index = lax.axis_index("z") * 4 + lax.axis_index("x") * 2 + lax.axis_index("core")
    seq_index = lax.axis_index("seq")
    taps, rows, wide = conv.shape
    subs = flags.shape[1]
    conv_out[0, 0:taps] = conv[...]
    line = None
    for v, (start, each) in zip(vectors, small):
        pick = (
            lax.broadcasted_iota(jnp.int32, (each, wide), 0) + start == lax.broadcasted_iota(jnp.int32, (each, wide), 1)
        ).astype(BF)
        part = dot(jnp.broadcast_to(v[...], (rows, each)), pick, NN)
        line = part if line is None else line + part
    conv_out[0, taps] = line.astype(BF)
    pair_out[0, 0] = up[...].T
    pair_out[0, 1] = down[...]
    halo[...] = jnp.where(seq_index == 0, final[...], first[...])
    ends = []
    total = 0
    for i in range(slots):
        total = total + lengths[0, i]
        ends.append(total)
    ids = []
    for j in range(-1, subs + 1):
        start = seq_index * count + j * SUB
        number = 0
        for end in ends:
            number = number + (start >= end).astype(jnp.int32)
        ids.append(jnp.where(start >= 0, number, -1))
    for j in range(subs):
        inside = (ids[j + 1] < slots).astype(jnp.int32)
        flags[0, j] = (ids[j] == ids[j + 1]).astype(jnp.int32) * inside
        flags[1, j] = (ids[j + 2] == ids[j + 1]).astype(jnp.int32) * inside
        flags[2, j] = inside
        flags[3, j] = batch_index % 2
        flags[4, j] = batch_index if j == 0 else seq_index
        bits = (lax.axis_index("x"), seq_index, lax.axis_index("z") % 2, lax.axis_index("z") // 2)
        flags[5, j] = bits[min(j, 3)]


def pack(lengths, x, conv, up, down, vectors, small):
    taps, rows, wide = conv.shape
    count, width = x.shape
    border = KERNEL_TAPS // 2 * DILATION_STEP
    smem = pl.BlockSpec(memory_space=pltpu.SMEM)
    arrays = [conv, up, down] + [v[None] for v in vectors]
    end_rows = pl.BlockSpec((border, width), lambda i: (0, 0))
    final_rows = pl.BlockSpec((border, width), lambda i: (count // border - 1, 0))
    sds = jax.ShapeDtypeStruct
    outs = [
        sds((6, count // SUB), jnp.int32),
        sds((border, width), BF),
        sds((1, taps + 1, rows, wide), BF),
        sds((1, 2) + down.shape, BF),
    ]
    return pl.pallas_call(
        functools.partial(pack_kernel, small, lengths.shape[1], count),
        grid=(1,),
        in_specs=[smem, end_rows, final_rows] + [whole_block(a.shape) for a in arrays],
        out_specs=[smem] + [whole_block(o.shape) for o in outs[1:]],
        out_shape=outs,
        compiler_params=pltpu.CompilerParams(vmem_limit_bytes=VMEM_PACK),
        name="pack",
    )(lengths, x, x, *arrays)


def swap(value, link):
    axis, bit = link
    return lax.ppermute(value, axis, [(i, i ^ bit) for i in range(lax.axis_size(axis))])


def half_of(link):
    return (lax.axis_index(link[0]) // link[1]) % 2


def give_half(value, link, dim):
    return lax.dynamic_index_in_dim(value, 1 - half_of(link), dim, keepdims=False).astype(BF)


def keep_half(value, link, dim):
    return lax.dynamic_index_in_dim(value, half_of(link), dim, keepdims=False).astype(F32)


def after(value, *others):
    return lax.optimization_barrier((value, *others))[0]


def shifted(offsets, b, s):
    return tuple((ob ^ b, os ^ s) for ob, os in offsets)


def both_cores(arrays, plan):
    other = [swap(a, CORE) for a in arrays]
    return arrays + other, tuple(plan) + tuple((shifted(o, 1, 0), first) for o, first in plan)


def gather_conv(own):
    cut = own.shape[1] // 2
    top = lambda value: swap(value[:, :cut], Y)
    bottom = lambda value: swap(value[:, cut:], X)
    far, own_x, own_y = lax.optimization_barrier((swap(own, Z1), swap(own, X), swap(own, Y)))
    column = jnp.concatenate([own, far], 0)
    near, far_x, far_y, own_top, own_bottom = lax.optimization_barrier(
        (swap(column, Z0), swap(far, X), swap(far, Y), top(own_x), bottom(own_y))
    )
    near_x, near_y, far_top, far_bottom = lax.optimization_barrier(
        (swap(near, X), swap(near, Y), top(far_x), bottom(far_y))
    )
    near_top, near_bottom = top(near_x), bottom(near_y)
    arrays, plan = [column, near], [(((0, 0), (8, 0)), 0), (((4, 0), (12, 0)), 0)]
    for offsets, members in (
        (((0, 0),), (own_x, own_y, own_top, own_bottom)),
        (((8, 0),), (far_x, far_y, far_top, far_bottom)),
        (((4, 0), (12, 0)), (near_x, near_y, near_top, near_bottom)),
    ):
        arrays += members
        plan += [(shifted(offsets, b, s), first) for b, s, first in ((2, 0, 0), (0, 1, 0), (2, 1, 0), (2, 1, cut))]
    return both_cores(arrays, plan)


def stage_kernel(columns, joined, flags, *refs):
    count = len(columns)
    outs = refs[2 * count :]
    at = 0
    for i, column in enumerate(columns):
        keep, got = refs[2 * i], refs[2 * i + 1]
        if joined is None:
            give_out, keep_out, where = outs[2 * i], outs[2 * i + 1], Ellipsis
        else:
            taps = keep.shape[1 + joined]
            give_out, keep_out = outs
            where = (*(slice(None),) * joined, slice(at, at + taps))
            at += taps
        bit = flags[5, column]
        give_out[where] = (keep[1 - bit].astype(F32) + got[1 - bit].astype(F32)).astype(BF)
        keep_out[where] = keep[bit].astype(F32) + got[bit].astype(F32)


def first_stage_kernel(cut, flags, keep, got, *outs):
    for i, taps in enumerate((slice(0, cut), slice(cut, keep.shape[3]))):
        bit = flags[5, i]
        give_out, keep_out = outs[2 * i], outs[2 * i + 1]
        for n in range(2):
            other, own = 2 * (1 - bit) + n, 2 * bit + n
            give_out[n] = (keep[other, :, :, taps].astype(F32) + got[other, :, :, taps].astype(F32)).astype(BF)
            keep_out[n] = keep[own, :, :, taps].astype(F32) + got[own, :, :, taps].astype(F32)


def first_stage(flags, keep, got, cut):
    tail = keep.shape[4:]
    outs = [jax.ShapeDtypeStruct((2, 2, 2, n) + tail, kind) for n in (cut, keep.shape[3] - cut) for kind in (BF, F32)]
    return pl.pallas_call(
        functools.partial(first_stage_kernel, cut),
        grid_spec=pltpu.PrefetchScalarGridSpec(
            num_scalar_prefetch=1,
            grid=(1,),
            in_specs=[whole_block(keep.shape)] * 2,
            out_specs=[whole_block(o.shape) for o in outs],
        ),
        out_shape=outs,
        compiler_params=pltpu.CompilerParams(vmem_limit_bytes=VMEM_SUM),
        name="stage",
    )(flags, keep, got)


def stage(flags, parts, columns, joined=None):
    shapes = [keep.shape[1:] for keep, _ in parts]
    if joined is not None:
        first = list(shapes[0])
        first[joined] = sum(shape[joined] for shape in shapes)
        shapes = [tuple(first)]
    outs = [jax.ShapeDtypeStruct(shape, kind) for shape in shapes for kind in (BF, F32)]
    arrays = [a for part in parts for a in part]
    return pl.pallas_call(
        functools.partial(stage_kernel, columns, joined),
        grid_spec=pltpu.PrefetchScalarGridSpec(
            num_scalar_prefetch=1,
            grid=(1,),
            in_specs=[whole_block(a.shape) for a in arrays],
            out_specs=[whole_block(o.shape) for o in outs],
        ),
        out_shape=outs,
        compiler_params=pltpu.CompilerParams(vmem_limit_bytes=VMEM_SUM),
        name="stage",
    )(flags, *arrays)


def local(inputs, window_lengths, conv_weight, conv_bias, norm1_gain, norm1_bias, up_weight, up_bias, down_weight,
          down_bias, norm2_gain, norm2_bias, out_grad):
    _, count, width = inputs.shape
    batch, seq = lax.axis_size(BATCH), lax.axis_size("seq")
    hidden = up_weight.shape[1] * batch
    border = KERNEL_TAPS // 2 * DILATION_STEP
    x, og = inputs[0], out_grad[0]
    fast = seq == 2 and batch == 16

    def ends(value):
        first, final = value[:border], value[count - border :]
        if fast:
            other = swap(jnp.where(lax.axis_index("seq") == 0, final, first), Y)
            return other, other
        up = [(i, i + 1) for i in range(seq - 1)]
        return lax.ppermute(final, "seq", up), lax.ppermute(first, "seq", [(j, i) for i, j in up])

    vectors = [conv_bias, norm1_gain, norm1_bias, down_bias, norm2_gain, norm2_bias, up_bias]
    sizes = [v.shape[0] for v in vectors]
    small = tuple((sum(sizes[:i]), n) for i, n in enumerate(sizes))
    conv_own = conv_weight.transpose(0, 2, 1)
    flags, halo, conv_block, pair_block = pack(window_lengths, x, conv_own, up_weight, down_weight, vectors, small)
    if fast:
        prev = nxt = swap(halo, Y)
        conv_pieces, conv_plan = gather_conv(conv_block)
        pair_pieces = [lax.all_gather(pair_block[0], (*BATCH, "seq"), axis=0)]
        pair_plan = ((tuple((d // 2, d % 2) for d in range(2 * batch)), -1),)
        table = None
    else:
        def every(value):
            value = lax.all_gather(value, "seq", axis=2, tiled=True)
            return lax.all_gather(value, BATCH, axis=1, tiled=True)

        prev, nxt = ends(x)
        conv_pieces, conv_plan = [every(conv_own)], ((None, 0),)
        pair_pieces, pair_plan = [every(pair_block[0])], ((None, 0),)
        full = [lax.all_gather(v, (*BATCH, "seq"), axis=0, tiled=True).astype(F32) for v in vectors]
        table = jnp.stack([jnp.pad(v, (0, hidden - v.shape[0])) for v in full + [full[0]]])
        small = ()
    conv_pieces, conv_plan = list(conv_pieces), tuple((None if o is None else tuple(o), f) for o, f in conv_plan)
    xhat, scale, conv_full, table = conv_forward(flags, prev, x, nxt, conv_pieces, conv_plan, small, table, 2, hidden)
    pair_plan = tuple((None if o is None else tuple(o), f) for o, f in pair_plan)
    block_output, grad_hidden, grad_conv, *ffn_grads = ffn(
        flags, x, xhat, scale, og, table, pair_pieces, pair_plan, 2 * SUB, min(1024, hidden), batch, fast
    )
    grad_prev, grad_next = ends(grad_conv)
    grads = (flags, prev, x, nxt, grad_conv, grad_prev, grad_next, grad_hidden, conv_full)
    if fast:
        input_grad, weight_grads = paired(grads, ffn_grads, batch, width, hidden)
    else:
        conv_grads = conv_weight_backward(flags, prev, x, nxt, grad_conv, batch, fast)
        input_grad = conv_input_backward(flags, grad_prev, grad_conv, grad_next, grad_hidden, conv_full, 2)
        weight_grads = whole_sums(conv_grads, ffn_grads, batch, seq, width, hidden)
    conv_grad, cb, g1, s1, up_grad, ub_grad, down_grad, db, g2, s2 = weight_grads
    return (block_output[None], input_grad[None], conv_grad, cb, g1, s1, up_grad, ub_grad, down_grad, db, g2, s2)


def paired(grads, ffn_grads, batch, width, hidden):
    flags, prev, x, nxt, grad_conv, grad_prev, grad_next, grad_hidden, conv_full = grads
    up_rows = width // 2 + 16
    ffn_send, ffn_keep = ffn_grads
    ffn_got = swap(ffn_send, CORE)
    send, keep = conv_weight_backward(flags, prev, x, nxt, grad_conv, batch, True)
    ffn_got, grad_prev, send = lax.optimization_barrier((ffn_got, grad_prev, send))
    got = swap(send, CORE)
    up_give, up_keep, down_give, down_keep = first_stage(flags, ffn_keep, ffn_got, up_rows)
    up_got, down_got = swap(up_give, X), swap(down_give, Y)
    upper_give, upper_keep, lower_give, lower_keep = first_stage(
        flags, keep, after(got, up_give), (KERNEL_TAPS + 1) // 2
    )
    upper_got, lower_got = swap(upper_give, X), swap(lower_give, Y)
    input_grad = conv_input_backward(
        flags, grad_prev, after(grad_conv, upper_give), grad_prev, grad_hidden, conv_full, 2
    )
    up_got, down_got, input_grad = lax.optimization_barrier((up_got, down_got, input_grad))
    parts = [(up_keep, up_got), (down_keep, down_got)]
    up_give, up_keep, down_give, down_keep = stage(flags, parts, (1, 0))
    up_got, down_got = swap(up_give, Y), swap(down_give, X)
    upper_got, lower_got, _ = lax.optimization_barrier((upper_got, lower_got, up_give))
    parts = [(upper_keep, upper_got), (lower_keep, lower_got)]
    upper_give, upper_keep, lower_give, lower_keep = stage(flags, parts, (1, 0))
    upper_got, lower_got = swap(upper_give, Y), swap(lower_give, X)
    up_got, down_got, _ = lax.optimization_barrier((up_got, down_got, upper_give))
    ffn_give, ffn_keep = stage(flags, [(up_keep, up_got), (down_keep, down_got)], (2, 2), 1)
    ffn_got = swap(ffn_give, Z0)
    upper_got, lower_got, _ = lax.optimization_barrier((upper_got, lower_got, ffn_give))
    conv_give, conv_keep = stage(flags, [(upper_keep, upper_got), (lower_keep, lower_got)], (2, 2), 1)
    conv_got = swap(conv_give, Z0)
    ffn_give, ffn_keep = stage(flags, [(ffn_keep, after(ffn_got, conv_give))], (3,))
    ffn_got = swap(ffn_give, Z1)
    conv_give, conv_keep = stage(flags, [(conv_keep, after(conv_got, ffn_give))], (3,))
    conv_got = swap(conv_give, Z1)
    pair_part = ffn_keep + after(ffn_got, conv_give).astype(F32)
    conv_grad = (conv_keep + conv_got.astype(F32)).transpose(0, 2, 1)
    head = width // 2
    up_grad = pair_part[:head]
    down_grad = pair_part[up_rows:].T
    each = width // (batch * 2)
    g2, s2, db, g1, s1, cb = (pair_part[head, i * each : (i + 1) * each] for i in range(6))
    ub_grad = pair_part[head + 1, : hidden // (batch * 2)]
    return input_grad, (conv_grad, cb, g1, s1, up_grad, ub_grad, down_grad, db, g2, s2)


def whole_sums(conv_grads, ffn_grads, batch, seq, width, hidden):
    def total(value, dims):
        value = lax.psum_scatter(value, BATCH, scatter_dimension=dims[1], tiled=True)
        return lax.psum_scatter(value, "seq", scatter_dimension=dims[0], tiled=True)

    conv_grad = total(conv_grads[0], (2, 1)).transpose(0, 2, 1)
    up_grad = total(ffn_grads[0], (0, 1))
    down_grad = total(ffn_grads[1], (0, 1)).T
    vec_grads = total(ffn_grads[2].reshape(6, batch, seq, -1), (2, 1)).reshape(6, -1)
    ub_grad = total(ffn_grads[3].reshape(batch, seq, -1), (1, 0)).reshape(-1)
    g2, s2, db, g1, s1, cb = (vec_grads[i] for i in range(6))
    return conv_grad, cb, g1, s1, up_grad, ub_grad, down_grad, db, g2, s2


def solution(mesh):
    batch, seq = mesh.shape["batch"], mesh.shape["seq"]
    split = Mesh(mesh.devices.reshape(batch // 4, 2, 2, seq), (*BATCH, "seq"))
    both = P((*BATCH, "seq"))
    rows = P(BATCH, "seq", None)
    conv, up, down = P(None, "seq", BATCH), P("seq", BATCH), P(BATCH, "seq")
    in_specs = (rows, P(BATCH, None), conv, both, both, both, up, both, down, both, both, both, rows)
    out_specs = (rows, rows, conv, both, both, both, up, both, down, both, both, both)
    return jax.shard_map(local, mesh=split, in_specs=in_specs, out_specs=out_specs, check_vma=False)
```

```python
import functools
import jax
import jax.numpy as jnp
from jax import lax
from jax.experimental import pallas as pl
from jax.experimental.pallas import tpu as pltpu
from jax.sharding import Mesh, PartitionSpec as P

KERNEL_TAPS = 9
DILATION_STEP = 32
EPSILON = 1e-05
SUB = 256
BF = jnp.bfloat16
F32 = jnp.float32
VMEM_CONV = 28 * 2**20
VMEM_FFN = 51 * 2**20
VMEM_FIRST = 30 * 2**20
VMEM_PACK = 60 * 2**20
VMEM_SUM = 24 * 2**20
COST = 1
BATCH = ("z", "x", "core")
X, Y, Z0, Z1, CORE = ("x", 1), ("seq", 1), ("z", 1), ("z", 2), ("core", 1)
NN = (((1,), (0,)), ((), ()))
NT = (((1,), (1,)), ((), ()))
TN = (((0,), (0,)), ((), ()))


def dot(a, b, dims):
    return lax.dot_general(a, b, dims, preferred_element_type=F32)


def conv_cost(count, width):
    return pl.CostEstimate(flops=2 * count * KERNEL_TAPS * width * width // COST, bytes_accessed=2**20, transcendentals=0)


def gelu_pair(v):
    size = jnp.abs(v)
    t = pl.reciprocal(1.0 + 0.23164189 * size, approx=True)
    poly = t * (0.127414796 + t * (-0.142248368 + t * (0.710706871 + t * (-0.726576013 + t * 0.530702714))))
    bell = jnp.exp2(-0.72134752 * (size * size))
    value = jnp.maximum(v, 0.0) - size * (poly * bell)
    low_side = bell * (poly - 0.39894228 * size)
    return value, jnp.where(v >= 0.0, 1.0 - low_side, low_side)


def row_mean(v):
    return jnp.sum(v, -1, keepdims=True) * (1.0 / v.shape[-1])


def fold(v):
    total = v[0:8]
    for r in range(8, v.shape[0], 8):
        total = total + v[r : r + 8]
    return total


def fill_columns(col, load, flags, block, subs, width):
    for r in range(subs):
        j = block * subs + r
        base = j * SUB
        own = flags[2, j].astype(F32).astype(BF)
        before = flags[0, j].astype(F32).astype(BF)
        after = flags[1, j].astype(F32).astype(BF)
        for k in range(KERNEL_TAPS):
            o = (k - KERNEL_TAPS // 2) * DILATION_STEP
            columns = slice(k * width, (k + 1) * width)
            first = r * SUB
            if o < 0:
                col[first : first - o, columns] = load(base + o, -o) * before
                col[first - o : first + SUB, columns] = load(base, SUB + o) * own
            elif o == 0:
                col[first : first + SUB, columns] = load(base, SUB) * own
            else:
                col[first : first + SUB - o, columns] = load(base + o, SUB - o) * own
                col[first + SUB - o : first + SUB, columns] = load(base + SUB, o) * after


def place(plan, batch_index, seq_index, sources, whole, sems):
    copies = []
    taps = whole.shape[0]
    for source, (offsets, first) in zip(sources, plan):
        if offsets is None:
            copies.append(pltpu.make_async_copy(source, whole, sems.at[len(copies)]))
            continue
        _, span, rows, wide = source.shape
        span = min(span, taps - max(first, 0))
        for n, (db, ds) in enumerate(offsets):
            b, s = (db, ds) if first < 0 else (batch_index ^ db, seq_index ^ ds)
            at_rows = pl.ds(pl.multiple_of(b * rows, rows), rows)
            at_columns = pl.ds(pl.multiple_of(s * wide, wide), wide)
            target = whole.at[pl.ds(max(first, 0), span), at_rows, at_columns]
            copies.append(pltpu.make_async_copy(source.at[n, pl.ds(0, span)], target, sems.at[len(copies)]))
    return copies


def count_copies(plan):
    return sum(1 if offsets is None else len(offsets) for offsets, _ in plan)


def spread_table(small, rows, out):
    devices, wide = rows.shape
    for v, (start, each) in enumerate(small):
        length = devices * each
        place_of = lax.broadcasted_iota(jnp.int32, (wide, length), 1) % each + start
        pick = (place_of == lax.broadcasted_iota(jnp.int32, (wide, length), 0)).astype(BF)
        values = dot(rows, pick, NN)
        owner = lax.broadcasted_iota(jnp.int32, (devices, length), 1) // each
        own = owner == lax.broadcasted_iota(jnp.int32, (devices, length), 0)
        out[v : v + 1, :length] = jnp.sum(jnp.where(own, values, 0.0), 0, keepdims=True)


def conv_kernel(subs, plan, small, taps, flags, prev, x, nxt, *rest):
    block = pl.program_id(0)
    width = x.shape[1]
    border = prev.shape[0]
    sources = rest[: len(plan)]
    if small:
        xhat_out, scale_out, w_out, table, ext, col, w, sems, out_sem, tails, tail_sems = rest[len(plan) :]
    else:
        table, xhat_out, scale_out, w_out, ext, col, w, sems, out_sem = rest[len(plan) :]

    def copies_in():
        copies = place(plan, flags[4, 0], flags[4, 1], sources, w, sems)
        if small:
            for source, (offsets, first) in zip(sources, plan):
                if first + source.shape[1] <= taps:
                    continue
                for db, ds in offsets:
                    n = offsets.index((db, ds))
                    device = 2 * (flags[4, 0] ^ db) + (flags[4, 1] ^ ds)
                    k = len(copies) - count_copies(plan)
                    copies.append(
                        pltpu.make_async_copy(
                            source.at[n, taps - first, pl.ds(0, 16)], tails.at[device], tail_sems.at[k]
                        )
                    )
        return copies

    @pl.when(block == 0)
    def _():
        for copy in copies_in():
            copy.start()
        ext[0:border] = prev[...]
        ext[border : border + x.shape[0]] = x[...]
        ext[border + x.shape[0] :] = nxt[...]

        for copy in copies_in():
            copy.wait()
        pltpu.make_async_copy(w, w_out, out_sem).start()
        if small:
            devices, high, wide = tails.shape
            first_row = lax.broadcasted_iota(jnp.int32, (devices, devices * high), 0) * high
            pick = (first_row == lax.broadcasted_iota(jnp.int32, (devices, devices * high), 1)).astype(BF)
            rows = dot(pick, tails[...].reshape(devices * high, wide), NN).astype(BF)
            spread_table(small, rows, table)

    @pl.when(block == pl.num_programs(0) - 1)
    def _():
        pltpu.make_async_copy(w, w_out, out_sem).wait()

    def load(start, count):
        return ext[pl.ds(pl.multiple_of(start + border, DILATION_STEP), count), :]

    fill_columns(col, load, flags, block, subs, width)
    total = None
    for k in range(KERNEL_TAPS):
        part = dot(col[:, k * width : (k + 1) * width], w[k], NT)
        total = part if total is None else total + part
    value, slope = gelu_pair(total + table[0:1, :width])
    centered = value - row_mean(value)
    rstd = lax.rsqrt(row_mean(centered * centered) + EPSILON)
    xhat_out[...] = centered * rstd
    scale_out[...] = slope * rstd


def whole_block(shape):
    return pl.BlockSpec(shape, lambda *_: (0,) * len(shape), pipeline_mode=pl.Buffered(1))


def conv_forward(flags, prev, x, nxt, sources, plan, small, table, subs, hidden):
    count, width = x.shape
    rows = subs * SUB
    anywhere = [pl.BlockSpec(memory_space=pl.ANY)] * len(sources)
    out_specs = [pl.BlockSpec((rows, width), lambda j, f: (j, 0))] * 2 + [pl.BlockSpec(memory_space=pltpu.HBM)]
    out_shape = [pltpu.HBM((count, width), F32)] * 2 + [pltpu.HBM((KERNEL_TAPS, width, width), BF)]
    scratch = [
        pltpu.VMEM((count + 2 * prev.shape[0], width), BF),
        pltpu.VMEM((rows, KERNEL_TAPS * width), BF),
        pltpu.VMEM((KERNEL_TAPS, width, width), BF),
        pltpu.SemaphoreType.DMA((count_copies(plan),)),
        pltpu.SemaphoreType.DMA,
    ]
    extra_specs, extra = [], []
    if small:
        out_specs = out_specs + [whole_block((8, hidden))]
        out_shape = out_shape + [jax.ShapeDtypeStruct((8, hidden), F32)]
        devices = width // small[0][1]
        scratch += [pltpu.VMEM((devices, 16, width // 2), BF), pltpu.SemaphoreType.DMA((devices,))]
    else:
        extra_specs, extra = [whole_block(table.shape)], [table]
    outs = pl.pallas_call(
        functools.partial(conv_kernel, subs, plan, small, KERNEL_TAPS),
        grid_spec=pltpu.PrefetchScalarGridSpec(
            num_scalar_prefetch=1,
            grid=(count // rows,),
            in_specs=[whole_block(prev.shape), whole_block(x.shape), whole_block(nxt.shape)] + anywhere + extra_specs,
            out_specs=out_specs,
            scratch_shapes=scratch,
        ),
        out_shape=out_shape,
        compiler_params=pltpu.CompilerParams(vmem_limit_bytes=VMEM_FIRST),
        cost_estimate=conv_cost(count, width),
        name="conv_forward",
    )(flags, prev, x, nxt, *sources, *extra)
    return outs if small else (*outs, table)


def ffn_kernel(chunk, fast, plan, flags, x, xhat, scale, og, table, *rest):
    sources, rest = rest[: len(plan)], rest[len(plan) :]
    out, gh_out, gc_out, *rest = rest
    act, slope, dup, ddown, sums, ub_sums, pair, sems = rest[-8:]
    step = pl.program_id(0)
    last = pl.num_programs(0) - 1
    _, hidden, width = pair.shape
    chunks = hidden // chunk
    gain1, shift1, db, gain2, shift2 = (table[i : i + 1, :width] for i in range(1, 6))
    ub = table[6:7, :]

    @pl.when(step == 0)
    def _():
        copies = place(plan, flags[4, 0], flags[4, 1], sources, pair, sems)
        for copy in copies:
            copy.start()
        dup[...] = jnp.zeros_like(dup)
        ddown[...] = jnp.zeros_like(ddown)
        sums[...] = jnp.zeros_like(sums)
        ub_sums[...] = jnp.zeros_like(ub_sums)
        for copy in copies:
            copy.wait()

    one = x[...].astype(F32) + (xhat[...] * gain1 + shift1)
    low = one.astype(BF)
    total = None
    for f in range(chunks):
        cols = slice(f * chunk, (f + 1) * chunk)
        value, s = gelu_pair(dot(low, pair[0, cols, :], NT) + ub[:, cols])
        a = value.astype(BF)
        act[:, cols] = a
        slope[:, cols] = s
        part = dot(a, pair[1, cols, :], NN)
        total = part if total is None else total + part
    d = total + db
    centered = d - row_mean(d)
    rstd = lax.rsqrt(row_mean(centered * centered) + EPSILON)
    hat = centered * rstd
    out[...] = (one + (hat * gain2 + shift2)).astype(BF)
    g = og[...].astype(F32)
    e = g * gain2
    gd = (rstd * (e - row_mean(e) - hat * row_mean(e * hat))).astype(BF)
    sums[0] += fold(g * hat)
    sums[1] += fold(g)
    sums[2] += fold(gd.astype(F32))
    gh = g
    for f in range(chunks):
        cols = slice(f * chunk, (f + 1) * chunk)
        ddown[:, cols] += dot(gd, act[:, cols], TN)
        gu = dot(gd, pair[1, cols, :], NT) * slope[:, cols]
        gul = gu.astype(BF)
        ub_sums[:, cols] += fold(gul.astype(F32))
        dup[:, cols] += dot(low, gul, TN)
        gh = gh + dot(gul, pair[0, cols, :], NN)
    gh_out[...] = gh
    sums[3] += fold(gh * xhat[...])
    sums[4] += fold(gh)
    e = gh * gain1
    gc = (scale[...] * (e - row_mean(e) - xhat[...] * row_mean(e * xhat[...]))).astype(BF)
    gc_out[...] = gc
    if fast:
        edge = rest[0]
        border = edge.shape[0]

        @pl.when((step == 0) & (flags[4, 1] == 1))
        def _():
            edge[...] = gc[:border]

        @pl.when((step == last) & (flags[4, 1] == 0))
        def _():
            edge[...] = gc[gc.shape[0] - border :]

    sums[5] += fold(gc.astype(F32))

    @pl.when(step == last)
    def _():
        if not fast:
            up_out, down_out, sums_out, ub_out = rest[:4]
            up_out[...] = dup[...]
            down_out[...] = ddown[...]
            sums_out[...] = jnp.sum(sums[...], 1)
            ub_out[...] = jnp.sum(ub_sums[...], 0, keepdims=True)
            return
        send, keep = rest[1:3]
        mine = flags[3, 0] == 0
        block = send.shape[-1]
        half = width // 2
        devices = 2 * (hidden // block)

        def own(length):
            each = length // devices
            place = lax.broadcasted_iota(jnp.int32, (devices, length), 1) // each
            return place == lax.broadcasted_iota(jnp.int32, (devices, length), 0)

        def pick(length, start):
            each = length // devices
            place = lax.broadcasted_iota(jnp.int32, (length, 128), 0) % each + start
            return (place == lax.broadcasted_iota(jnp.int32, (length, 128), 1)).astype(BF)

        first = None
        for v in range(6):
            line = jnp.sum(sums[v], 0, keepdims=True)
            part = dot(jnp.where(own(width), line, 0.0).astype(BF), pick(width, v * (width // devices)), NN)
            first = part if first is None else first + part
        line = jnp.sum(ub_sums[...], 0, keepdims=True)
        second = dot(jnp.where(own(hidden), line, 0.0).astype(BF), pick(hidden, 0), NN)
        index = lax.broadcasted_iota(jnp.int32, (16, 128), 0)

        def tail(b, s):
            at = 2 * b + s
            return jnp.where(index == 0, first[at : at + 1], jnp.where(index == 1, second[at : at + 1], 0.0)).astype(BF)

        for b in range(0, hidden // block, 2):
            for s in range(2):
                take = slice(s * half, (s + 1) * half)
                x_bit, z = b // 2 % 2, (b // 4 % 2, b // 8)
                up_at, down_at = (2 * x_bit + s, *z), (2 * s + x_bit, *z)
                for acc, at, start in ((dup, up_at, 0), (ddown, down_at, half + 16)):
                    lo = acc[take, b * block : (b + 1) * block].astype(BF)
                    hi = acc[take, (b + 1) * block : (b + 2) * block].astype(BF)
                    send[(*at, slice(start, start + half))] = jnp.where(mine, hi, lo)
                    keep[(*at, slice(start, start + half))] = jnp.where(mine, lo, hi)
                lo, hi = tail(b, s), tail(b + 1, s)
                send[(*up_at, slice(half, half + 16))] = jnp.where(mine, hi, lo)
                keep[(*up_at, slice(half, half + 16))] = jnp.where(mine, lo, hi)


def ffn(flags, x, xhat, scale, og, table, sources, plan, rows, chunk, batch, fast):
    count, width = x.shape
    hidden = table.shape[1]
    tile = pl.BlockSpec((rows, width), lambda j, f: (j, 0))
    sds = jax.ShapeDtypeStruct
    if fast:
        border = KERNEL_TAPS // 2 * DILATION_STEP
        shapes = [sds((border, width), BF)] + [sds((4, 2, 2, width + 16, hidden // batch), BF)] * 2
    else:
        shapes = [sds(s, F32) for s in ((width, hidden), (width, hidden), (6, width), (1, hidden))]
    anywhere = [pl.BlockSpec(memory_space=pl.ANY)] * len(sources)
    return pl.pallas_call(
        functools.partial(ffn_kernel, chunk, fast, plan),
        grid_spec=pltpu.PrefetchScalarGridSpec(
            num_scalar_prefetch=1,
            grid=(count // rows,),
            in_specs=[tile, tile, tile, tile, whole_block(table.shape)] + anywhere,
            out_specs=[tile, tile, tile] + [whole_block(s.shape) for s in shapes],
            scratch_shapes=[
                pltpu.VMEM((rows, hidden), BF),
                pltpu.VMEM((rows, hidden), F32),
                pltpu.VMEM((width, hidden), F32),
                pltpu.VMEM((width, hidden), F32),
                pltpu.VMEM((6, 8, width), F32),
                pltpu.VMEM((8, hidden), F32),
                pltpu.VMEM((2, hidden, width), BF),
                pltpu.SemaphoreType.DMA((count_copies(plan),)),
            ],
        ),
        out_shape=[pltpu.HBM((count, width), BF), pltpu.HBM((count, width), F32), (pltpu.VMEM if fast else pltpu.HBM)((count, width), BF)] + shapes,
        compiler_params=pltpu.CompilerParams(vmem_limit_bytes=VMEM_FFN if fast else VMEM_PACK),
        cost_estimate=pl.CostEstimate(flops=12 * count * width * hidden // COST, bytes_accessed=2**20, transcendentals=0),
        name="feed_forward",
    )(flags, x, xhat, scale, og, table, *sources)


def conv_weight_kernel(fast, first, flags, prev, x, nxt, g, *rest):
    ext, col = rest[-2:]
    outs = rest[:-2] if first == 0 else rest[2:-2]
    tap = pl.program_id(0) + first
    count, width = g.shape
    border = prev.shape[0]
    subs = count // SUB

    @pl.when(tap == first)
    def _():
        ext[0:border] = prev[...]
        ext[border : border + count] = x[...]
        ext[border + count :] = nxt[...]

    o = (tap - KERNEL_TAPS // 2) * DILATION_STEP
    offset = lax.broadcasted_iota(jnp.int32, (SUB, 1), 0) + o
    for r in range(subs):
        own = flags[2, r].astype(F32)
        before = flags[0, r].astype(F32)
        after = flags[1, r].astype(F32)
        mask = jnp.where(offset < 0, before, jnp.where(offset >= SUB, after, own)).astype(BF)
        rows = ext[pl.ds(pl.multiple_of(r * SUB + o + border, DILATION_STEP), SUB), :]
        col[r * SUB : (r + 1) * SUB, :] = rows * mask

    grad = dot(g[...], col[...], TN)
    if not fast:
        outs[0][0] = grad
        return
    mine = flags[3, 0] == 0
    half = width // 2

    send, keep = outs
    block = send.shape[4]
    early = (tap < (KERNEL_TAPS + 1) // 2).astype(jnp.int32)
    for s in range(2):
        columns = slice(s * half, (s + 1) * half)
        for b in range(0, width // block, 2):
            bit = b // 2 % 2
            at = (early * (2 * bit + s) + (1 - early) * (2 * s + bit), b // 4 % 2, b // 8, 0)
            lo = grad[b * block : (b + 1) * block, columns].astype(BF)
            hi = grad[(b + 1) * block : (b + 2) * block, columns].astype(BF)
            send[at] = jnp.where(mine, hi, lo)
            keep[at] = jnp.where(mine, lo, hi)


def conv_weight_backward(flags, prev, x, nxt, g, batch, fast, first=0, taps=KERNEL_TAPS, into=()):
    count, width = x.shape
    if fast:
        block = (4, 2, 2, 1, width // batch, width // 2)
        specs = [pl.BlockSpec(block, lambda k, f: (0, 0, 0, k + first, 0, 0))] * 2
        shapes = [jax.ShapeDtypeStruct(block[:3] + (KERNEL_TAPS,) + block[4:], BF)] * 2
    else:
        specs = [pl.BlockSpec((1, width, width), lambda k, f: (k, 0, 0))]
        shapes = [jax.ShapeDtypeStruct((KERNEL_TAPS, width, width), F32)]
    return pl.pallas_call(
        functools.partial(conv_weight_kernel, fast, first),
        grid_spec=pltpu.PrefetchScalarGridSpec(
            num_scalar_prefetch=1,
            grid=(taps,),
            in_specs=[whole_block(a.shape) for a in (prev, x, nxt, g)] + [pl.BlockSpec(memory_space=pl.ANY)] * len(into),
            out_specs=specs,
            scratch_shapes=[
                pltpu.VMEM((count + 2 * prev.shape[0], width), BF),
                pltpu.VMEM((count, width), BF),
            ],
        ),
        out_shape=shapes,
        compiler_params=pltpu.CompilerParams(vmem_limit_bytes=VMEM_CONV),
        cost_estimate=conv_cost(count * taps // KERNEL_TAPS, width),
        input_output_aliases={5 + i: i for i in range(len(into))},
        name="conv_weight_backward",
    )(flags, prev, x, nxt, g, *into)


def conv_input_kernel(subs, flags, prev, g, nxt, gh, w, out, ext, col):
    step = pl.program_id(0)
    count, width = g.shape
    border = prev.shape[0]

    @pl.when(step == 0)
    def _():
        ext[0:border] = prev[...]
        ext[border : border + count] = g[...]
        ext[border + count :] = nxt[...]

    def load(start, size):
        return ext[pl.ds(pl.multiple_of(start + border, DILATION_STEP), size), :]

    fill_columns(col, load, flags, step, subs, width)
    total = gh[...]
    for k in range(KERNEL_TAPS):
        total = total + dot(col[:, k * width : (k + 1) * width], w[KERNEL_TAPS - 1 - k], NN)
    out[...] = total


def conv_input_backward(flags, prev, g, nxt, gh, weights, subs):
    count, width = g.shape
    rows = subs * SUB
    tile = pl.BlockSpec((rows, width), lambda j, f: (j, 0))
    return pl.pallas_call(
        functools.partial(conv_input_kernel, subs),
        grid_spec=pltpu.PrefetchScalarGridSpec(
            num_scalar_prefetch=1,
            grid=(count // rows,),
            in_specs=[whole_block(a.shape) for a in (prev, g, nxt)] + [tile, whole_block(weights.shape)],
            out_specs=tile,
            scratch_shapes=[
                pltpu.VMEM((count + 2 * prev.shape[0], width), BF),
                pltpu.VMEM((rows, KERNEL_TAPS * width), BF),
            ],
        ),
        out_shape=jax.ShapeDtypeStruct((count, width), F32),
        compiler_params=pltpu.CompilerParams(vmem_limit_bytes=VMEM_CONV),
        cost_estimate=conv_cost(count, width),
        name="conv_input_backward",
    )(flags, prev, g, nxt, gh, weights)


def pack_kernel(small, slots, count, lengths, first, final, conv, up, down, *rest):
    vectors, (flags, halo, conv_out, pair_out) = rest[: len(small)], rest[len(small) :]
    batch_index = lax.axis_index("z") * 4 + lax.axis_index("x") * 2 + lax.axis_index("core")
    seq_index = lax.axis_index("seq")
    taps, rows, wide = conv.shape
    subs = flags.shape[1]
    conv_out[0, 0:taps] = conv[...]
    line = None
    for v, (start, each) in zip(vectors, small):
        pick = (
            lax.broadcasted_iota(jnp.int32, (each, wide), 0) + start == lax.broadcasted_iota(jnp.int32, (each, wide), 1)
        ).astype(BF)
        part = dot(jnp.broadcast_to(v[...], (rows, each)), pick, NN)
        line = part if line is None else line + part
    conv_out[0, taps] = line.astype(BF)
    pair_out[0, 0] = up[...].T
    pair_out[0, 1] = down[...]
    halo[...] = jnp.where(seq_index == 0, final[...], first[...])
    ends = []
    total = 0
    for i in range(slots):
        total = total + lengths[0, i]
        ends.append(total)
    ids = []
    for j in range(-1, subs + 1):
        start = seq_index * count + j * SUB
        number = 0
        for end in ends:
            number = number + (start >= end).astype(jnp.int32)
        ids.append(jnp.where(start >= 0, number, -1))
    for j in range(subs):
        inside = (ids[j + 1] < slots).astype(jnp.int32)
        flags[0, j] = (ids[j] == ids[j + 1]).astype(jnp.int32) * inside
        flags[1, j] = (ids[j + 2] == ids[j + 1]).astype(jnp.int32) * inside
        flags[2, j] = inside
        flags[3, j] = batch_index % 2
        flags[4, j] = batch_index if j == 0 else seq_index
        bits = (lax.axis_index("x"), seq_index, lax.axis_index("z") % 2, lax.axis_index("z") // 2)
        flags[5, j] = bits[min(j, 3)]


def pack(lengths, x, conv, up, down, vectors, small):
    taps, rows, wide = conv.shape
    count, width = x.shape
    border = KERNEL_TAPS // 2 * DILATION_STEP
    smem = pl.BlockSpec(memory_space=pltpu.SMEM)
    arrays = [conv, up, down] + [v[None] for v in vectors]
    end_rows = pl.BlockSpec((border, width), lambda i: (0, 0))
    final_rows = pl.BlockSpec((border, width), lambda i: (count // border - 1, 0))
    sds = jax.ShapeDtypeStruct
    outs = [
        sds((6, count // SUB), jnp.int32),
        sds((border, width), BF),
        sds((1, taps + 1, rows, wide), BF),
        sds((1, 2) + down.shape, BF),
    ]
    return pl.pallas_call(
        functools.partial(pack_kernel, small, lengths.shape[1], count),
        grid=(1,),
        in_specs=[smem, end_rows, final_rows] + [whole_block(a.shape) for a in arrays],
        out_specs=[smem] + [whole_block(o.shape) for o in outs[1:]],
        out_shape=outs,
        compiler_params=pltpu.CompilerParams(vmem_limit_bytes=VMEM_PACK),
        name="pack",
    )(lengths, x, x, *arrays)


def swap(value, link):
    axis, bit = link
    return lax.ppermute(value, axis, [(i, i ^ bit) for i in range(lax.axis_size(axis))])


def half_of(link):
    return (lax.axis_index(link[0]) // link[1]) % 2


def give_half(value, link, dim):
    return lax.dynamic_index_in_dim(value, 1 - half_of(link), dim, keepdims=False).astype(BF)


def keep_half(value, link, dim):
    return lax.dynamic_index_in_dim(value, half_of(link), dim, keepdims=False).astype(F32)


def after(value, *others):
    return lax.optimization_barrier((value, *others))[0]


def shifted(offsets, b, s):
    return tuple((ob ^ b, os ^ s) for ob, os in offsets)


def both_cores(arrays, plan):
    other = [swap(a, CORE) for a in arrays]
    return arrays + other, tuple(plan) + tuple((shifted(o, 1, 0), first) for o, first in plan)


def gather(own, pair, halo):
    cut = own.shape[1] // 2
    top = lambda value: swap(value[:, :cut], Y)
    bottom = lambda value: swap(value[:, cut:], X)
    halo, own_y, own_x, far = lax.optimization_barrier((swap(halo, Y), swap(own, Y), swap(own, X), swap(own, Z1)))
    column = jnp.concatenate([own, far], 0)
    near, far_x, far_y, own_top, own_bottom = lax.optimization_barrier(
        (swap(column, Z0), swap(far, X), swap(far, Y), top(own_x), bottom(own_y))
    )
    pair = after(pair, near, own_top)
    near_x, near_y, far_top, far_bottom, pair_far = lax.optimization_barrier(
        (swap(near, X), swap(near, Y), top(far_x), bottom(far_y), swap(pair, Z1))
    )
    near_top, near_bottom = top(near_x), bottom(near_y)
    pair = jnp.concatenate([pair, pair_far], 0)
    pair = jnp.concatenate([pair, swap(pair, Z0)], 0)
    pair_x, pair_y = swap(pair, X), swap(pair, Y)
    across = lax.ppermute(pair, ("x", "seq"), [(i, i ^ 3) for i in range(4)])
    offsets = ((0, 0), (8, 0), (4, 0), (12, 0))
    pair_plan = [(shifted(offsets, b, s), 0) for b, s in ((0, 0), (2, 0), (0, 1), (2, 1))]
    arrays, plan = [column, near], [(((0, 0), (8, 0)), 0), (((4, 0), (12, 0)), 0)]
    for offsets, members in (
        (((0, 0),), (own_x, own_y, own_top, own_bottom)),
        (((8, 0),), (far_x, far_y, far_top, far_bottom)),
        (((4, 0), (12, 0)), (near_x, near_y, near_top, near_bottom)),
    ):
        arrays += members
        plan += [(shifted(offsets, b, s), first) for b, s, first in ((2, 0, 0), (0, 1, 0), (2, 1, 0), (2, 1, cut))]
    return halo, both_cores(arrays, plan), ([pair, pair_x, pair_y, across], pair_plan)


def stage_kernel(columns, joined, flags, *refs):
    count = len(columns)
    outs = refs[2 * count :]
    at = 0
    for i, column in enumerate(columns):
        keep, got = refs[2 * i], refs[2 * i + 1]
        if joined is None:
            give_out, keep_out, where = outs[2 * i], outs[2 * i + 1], Ellipsis
        else:
            taps = keep.shape[1 + joined]
            give_out, keep_out = outs
            where = (*(slice(None),) * joined, slice(at, at + taps))
            at += taps
        bit = flags[5, column]
        give_out[where] = (keep[1 - bit].astype(F32) + got[1 - bit].astype(F32)).astype(BF)
        keep_out[where] = keep[bit].astype(F32) + got[bit].astype(F32)


def first_stage_kernel(cut, flags, keep, got, *outs):
    for i, taps in enumerate((slice(0, cut), slice(cut, keep.shape[3]))):
        bit = flags[5, i]
        give_out, keep_out = outs[2 * i], outs[2 * i + 1]
        for n in range(2):
            other, own = 2 * (1 - bit) + n, 2 * bit + n
            give_out[n] = (keep[other, :, :, taps].astype(F32) + got[other, :, :, taps].astype(F32)).astype(BF)
            keep_out[n] = keep[own, :, :, taps].astype(F32) + got[own, :, :, taps].astype(F32)


def first_stage(flags, keep, got, cut):
    tail = keep.shape[4:]
    outs = [jax.ShapeDtypeStruct((2, 2, 2, n) + tail, kind) for n in (cut, keep.shape[3] - cut) for kind in (BF, F32)]
    return pl.pallas_call(
        functools.partial(first_stage_kernel, cut),
        grid_spec=pltpu.PrefetchScalarGridSpec(
            num_scalar_prefetch=1,
            grid=(1,),
            in_specs=[whole_block(keep.shape)] * 2,
            out_specs=[whole_block(o.shape) for o in outs],
        ),
        out_shape=outs,
        compiler_params=pltpu.CompilerParams(vmem_limit_bytes=VMEM_SUM),
        name="stage",
    )(flags, keep, got)


def stage(flags, parts, columns, joined=None):
    shapes = [keep.shape[1:] for keep, _ in parts]
    if joined is not None:
        first = list(shapes[0])
        first[joined] = sum(shape[joined] for shape in shapes)
        shapes = [tuple(first)]
    outs = [jax.ShapeDtypeStruct(shape, kind) for shape in shapes for kind in (BF, F32)]
    arrays = [a for part in parts for a in part]
    return pl.pallas_call(
        functools.partial(stage_kernel, columns, joined),
        grid_spec=pltpu.PrefetchScalarGridSpec(
            num_scalar_prefetch=1,
            grid=(1,),
            in_specs=[whole_block(a.shape) for a in arrays],
            out_specs=[whole_block(o.shape) for o in outs],
        ),
        out_shape=outs,
        compiler_params=pltpu.CompilerParams(vmem_limit_bytes=VMEM_SUM),
        name="stage",
    )(flags, *arrays)


def local(inputs, window_lengths, conv_weight, conv_bias, norm1_gain, norm1_bias, up_weight, up_bias, down_weight,
          down_bias, norm2_gain, norm2_bias, out_grad):
    _, count, width = inputs.shape
    batch, seq = lax.axis_size(BATCH), lax.axis_size("seq")
    hidden = up_weight.shape[1] * batch
    border = KERNEL_TAPS // 2 * DILATION_STEP
    x, og = inputs[0], pltpu.with_memory_space_constraint(out_grad[0], pltpu.HBM)
    fast = seq == 2 and batch == 16

    def ends(value):
        first, final = value[:border], value[count - border :]
        if fast:
            other = swap(jnp.where(lax.axis_index("seq") == 0, final, first), Y)
            return other, other
        up = [(i, i + 1) for i in range(seq - 1)]
        return lax.ppermute(final, "seq", up), lax.ppermute(first, "seq", [(j, i) for i, j in up])

    vectors = [conv_bias, norm1_gain, norm1_bias, down_bias, norm2_gain, norm2_bias, up_bias]
    sizes = [v.shape[0] for v in vectors]
    small = tuple((sum(sizes[:i]), n) for i, n in enumerate(sizes))
    conv_own = conv_weight.transpose(0, 2, 1)
    flags, halo, conv_block, pair_block = pack(window_lengths, x, conv_own, up_weight, down_weight, vectors, small)
    if fast:
        halo, (conv_pieces, conv_plan), (pair_pieces, pair_plan) = gather(conv_block, pair_block, halo)
        prev = nxt = halo
        table = None
    else:
        def every(value):
            value = lax.all_gather(value, "seq", axis=2, tiled=True)
            return lax.all_gather(value, BATCH, axis=1, tiled=True)

        prev, nxt = ends(x)
        conv_pieces, conv_plan = [every(conv_own)], ((None, 0),)
        pair_pieces, pair_plan = [every(pair_block[0])], ((None, 0),)
        full = [lax.all_gather(v, (*BATCH, "seq"), axis=0, tiled=True).astype(F32) for v in vectors]
        table = jnp.stack([jnp.pad(v, (0, hidden - v.shape[0])) for v in full + [full[0]]])
        small = ()
    conv_pieces, conv_plan = list(conv_pieces), tuple((None if o is None else tuple(o), f) for o, f in conv_plan)
    xhat, scale, conv_full, table = conv_forward(flags, prev, x, nxt, conv_pieces, conv_plan, small, table, 2, hidden)
    if fast:
        (column, over_x, over_y, across), table = lax.optimization_barrier((pair_pieces, table))
        others = [swap(a, CORE) for a in (column, over_x, over_y)]
        others, across = lax.optimization_barrier((others, across))
        pair_pieces = [column, over_x, over_y, across] + others + [swap(across, CORE)]
        pair_plan = tuple(pair_plan) + tuple((shifted(o, 1, 0), first) for o, first in pair_plan)
    pair_plan = tuple((None if o is None else tuple(o), f) for o, f in pair_plan)
    block_output, grad_hidden, grad_conv, *ffn_grads = ffn(
        flags, x, xhat, scale, og, table, pair_pieces, pair_plan, 2 * SUB, min(1024, hidden), batch, fast
    )
    grads = (flags, prev, x, nxt, grad_conv, grad_hidden, conv_full)
    if fast:
        input_grad, weight_grads = paired(grads, ffn_grads, batch, width, hidden)
    else:
        grad_prev, grad_next = ends(grad_conv)
        conv_grads = conv_weight_backward(flags, prev, x, nxt, grad_conv, batch, fast)
        input_grad = conv_input_backward(flags, grad_prev, grad_conv, grad_next, grad_hidden, conv_full, 2)
        weight_grads = whole_sums(conv_grads, ffn_grads, batch, seq, width, hidden)
    conv_grad, cb, g1, s1, up_grad, ub_grad, down_grad, db, g2, s2 = weight_grads
    return (block_output[None], input_grad[None], conv_grad, cb, g1, s1, up_grad, ub_grad, down_grad, db, g2, s2)


def paired(grads, ffn_grads, batch, width, hidden):
    flags, prev, x, nxt, grad_conv, grad_hidden, conv_full = grads
    up_rows = width // 2 + 16
    edge, ffn_send, ffn_keep = ffn_grads
    ffn_got, grad_prev = swap(ffn_send, CORE), swap(edge, Y)
    early = 2
    parts = conv_weight_backward(flags, prev, x, prev, grad_conv, batch, True, 0, early)
    ffn_got, grad_prev, parts = lax.optimization_barrier((ffn_got, grad_prev, parts))
    up_give, up_keep, down_give, down_keep = first_stage(flags, ffn_keep, ffn_got, up_rows)
    up_got, down_got = swap(up_give, X), swap(down_give, Y)
    first = after(prev, up_give)
    send, keep = conv_weight_backward(
        flags, first, x, first, grad_conv, batch, True, early, KERNEL_TAPS - early, parts
    )
    up_got, down_got, send = lax.optimization_barrier((up_got, down_got, send))
    got = swap(send, CORE)
    parts = [(up_keep, up_got), (down_keep, down_got)]
    up_give, up_keep, down_give, down_keep = stage(flags, parts, (1, 0))
    up_got, down_got = swap(up_give, Y), swap(down_give, X)
    upper_give, upper_keep, lower_give, lower_keep = first_stage(
        flags, keep, after(got, up_give), (KERNEL_TAPS + 1) // 2
    )
    upper_got, lower_got = swap(upper_give, X), swap(lower_give, Y)
    second = after(grad_prev, upper_give)
    input_grad = conv_input_backward(flags, second, grad_conv, second, grad_hidden, conv_full, 2)
    up_got, down_got, input_grad = lax.optimization_barrier((up_got, down_got, input_grad))
    ffn_give, ffn_keep = stage(flags, [(up_keep, up_got), (down_keep, down_got)], (2, 2), 1)
    ffn_got = swap(ffn_give, Z0)
    upper_got, lower_got, _ = lax.optimization_barrier((upper_got, lower_got, ffn_give))
    parts = [(upper_keep, upper_got), (lower_keep, lower_got)]
    upper_give, upper_keep, lower_give, lower_keep = stage(flags, parts, (1, 0))
    upper_got, lower_got = swap(upper_give, Y), swap(lower_give, X)
    ffn_give, ffn_keep = stage(flags, [(ffn_keep, after(ffn_got, upper_give))], (3,))
    ffn_got = swap(ffn_give, Z1)
    upper_got, lower_got, _ = lax.optimization_barrier((upper_got, lower_got, ffn_give))
    conv_give, conv_keep = stage(flags, [(upper_keep, upper_got), (lower_keep, lower_got)], (2, 2), 1)
    conv_got = swap(conv_give, Z0)
    pair_part = ffn_keep + after(ffn_got, conv_give).astype(F32)
    conv_give, conv_keep = stage(flags, [(conv_keep, conv_got)], (3,))
    conv_got = swap(conv_give, Z1)
    conv_grad = (conv_keep + conv_got.astype(F32)).transpose(0, 2, 1)
    head = width // 2
    up_grad = pair_part[:head]
    down_grad = pair_part[up_rows:].T
    each = width // (batch * 2)
    g2, s2, db, g1, s1, cb = (pair_part[head, i * each : (i + 1) * each] for i in range(6))
    ub_grad = pair_part[head + 1, : hidden // (batch * 2)]
    return input_grad, (conv_grad, cb, g1, s1, up_grad, ub_grad, down_grad, db, g2, s2)


def whole_sums(conv_grads, ffn_grads, batch, seq, width, hidden):
    def total(value, dims):
        value = lax.psum_scatter(value, BATCH, scatter_dimension=dims[1], tiled=True)
        return lax.psum_scatter(value, "seq", scatter_dimension=dims[0], tiled=True)

    conv_grad = total(conv_grads[0], (2, 1)).transpose(0, 2, 1)
    up_grad = total(ffn_grads[0], (0, 1))
    down_grad = total(ffn_grads[1], (0, 1)).T
    vec_grads = total(ffn_grads[2].reshape(6, batch, seq, -1), (2, 1)).reshape(6, -1)
    ub_grad = total(ffn_grads[3].reshape(batch, seq, -1), (1, 0)).reshape(-1)
    g2, s2, db, g1, s1, cb = (vec_grads[i] for i in range(6))
    return conv_grad, cb, g1, s1, up_grad, ub_grad, down_grad, db, g2, s2


def solution(mesh):
    batch, seq = mesh.shape["batch"], mesh.shape["seq"]
    split = Mesh(mesh.devices.reshape(batch // 4, 2, 2, seq), (*BATCH, "seq"))
    both = P((*BATCH, "seq"))
    rows = P(BATCH, "seq", None)
    conv, up, down = P(None, "seq", BATCH), P("seq", BATCH), P(BATCH, "seq")
    in_specs = (rows, P(BATCH, None), conv, both, both, both, up, both, down, both, both, both, rows)
    out_specs = (rows, rows, conv, both, both, both, up, both, down, both, both, both)
    return jax.shard_map(local, mesh=split, in_specs=in_specs, out_specs=out_specs, check_vma=False)
```

```python
import functools
import jax
import jax.numpy as jnp
from jax import lax
from jax.experimental import pallas as pl
from jax.experimental.pallas import tpu as pltpu
from jax.sharding import Mesh, PartitionSpec as P

KERNEL_TAPS = 9
DILATION_STEP = 32
EPSILON = 1e-05
SUB = 256
BF = jnp.bfloat16
F32 = jnp.float32
VMEM_CONV = 28 * 2**20
VMEM_FFN = 51 * 2**20
VMEM_FIRST = 30 * 2**20
VMEM_PACK = 60 * 2**20
VMEM_SUM = 24 * 2**20
COST = 1
BATCH = ("z", "x", "core")
X, Y, Z0, Z1, CORE = ("x", 1), ("seq", 1), ("z", 1), ("z", 2), ("core", 1)
NN = (((1,), (0,)), ((), ()))
NT = (((1,), (1,)), ((), ()))
TN = (((0,), (0,)), ((), ()))


def dot(a, b, dims):
    return lax.dot_general(a, b, dims, preferred_element_type=F32)


def conv_cost(count, width):
    return pl.CostEstimate(flops=2 * count * KERNEL_TAPS * width * width // COST, bytes_accessed=2**20, transcendentals=0)


def gelu_pair(v):
    size = jnp.abs(v)
    t = pl.reciprocal(1.0 + 0.23164189 * size, approx=True)
    poly = t * (0.127414796 + t * (-0.142248368 + t * (0.710706871 + t * (-0.726576013 + t * 0.530702714))))
    bell = jnp.exp2(-0.72134752 * (size * size))
    value = jnp.maximum(v, 0.0) - size * (poly * bell)
    low_side = bell * (poly - 0.39894228 * size)
    return value, jnp.where(v >= 0.0, 1.0 - low_side, low_side)


def row_mean(v):
    return jnp.sum(v, -1, keepdims=True) * (1.0 / v.shape[-1])


def fold(v):
    total = v[0:8]
    for r in range(8, v.shape[0], 8):
        total = total + v[r : r + 8]
    return total


def fill_columns(col, load, flags, block, subs, width):
    for r in range(subs):
        j = block * subs + r
        base = j * SUB
        own = flags[2, j].astype(F32).astype(BF)
        before = flags[0, j].astype(F32).astype(BF)
        after = flags[1, j].astype(F32).astype(BF)
        for k in range(KERNEL_TAPS):
            o = (k - KERNEL_TAPS // 2) * DILATION_STEP
            columns = slice(k * width, (k + 1) * width)
            first = r * SUB
            if o < 0:
                col[first : first - o, columns] = load(base + o, -o) * before
                col[first - o : first + SUB, columns] = load(base, SUB + o) * own
            elif o == 0:
                col[first : first + SUB, columns] = load(base, SUB) * own
            else:
                col[first : first + SUB - o, columns] = load(base + o, SUB - o) * own
                col[first + SUB - o : first + SUB, columns] = load(base + SUB, o) * after


def place(plan, batch_index, seq_index, sources, whole, sems):
    copies = []
    taps = whole.shape[0]
    for source, (offsets, first) in zip(sources, plan):
        if offsets is None:
            copies.append(pltpu.make_async_copy(source, whole, sems.at[len(copies)]))
            continue
        _, span, rows, wide = source.shape
        span = min(span, taps - max(first, 0))
        for n, (db, ds) in enumerate(offsets):
            b, s = (db, ds) if first < 0 else (batch_index ^ db, seq_index ^ ds)
            at_rows = pl.ds(pl.multiple_of(b * rows, rows), rows)
            at_columns = pl.ds(pl.multiple_of(s * wide, wide), wide)
            target = whole.at[pl.ds(max(first, 0), span), at_rows, at_columns]
            copies.append(pltpu.make_async_copy(source.at[n, pl.ds(0, span)], target, sems.at[len(copies)]))
    return copies


def count_copies(plan):
    return sum(1 if offsets is None else len(offsets) for offsets, _ in plan)


def spread_table(small, rows, out):
    devices, wide = rows.shape
    for v, (start, each) in enumerate(small):
        length = devices * each
        place_of = lax.broadcasted_iota(jnp.int32, (wide, length), 1) % each + start
        pick = (place_of == lax.broadcasted_iota(jnp.int32, (wide, length), 0)).astype(BF)
        values = dot(rows, pick, NN)
        owner = lax.broadcasted_iota(jnp.int32, (devices, length), 1) // each
        row = lax.broadcasted_iota(jnp.int32, (devices, length), 0)
        own = owner == 2 * (row % (devices // 2)) + row // (devices // 2)
        out[v : v + 1, :length] = jnp.sum(jnp.where(own, values, 0.0), 0, keepdims=True)


def conv_kernel(subs, plan, small, flags, prev, x, nxt, *rest):
    block = pl.program_id(0)
    width = x.shape[1]
    border = prev.shape[0]
    sources = rest[: len(plan)]
    if small:
        xhat_out, scale_out, w_out, table, ext, col, w, sems, out_sem = rest[len(plan) :]
        small_rows = sources[0].shape[2]
    else:
        table, xhat_out, scale_out, w_out, ext, col, w, sems, out_sem = rest[len(plan) :]

    def copies_in():
        return place(plan, flags[4, 0], flags[4, 1], sources, w, sems)

    def whole_out():
        return pltpu.make_async_copy(w.at[pl.ds(0, KERNEL_TAPS)], w_out, out_sem)

    @pl.when(block == 0)
    def _():
        for copy in copies_in():
            copy.start()
        ext[0:border] = prev[...]
        ext[border : border + x.shape[0]] = x[...]
        ext[border + x.shape[0] :] = nxt[...]

        for copy in copies_in():
            copy.wait()
        whole_out().start()
        if small:
            blocks = width // small_rows
            first_row = lax.broadcasted_iota(jnp.int32, (blocks, width), 0) * small_rows
            pick = (first_row == lax.broadcasted_iota(jnp.int32, (blocks, width), 1)).astype(BF)
            rows = dot(pick, w[KERNEL_TAPS], NN).astype(BF)
            spread_table(small, jnp.concatenate([rows[:, : width // 2], rows[:, width // 2 :]], 0), table)

    @pl.when(block == pl.num_programs(0) - 1)
    def _():
        whole_out().wait()

    def load(start, count):
        return ext[pl.ds(pl.multiple_of(start + border, DILATION_STEP), count), :]

    fill_columns(col, load, flags, block, subs, width)
    total = None
    for k in range(KERNEL_TAPS):
        part = dot(col[:, k * width : (k + 1) * width], w[k], NT)
        total = part if total is None else total + part
    value, slope = gelu_pair(total + table[0:1, :width])
    centered = value - row_mean(value)
    rstd = lax.rsqrt(row_mean(centered * centered) + EPSILON)
    xhat_out[...] = centered * rstd
    scale_out[...] = slope * rstd


def whole_block(shape):
    return pl.BlockSpec(shape, lambda *_: (0,) * len(shape), pipeline_mode=pl.Buffered(1))


def conv_forward(flags, prev, x, nxt, sources, plan, small, table, subs, hidden):
    count, width = x.shape
    rows = subs * SUB
    anywhere = [pl.BlockSpec(memory_space=pl.ANY)] * len(sources)
    out_specs = [pl.BlockSpec((rows, width), lambda j, f: (j, 0))] * 2 + [pl.BlockSpec(memory_space=pltpu.HBM)]
    out_shape = [pltpu.HBM((count, width), F32)] * 2 + [pltpu.HBM((KERNEL_TAPS, width, width), BF)]
    scratch = [
        pltpu.VMEM((count + 2 * prev.shape[0], width), BF),
        pltpu.VMEM((rows, KERNEL_TAPS * width), BF),
        pltpu.VMEM((KERNEL_TAPS + bool(small), width, width), BF),
        pltpu.SemaphoreType.DMA((count_copies(plan),)),
        pltpu.SemaphoreType.DMA,
    ]
    extra_specs, extra = [], []
    if small:
        out_specs = out_specs + [whole_block((8, hidden))]
        out_shape = out_shape + [jax.ShapeDtypeStruct((8, hidden), F32)]
    else:
        extra_specs, extra = [whole_block(table.shape)], [table]
    outs = pl.pallas_call(
        functools.partial(conv_kernel, subs, plan, small),
        grid_spec=pltpu.PrefetchScalarGridSpec(
            num_scalar_prefetch=1,
            grid=(count // rows,),
            in_specs=[whole_block(prev.shape), whole_block(x.shape), whole_block(nxt.shape)] + anywhere + extra_specs,
            out_specs=out_specs,
            scratch_shapes=scratch,
        ),
        out_shape=out_shape,
        compiler_params=pltpu.CompilerParams(vmem_limit_bytes=VMEM_FIRST),
        cost_estimate=pl.CostEstimate(flops=1, bytes_accessed=1, transcendentals=0),
        name="conv_forward",
    )(flags, prev, x, nxt, *sources, *extra)
    return outs if small else (*outs, table)


def ffn_kernel(chunk, fast, plan, flags, x, xhat, scale, og, table, *rest):
    sources, rest = rest[: len(plan)], rest[len(plan) :]
    out, gh_out, gc_out, *rest = rest
    act, slope, dup, ddown, sums, ub_sums, pair, sems = rest[-8:]
    step = pl.program_id(0)
    last = pl.num_programs(0) - 1
    _, hidden, width = pair.shape
    chunks = hidden // chunk
    gain1, shift1, db, gain2, shift2 = (table[i : i + 1, :width] for i in range(1, 6))
    ub = table[6:7, :]

    @pl.when(step == 0)
    def _():
        copies = place(plan, flags[4, 0], flags[4, 1], sources, pair, sems)
        for copy in copies:
            copy.start()
        dup[...] = jnp.zeros_like(dup)
        ddown[...] = jnp.zeros_like(ddown)
        sums[...] = jnp.zeros_like(sums)
        ub_sums[...] = jnp.zeros_like(ub_sums)
        for copy in copies:
            copy.wait()

    one = x[...].astype(F32) + (xhat[...] * gain1 + shift1)
    low = one.astype(BF)
    total = None
    for f in range(chunks):
        cols = slice(f * chunk, (f + 1) * chunk)
        value, s = gelu_pair(dot(low, pair[0, cols, :], NT) + ub[:, cols])
        a = value.astype(BF)
        act[:, cols] = a
        slope[:, cols] = s
        part = dot(a, pair[1, cols, :], NN)
        total = part if total is None else total + part
    d = total + db
    centered = d - row_mean(d)
    rstd = lax.rsqrt(row_mean(centered * centered) + EPSILON)
    hat = centered * rstd
    out[...] = (one + (hat * gain2 + shift2)).astype(BF)
    g = og[...].astype(F32)
    e = g * gain2
    gd = (rstd * (e - row_mean(e) - hat * row_mean(e * hat))).astype(BF)
    sums[0] += fold(g * hat)
    sums[1] += fold(g)
    sums[2] += fold(gd.astype(F32))
    gh = g
    for f in range(chunks):
        cols = slice(f * chunk, (f + 1) * chunk)
        ddown[:, cols] += dot(gd, act[:, cols], TN)
        gu = dot(gd, pair[1, cols, :], NT) * slope[:, cols]
        gul = gu.astype(BF)
        ub_sums[:, cols] += fold(gul.astype(F32))
        dup[:, cols] += dot(low, gul, TN)
        gh = gh + dot(gul, pair[0, cols, :], NN)
    gh_out[...] = gh
    sums[3] += fold(gh * xhat[...])
    sums[4] += fold(gh)
    e = gh * gain1
    gc = (scale[...] * (e - row_mean(e) - xhat[...] * row_mean(e * xhat[...]))).astype(BF)
    gc_out[...] = gc
    if fast:
        edge = rest[0]
        border = edge.shape[0]

        @pl.when((step == 0) & (flags[4, 1] == 1))
        def _():
            edge[...] = gc[:border]

        @pl.when((step == last) & (flags[4, 1] == 0))
        def _():
            edge[...] = gc[gc.shape[0] - border :]

    sums[5] += fold(gc.astype(F32))

    @pl.when(step == last)
    def _():
        if not fast:
            up_out, down_out, sums_out, ub_out = rest[:4]
            up_out[...] = dup[...]
            down_out[...] = ddown[...]
            sums_out[...] = jnp.sum(sums[...], 1)
            ub_out[...] = jnp.sum(ub_sums[...], 0, keepdims=True)
            return
        send, keep = rest[1:3]
        mine = flags[3, 0] == 0
        block = send.shape[-1]
        half = width // 2
        devices = 2 * (hidden // block)

        def own(length):
            each = length // devices
            place = lax.broadcasted_iota(jnp.int32, (devices, length), 1) // each
            return place == lax.broadcasted_iota(jnp.int32, (devices, length), 0)

        def pick(length, start):
            each = length // devices
            place = lax.broadcasted_iota(jnp.int32, (length, 128), 0) % each + start
            return (place == lax.broadcasted_iota(jnp.int32, (length, 128), 1)).astype(BF)

        first = None
        for v in range(6):
            line = jnp.sum(sums[v], 0, keepdims=True)
            part = dot(jnp.where(own(width), line, 0.0).astype(BF), pick(width, v * (width // devices)), NN)
            first = part if first is None else first + part
        line = jnp.sum(ub_sums[...], 0, keepdims=True)
        second = dot(jnp.where(own(hidden), line, 0.0).astype(BF), pick(hidden, 0), NN)
        index = lax.broadcasted_iota(jnp.int32, (16, 128), 0)

        def tail(b, s):
            at = 2 * b + s
            return jnp.where(index == 0, first[at : at + 1], jnp.where(index == 1, second[at : at + 1], 0.0)).astype(BF)

        for b in range(0, hidden // block, 2):
            for s in range(2):
                take = slice(s * half, (s + 1) * half)
                x_bit, z = b // 2 % 2, (b // 4 % 2, b // 8)
                up_at, down_at = (2 * x_bit + s, *z), (2 * s + x_bit, *z)
                for acc, at, start in ((dup, up_at, 0), (ddown, down_at, half + 16)):
                    lo = acc[take, b * block : (b + 1) * block].astype(BF)
                    hi = acc[take, (b + 1) * block : (b + 2) * block].astype(BF)
                    send[(*at, slice(start, start + half))] = jnp.where(mine, hi, lo)
                    keep[(*at, slice(start, start + half))] = jnp.where(mine, lo, hi)
                lo, hi = tail(b, s), tail(b + 1, s)
                send[(*up_at, slice(half, half + 16))] = jnp.where(mine, hi, lo)
                keep[(*up_at, slice(half, half + 16))] = jnp.where(mine, lo, hi)


def ffn(flags, x, xhat, scale, og, table, sources, plan, rows, chunk, batch, fast):
    count, width = x.shape
    hidden = table.shape[1]
    tile = pl.BlockSpec((rows, width), lambda j, f: (j, 0))
    sds = jax.ShapeDtypeStruct
    if fast:
        border = KERNEL_TAPS // 2 * DILATION_STEP
        shapes = [sds((border, width), BF)] + [sds((4, 2, 2, width + 16, hidden // batch), BF)] * 2
    else:
        shapes = [sds(s, F32) for s in ((width, hidden), (width, hidden), (6, width), (1, hidden))]
    anywhere = [pl.BlockSpec(memory_space=pl.ANY)] * len(sources)
    return pl.pallas_call(
        functools.partial(ffn_kernel, chunk, fast, plan),
        grid_spec=pltpu.PrefetchScalarGridSpec(
            num_scalar_prefetch=1,
            grid=(count // rows,),
            in_specs=[tile, tile, tile, tile, whole_block(table.shape)] + anywhere,
            out_specs=[tile, tile, tile] + [whole_block(s.shape) for s in shapes],
            scratch_shapes=[
                pltpu.VMEM((rows, hidden), BF),
                pltpu.VMEM((rows, hidden), F32),
                pltpu.VMEM((width, hidden), F32),
                pltpu.VMEM((width, hidden), F32),
                pltpu.VMEM((6, 8, width), F32),
                pltpu.VMEM((8, hidden), F32),
                pltpu.VMEM((2, hidden, width), BF),
                pltpu.SemaphoreType.DMA((count_copies(plan),)),
            ],
        ),
        out_shape=[pltpu.HBM((count, width), BF), pltpu.HBM((count, width), F32), (pltpu.VMEM if fast else pltpu.HBM)((count, width), BF)] + shapes,
        compiler_params=pltpu.CompilerParams(vmem_limit_bytes=VMEM_FFN if fast else VMEM_PACK),
        cost_estimate=pl.CostEstimate(flops=12 * count * width * hidden // COST, bytes_accessed=2**20, transcendentals=0),
        name="feed_forward",
    )(flags, x, xhat, scale, og, table, *sources)


def conv_weight_kernel(fast, first, flags, prev, x, nxt, g, *rest):
    ext, col = rest[-2:]
    outs = rest[:-2] if first == 0 else rest[2:-2]
    tap = pl.program_id(0) + first
    count, width = g.shape
    border = prev.shape[0]
    subs = count // SUB

    @pl.when(tap == first)
    def _():
        ext[0:border] = prev[...]
        ext[border : border + count] = x[...]
        ext[border + count :] = nxt[...]

    o = (tap - KERNEL_TAPS // 2) * DILATION_STEP
    offset = lax.broadcasted_iota(jnp.int32, (SUB, 1), 0) + o
    for r in range(subs):
        own = flags[2, r].astype(F32)
        before = flags[0, r].astype(F32)
        after = flags[1, r].astype(F32)
        mask = jnp.where(offset < 0, before, jnp.where(offset >= SUB, after, own)).astype(BF)
        rows = ext[pl.ds(pl.multiple_of(r * SUB + o + border, DILATION_STEP), SUB), :]
        col[r * SUB : (r + 1) * SUB, :] = rows * mask

    grad = dot(g[...], col[...], TN)
    if not fast:
        outs[0][0] = grad
        return
    mine = flags[3, 0] == 0
    half = width // 2

    send, keep = outs
    block = send.shape[4]
    early = (tap < (KERNEL_TAPS + 1) // 2).astype(jnp.int32)
    for s in range(2):
        columns = slice(s * half, (s + 1) * half)
        for b in range(0, width // block, 2):
            bit = b // 2 % 2
            at = (early * (2 * bit + s) + (1 - early) * (2 * s + bit), b // 4 % 2, b // 8, 0)
            lo = grad[b * block : (b + 1) * block, columns].astype(BF)
            hi = grad[(b + 1) * block : (b + 2) * block, columns].astype(BF)
            send[at] = jnp.where(mine, hi, lo)
            keep[at] = jnp.where(mine, lo, hi)


def conv_weight_backward(flags, prev, x, nxt, g, batch, fast, first=0, taps=KERNEL_TAPS, into=()):
    count, width = x.shape
    if fast:
        block = (4, 2, 2, 1, width // batch, width // 2)
        specs = [pl.BlockSpec(block, lambda k, f: (0, 0, 0, k + first, 0, 0))] * 2
        shapes = [jax.ShapeDtypeStruct(block[:3] + (KERNEL_TAPS,) + block[4:], BF)] * 2
    else:
        specs = [pl.BlockSpec((1, width, width), lambda k, f: (k, 0, 0))]
        shapes = [jax.ShapeDtypeStruct((KERNEL_TAPS, width, width), F32)]
    return pl.pallas_call(
        functools.partial(conv_weight_kernel, fast, first),
        grid_spec=pltpu.PrefetchScalarGridSpec(
            num_scalar_prefetch=1,
            grid=(taps,),
            in_specs=[whole_block(a.shape) for a in (prev, x, nxt, g)] + [pl.BlockSpec(memory_space=pl.ANY)] * len(into),
            out_specs=specs,
            scratch_shapes=[
                pltpu.VMEM((count + 2 * prev.shape[0], width), BF),
                pltpu.VMEM((count, width), BF),
            ],
        ),
        out_shape=shapes,
        compiler_params=pltpu.CompilerParams(vmem_limit_bytes=VMEM_CONV),
        cost_estimate=conv_cost(count * taps // KERNEL_TAPS, width),
        input_output_aliases={5 + i: i for i in range(len(into))},
        name="conv_weight_backward",
    )(flags, prev, x, nxt, g, *into)


def conv_input_kernel(subs, flags, prev, g, nxt, gh, w, out, ext, col):
    step = pl.program_id(0)
    count, width = g.shape
    border = prev.shape[0]

    @pl.when(step == 0)
    def _():
        ext[0:border] = prev[...]
        ext[border : border + count] = g[...]
        ext[border + count :] = nxt[...]

    def load(start, size):
        return ext[pl.ds(pl.multiple_of(start + border, DILATION_STEP), size), :]

    fill_columns(col, load, flags, step, subs, width)
    total = gh[...]
    for k in range(KERNEL_TAPS):
        total = total + dot(col[:, k * width : (k + 1) * width], w[KERNEL_TAPS - 1 - k], NN)
    out[...] = total


def conv_input_backward(flags, prev, g, nxt, gh, weights, subs):
    count, width = g.shape
    rows = subs * SUB
    tile = pl.BlockSpec((rows, width), lambda j, f: (j, 0))
    return pl.pallas_call(
        functools.partial(conv_input_kernel, subs),
        grid_spec=pltpu.PrefetchScalarGridSpec(
            num_scalar_prefetch=1,
            grid=(count // rows,),
            in_specs=[whole_block(a.shape) for a in (prev, g, nxt)] + [tile, whole_block(weights.shape)],
            out_specs=tile,
            scratch_shapes=[
                pltpu.VMEM((count + 2 * prev.shape[0], width), BF),
                pltpu.VMEM((rows, KERNEL_TAPS * width), BF),
            ],
        ),
        out_shape=jax.ShapeDtypeStruct((count, width), F32),
        compiler_params=pltpu.CompilerParams(vmem_limit_bytes=VMEM_CONV),
        cost_estimate=conv_cost(count, width),
        name="conv_input_backward",
    )(flags, prev, g, nxt, gh, weights)


def pack_kernel(small, slots, count, lengths, first, final, conv, up, down, *rest):
    vectors, (flags, halo, conv_out, pair_out) = rest[: len(small)], rest[len(small) :]
    batch_index = lax.axis_index("z") * 4 + lax.axis_index("x") * 2 + lax.axis_index("core")
    seq_index = lax.axis_index("seq")
    taps, rows, wide = conv.shape
    subs = flags.shape[1]
    conv_out[0, 0:taps] = conv[...]
    line = None
    for v, (start, each) in zip(vectors, small):
        pick = (
            lax.broadcasted_iota(jnp.int32, (each, wide), 0) + start == lax.broadcasted_iota(jnp.int32, (each, wide), 1)
        ).astype(BF)
        part = dot(jnp.broadcast_to(v[...], (rows, each)), pick, NN)
        line = part if line is None else line + part
    conv_out[0, taps] = line.astype(BF)
    pair_out[0, 0] = up[...].T
    pair_out[0, 1] = down[...]
    halo[...] = jnp.where(seq_index == 0, final[...], first[...])
    ends = []
    total = 0
    for i in range(slots):
        total = total + lengths[0, i]
        ends.append(total)
    ids = []
    for j in range(-1, subs + 1):
        start = seq_index * count + j * SUB
        number = 0
        for end in ends:
            number = number + (start >= end).astype(jnp.int32)
        ids.append(jnp.where(start >= 0, number, -1))
    for j in range(subs):
        inside = (ids[j + 1] < slots).astype(jnp.int32)
        flags[0, j] = (ids[j] == ids[j + 1]).astype(jnp.int32) * inside
        flags[1, j] = (ids[j + 2] == ids[j + 1]).astype(jnp.int32) * inside
        flags[2, j] = inside
        flags[3, j] = batch_index % 2
        flags[4, j] = batch_index if j == 0 else seq_index
        bits = (lax.axis_index("x"), seq_index, lax.axis_index("z") % 2, lax.axis_index("z") // 2)
        flags[5, j] = bits[min(j, 3)]


def pack(lengths, x, conv, up, down, vectors, small):
    taps, rows, wide = conv.shape
    count, width = x.shape
    border = KERNEL_TAPS // 2 * DILATION_STEP
    smem = pl.BlockSpec(memory_space=pltpu.SMEM)
    arrays = [conv, up, down] + [v[None] for v in vectors]
    end_rows = pl.BlockSpec((border, width), lambda i: (0, 0))
    final_rows = pl.BlockSpec((border, width), lambda i: (count // border - 1, 0))
    sds = jax.ShapeDtypeStruct
    outs = [
        sds((6, count // SUB), jnp.int32),
        sds((border, width), BF),
        sds((1, taps + 1, rows, wide), BF),
        sds((1, 2) + down.shape, BF),
    ]
    return pl.pallas_call(
        functools.partial(pack_kernel, small, lengths.shape[1], count),
        grid=(1,),
        in_specs=[smem, end_rows, final_rows] + [whole_block(a.shape) for a in arrays],
        out_specs=[smem] + [whole_block(o.shape) for o in outs[1:]],
        out_shape=outs,
        compiler_params=pltpu.CompilerParams(vmem_limit_bytes=VMEM_PACK),
        name="pack",
    )(lengths, x, x, *arrays)


def swap(value, link):
    axis, bit = link
    return lax.ppermute(value, axis, [(i, i ^ bit) for i in range(lax.axis_size(axis))])


def half_of(link):
    return (lax.axis_index(link[0]) // link[1]) % 2


def give_half(value, link, dim):
    return lax.dynamic_index_in_dim(value, 1 - half_of(link), dim, keepdims=False).astype(BF)


def keep_half(value, link, dim):
    return lax.dynamic_index_in_dim(value, half_of(link), dim, keepdims=False).astype(F32)


def after(value, *others):
    return lax.optimization_barrier((value, *others))[0]


def shifted(offsets, b, s):
    return tuple((ob ^ b, os ^ s) for ob, os in offsets)


def both_cores(arrays, plan):
    other = [swap(a, CORE) for a in arrays]
    return arrays + other, tuple(plan) + tuple((shifted(o, 1, 0), first) for o, first in plan)


def gather(own, pair, halo):
    cut = own.shape[1] // 2
    top = lambda value: swap(value[:, :cut], Y)
    bottom = lambda value: swap(value[:, cut:], X)
    halo, own_y, own_x, far = lax.optimization_barrier((swap(halo, Y), swap(own, Y), swap(own, X), swap(own, Z1)))
    column = jnp.concatenate([own, far], 0)
    near, far_x, far_y, own_top, own_bottom = lax.optimization_barrier(
        (swap(column, Z0), swap(far, X), swap(far, Y), top(own_x), bottom(own_y))
    )
    pair = after(pair, near, own_top)
    near_y, near_x, far_top, far_bottom, pair_far = lax.optimization_barrier(
        (swap(near, Y), swap(near, X), top(far_x), bottom(far_y), swap(pair, Z1))
    )
    near_top, near_bottom = top(near_x), bottom(near_y)
    pair = jnp.concatenate([pair, pair_far], 0)
    pair = jnp.concatenate([pair, swap(pair, Z0)], 0)
    pair_x, pair_y = swap(pair, X), swap(pair, Y)
    across = lax.ppermute(pair, ("x", "seq"), [(i, i ^ 3) for i in range(4)])
    offsets = ((0, 0), (8, 0), (4, 0), (12, 0))
    pair_plan = [(shifted(offsets, b, s), 0) for b, s in ((0, 0), (2, 0), (0, 1), (2, 1))]
    arrays, plan = [column, near], [(((0, 0), (8, 0)), 0), (((4, 0), (12, 0)), 0)]
    for offsets, members in (
        (((0, 0),), (own_x, own_y, own_top, own_bottom)),
        (((8, 0),), (far_x, far_y, far_top, far_bottom)),
        (((4, 0), (12, 0)), (near_x, near_y, near_top, near_bottom)),
    ):
        arrays += members
        plan += [(shifted(offsets, b, s), first) for b, s, first in ((2, 0, 0), (0, 1, 0), (2, 1, 0), (2, 1, cut))]
    return halo, both_cores(arrays, plan), ([pair, pair_x, pair_y, across], pair_plan)


def stage_kernel(columns, joined, flags, *refs):
    count = len(columns)
    outs = refs[2 * count :]
    at = 0
    for i, column in enumerate(columns):
        keep, got = refs[2 * i], refs[2 * i + 1]
        if joined is None:
            give_out, keep_out, where = outs[2 * i], outs[2 * i + 1], Ellipsis
        else:
            taps = keep.shape[1 + joined]
            give_out, keep_out = outs
            where = (*(slice(None),) * joined, slice(at, at + taps))
            at += taps
        bit = flags[5, column]
        give_out[where] = (keep[1 - bit].astype(F32) + got[1 - bit].astype(F32)).astype(BF)
        keep_out[where] = keep[bit].astype(F32) + got[bit].astype(F32)


def first_stage_kernel(cut, flags, keep, got, *outs):
    for i, taps in enumerate((slice(0, cut), slice(cut, keep.shape[3]))):
        bit = flags[5, i]
        give_out, keep_out = outs[2 * i], outs[2 * i + 1]
        for n in range(2):
            other, own = 2 * (1 - bit) + n, 2 * bit + n
            give_out[n] = (keep[other, :, :, taps].astype(F32) + got[other, :, :, taps].astype(F32)).astype(BF)
            keep_out[n] = keep[own, :, :, taps].astype(F32) + got[own, :, :, taps].astype(F32)


def first_stage(flags, keep, got, cut):
    tail = keep.shape[4:]
    outs = [jax.ShapeDtypeStruct((2, 2, 2, n) + tail, kind) for n in (cut, keep.shape[3] - cut) for kind in (BF, F32)]
    return pl.pallas_call(
        functools.partial(first_stage_kernel, cut),
        grid_spec=pltpu.PrefetchScalarGridSpec(
            num_scalar_prefetch=1,
            grid=(1,),
            in_specs=[whole_block(keep.shape)] * 2,
            out_specs=[whole_block(o.shape) for o in outs],
        ),
        out_shape=outs,
        compiler_params=pltpu.CompilerParams(vmem_limit_bytes=VMEM_SUM),
        name="stage",
    )(flags, keep, got)


def stage(flags, parts, columns, joined=None):
    shapes = [keep.shape[1:] for keep, _ in parts]
    if joined is not None:
        first = list(shapes[0])
        first[joined] = sum(shape[joined] for shape in shapes)
        shapes = [tuple(first)]
    outs = [jax.ShapeDtypeStruct(shape, kind) for shape in shapes for kind in (BF, F32)]
    arrays = [a for part in parts for a in part]
    return pl.pallas_call(
        functools.partial(stage_kernel, columns, joined),
        grid_spec=pltpu.PrefetchScalarGridSpec(
            num_scalar_prefetch=1,
            grid=(1,),
            in_specs=[whole_block(a.shape) for a in arrays],
            out_specs=[whole_block(o.shape) for o in outs],
        ),
        out_shape=outs,
        compiler_params=pltpu.CompilerParams(vmem_limit_bytes=VMEM_SUM),
        name="stage",
    )(flags, *arrays)


def local(inputs, window_lengths, conv_weight, conv_bias, norm1_gain, norm1_bias, up_weight, up_bias, down_weight,
          down_bias, norm2_gain, norm2_bias, out_grad):
    _, count, width = inputs.shape
    batch, seq = lax.axis_size(BATCH), lax.axis_size("seq")
    hidden = up_weight.shape[1] * batch
    border = KERNEL_TAPS // 2 * DILATION_STEP
    x, og = inputs[0], pltpu.with_memory_space_constraint(out_grad[0], pltpu.HBM)
    fast = seq == 2 and batch == 16

    def ends(value):
        first, final = value[:border], value[count - border :]
        if fast:
            other = swap(jnp.where(lax.axis_index("seq") == 0, final, first), Y)
            return other, other
        up = [(i, i + 1) for i in range(seq - 1)]
        return lax.ppermute(final, "seq", up), lax.ppermute(first, "seq", [(j, i) for i, j in up])

    vectors = [conv_bias, norm1_gain, norm1_bias, down_bias, norm2_gain, norm2_bias, up_bias]
    sizes = [v.shape[0] for v in vectors]
    small = tuple((sum(sizes[:i]), n) for i, n in enumerate(sizes))
    conv_own = conv_weight.transpose(0, 2, 1)
    flags, halo, conv_block, pair_block = pack(window_lengths, x, conv_own, up_weight, down_weight, vectors, small)
    if fast:
        halo, (conv_pieces, conv_plan), (pair_pieces, pair_plan) = gather(conv_block, pair_block, halo)
        prev = nxt = halo
        table = None
    else:
        def every(value):
            value = lax.all_gather(value, "seq", axis=2, tiled=True)
            return lax.all_gather(value, BATCH, axis=1, tiled=True)

        prev, nxt = ends(x)
        conv_pieces, conv_plan = [every(conv_own)], ((None, 0),)
        pair_pieces, pair_plan = [every(pair_block[0])], ((None, 0),)
        full = [lax.all_gather(v, (*BATCH, "seq"), axis=0, tiled=True).astype(F32) for v in vectors]
        table = jnp.stack([jnp.pad(v, (0, hidden - v.shape[0])) for v in full + [full[0]]])
        small = ()
    conv_pieces, conv_plan = list(conv_pieces), tuple((None if o is None else tuple(o), f) for o, f in conv_plan)
    xhat, scale, conv_full, table = conv_forward(flags, prev, x, nxt, conv_pieces, conv_plan, small, table, 2, hidden)
    if fast:
        (column, over_x, over_y, across), table = lax.optimization_barrier((pair_pieces, table))
        others = [swap(a, CORE) for a in (column, over_x, over_y)]
        others, across = lax.optimization_barrier((others, across))
        pair_pieces = [column, over_x, over_y, across] + others + [swap(across, CORE)]
        pair_plan = tuple(pair_plan) + tuple((shifted(o, 1, 0), first) for o, first in pair_plan)
    pair_plan = tuple((None if o is None else tuple(o), f) for o, f in pair_plan)
    block_output, grad_hidden, grad_conv, *ffn_grads = ffn(
        flags, x, xhat, scale, og, table, pair_pieces, pair_plan, 2 * SUB, min(1024, hidden), batch, fast
    )
    grads = (flags, prev, x, nxt, grad_conv, grad_hidden, conv_full)
    if fast:
        input_grad, weight_grads = paired(grads, ffn_grads, batch, width, hidden)
    else:
        grad_prev, grad_next = ends(grad_conv)
        conv_grads = conv_weight_backward(flags, prev, x, nxt, grad_conv, batch, fast)
        input_grad = conv_input_backward(flags, grad_prev, grad_conv, grad_next, grad_hidden, conv_full, 2)
        weight_grads = whole_sums(conv_grads, ffn_grads, batch, seq, width, hidden)
    conv_grad, cb, g1, s1, up_grad, ub_grad, down_grad, db, g2, s2 = weight_grads
    return (block_output[None], input_grad[None], conv_grad, cb, g1, s1, up_grad, ub_grad, down_grad, db, g2, s2)


def paired(grads, ffn_grads, batch, width, hidden):
    flags, prev, x, nxt, grad_conv, grad_hidden, conv_full = grads
    up_rows = width // 2 + 16
    edge, ffn_send, ffn_keep = ffn_grads
    ffn_got, grad_prev = swap(ffn_send, CORE), swap(edge, Y)
    early = 2
    parts = conv_weight_backward(flags, prev, x, prev, grad_conv, batch, True, 0, early)
    ffn_got, grad_prev, parts = lax.optimization_barrier((ffn_got, grad_prev, parts))
    up_give, up_keep, down_give, down_keep = first_stage(flags, ffn_keep, ffn_got, up_rows)
    up_got, down_got = swap(up_give, X), swap(down_give, Y)
    first = after(prev, up_give)
    send, keep = conv_weight_backward(
        flags, first, x, first, grad_conv, batch, True, early, KERNEL_TAPS - early, parts
    )
    up_got, down_got, send = lax.optimization_barrier((up_got, down_got, send))
    got = swap(send, CORE)
    parts = [(up_keep, up_got), (down_keep, down_got)]
    up_give, up_keep, down_give, down_keep = stage(flags, parts, (1, 0))
    up_got, down_got = swap(up_give, Y), swap(down_give, X)
    upper_give, upper_keep, lower_give, lower_keep = first_stage(
        flags, keep, after(got, up_give), (KERNEL_TAPS + 1) // 2
    )
    upper_got, lower_got = swap(upper_give, X), swap(lower_give, Y)
    second = after(grad_prev, upper_give)
    input_grad = conv_input_backward(flags, second, grad_conv, second, grad_hidden, conv_full, 2)
    up_got, down_got, input_grad = lax.optimization_barrier((up_got, down_got, input_grad))
    ffn_give, ffn_keep = stage(flags, [(up_keep, up_got), (down_keep, down_got)], (2, 2), 1)
    ffn_got = swap(ffn_give, Z0)
    upper_got, lower_got, _ = lax.optimization_barrier((upper_got, lower_got, ffn_give))
    parts = [(upper_keep, upper_got), (lower_keep, lower_got)]
    upper_give, upper_keep, lower_give, lower_keep = stage(flags, parts, (1, 0))
    upper_got, lower_got = swap(upper_give, Y), swap(lower_give, X)
    ffn_give, ffn_keep = stage(flags, [(ffn_keep, after(ffn_got, upper_give))], (3,))
    ffn_got = swap(ffn_give, Z1)
    upper_got, lower_got, _ = lax.optimization_barrier((upper_got, lower_got, ffn_give))
    conv_give, conv_keep = stage(flags, [(upper_keep, upper_got), (lower_keep, lower_got)], (2, 2), 1)
    conv_got = swap(conv_give, Z0)
    pair_part = ffn_keep + after(ffn_got, conv_give).astype(F32)
    conv_give, conv_keep = stage(flags, [(conv_keep, conv_got)], (3,))
    conv_got = swap(conv_give, Z1)
    conv_grad = (conv_keep + conv_got.astype(F32)).transpose(0, 2, 1)
    head = width // 2
    up_grad = pair_part[:head]
    down_grad = pair_part[up_rows:].T
    each = width // (batch * 2)
    g2, s2, db, g1, s1, cb = (pair_part[head, i * each : (i + 1) * each] for i in range(6))
    ub_grad = pair_part[head + 1, : hidden // (batch * 2)]
    return input_grad, (conv_grad, cb, g1, s1, up_grad, ub_grad, down_grad, db, g2, s2)


def whole_sums(conv_grads, ffn_grads, batch, seq, width, hidden):
    def total(value, dims):
        value = lax.psum_scatter(value, BATCH, scatter_dimension=dims[1], tiled=True)
        return lax.psum_scatter(value, "seq", scatter_dimension=dims[0], tiled=True)

    conv_grad = total(conv_grads[0], (2, 1)).transpose(0, 2, 1)
    up_grad = total(ffn_grads[0], (0, 1))
    down_grad = total(ffn_grads[1], (0, 1)).T
    vec_grads = total(ffn_grads[2].reshape(6, batch, seq, -1), (2, 1)).reshape(6, -1)
    ub_grad = total(ffn_grads[3].reshape(batch, seq, -1), (1, 0)).reshape(-1)
    g2, s2, db, g1, s1, cb = (vec_grads[i] for i in range(6))
    return conv_grad, cb, g1, s1, up_grad, ub_grad, down_grad, db, g2, s2


def solution(mesh):
    batch, seq = mesh.shape["batch"], mesh.shape["seq"]
    split = Mesh(mesh.devices.reshape(batch // 4, 2, 2, seq), (*BATCH, "seq"))
    both = P((*BATCH, "seq"))
    rows = P(BATCH, "seq", None)
    conv, up, down = P(None, "seq", BATCH), P("seq", BATCH), P(BATCH, "seq")
    in_specs = (rows, P(BATCH, None), conv, both, both, both, up, both, down, both, both, both, rows)
    out_specs = (rows, rows, conv, both, both, both, up, both, down, both, both, both)
    return jax.shard_map(local, mesh=split, in_specs=in_specs, out_specs=out_specs, check_vma=False)
```

```python
import functools
import jax
import jax.numpy as jnp
from jax import lax
from jax.experimental import pallas as pl
from jax.experimental.pallas import tpu as pltpu
from jax.sharding import Mesh, PartitionSpec as P

KERNEL_TAPS = 9
DILATION_STEP = 32
EPSILON = 1e-05
SUB = 256
BF = jnp.bfloat16
F32 = jnp.float32
VMEM_CONV = 28 * 2**20
VMEM_FFN = 51 * 2**20
VMEM_FIRST = 30 * 2**20
VMEM_PACK = 60 * 2**20
VMEM_SUM = 24 * 2**20
COST = 1
BATCH = ("z", "x", "core")
X, Y, Z0, Z1, CORE = ("x", 1), ("seq", 1), ("z", 1), ("z", 2), ("core", 1)
NN = (((1,), (0,)), ((), ()))
NT = (((1,), (1,)), ((), ()))
TN = (((0,), (0,)), ((), ()))


def dot(a, b, dims):
    return lax.dot_general(a, b, dims, preferred_element_type=F32)


def conv_cost(count, width):
    return pl.CostEstimate(flops=2 * count * KERNEL_TAPS * width * width // COST, bytes_accessed=2**20, transcendentals=0)


def gelu_pair(v):
    size = jnp.abs(v)
    t = pl.reciprocal(1.0 + 0.23164189 * size, approx=True)
    poly = t * (0.127414796 + t * (-0.142248368 + t * (0.710706871 + t * (-0.726576013 + t * 0.530702714))))
    bell = jnp.exp2(-0.72134752 * (size * size))
    value = jnp.maximum(v, 0.0) - size * (poly * bell)
    low_side = bell * (poly - 0.39894228 * size)
    return value, jnp.where(v >= 0.0, 1.0 - low_side, low_side)


def row_mean(v):
    return jnp.sum(v, -1, keepdims=True) * (1.0 / v.shape[-1])


def fold(v):
    total = v[0:8]
    for r in range(8, v.shape[0], 8):
        total = total + v[r : r + 8]
    return total


def fill_columns(col, load, flags, block, subs, width):
    for r in range(subs):
        j = block * subs + r
        base = j * SUB
        own = flags[2, j].astype(F32).astype(BF)
        before = flags[0, j].astype(F32).astype(BF)
        after = flags[1, j].astype(F32).astype(BF)
        for k in range(KERNEL_TAPS):
            o = (k - KERNEL_TAPS // 2) * DILATION_STEP
            columns = slice(k * width, (k + 1) * width)
            first = r * SUB
            if o < 0:
                col[first : first - o, columns] = load(base + o, -o) * before
                col[first - o : first + SUB, columns] = load(base, SUB + o) * own
            elif o == 0:
                col[first : first + SUB, columns] = load(base, SUB) * own
            else:
                col[first : first + SUB - o, columns] = load(base + o, SUB - o) * own
                col[first + SUB - o : first + SUB, columns] = load(base + SUB, o) * after


def place(plan, batch_index, seq_index, sources, whole, sems):
    copies = []
    taps = whole.shape[0]
    for source, (offsets, first) in zip(sources, plan):
        if offsets is None:
            copies.append(pltpu.make_async_copy(source, whole, sems.at[len(copies)]))
            continue
        _, span, rows, wide = source.shape
        span = min(span, taps - max(first, 0))
        for n, (db, ds) in enumerate(offsets):
            b, s = (db, ds) if first < 0 else (batch_index ^ db, seq_index ^ ds)
            at_rows = pl.ds(pl.multiple_of(b * rows, rows), rows)
            at_columns = pl.ds(pl.multiple_of(s * wide, wide), wide)
            target = whole.at[pl.ds(max(first, 0), span), at_rows, at_columns]
            copies.append(pltpu.make_async_copy(source.at[n, pl.ds(0, span)], target, sems.at[len(copies)]))
    return copies


def count_copies(plan):
    return sum(1 if offsets is None else len(offsets) for offsets, _ in plan)


def spread_table(small, rows, out):
    devices, wide = rows.shape
    for v, (start, each) in enumerate(small):
        length = devices * each
        place_of = lax.broadcasted_iota(jnp.int32, (wide, length), 1) % each + start
        pick = (place_of == lax.broadcasted_iota(jnp.int32, (wide, length), 0)).astype(BF)
        values = dot(rows, pick, NN)
        owner = lax.broadcasted_iota(jnp.int32, (devices, length), 1) // each
        row = lax.broadcasted_iota(jnp.int32, (devices, length), 0)
        own = owner == 2 * (row % (devices // 2)) + row // (devices // 2)
        out[v : v + 1, :length] = jnp.sum(jnp.where(own, values, 0.0), 0, keepdims=True)


def conv_kernel(subs, plan, small, flags, prev, x, nxt, *rest):
    block = pl.program_id(0)
    width = x.shape[1]
    border = prev.shape[0]
    sources = rest[: len(plan)]
    if small:
        xhat_out, scale_out, w_out, table, ext, col, w, sems, out_sem = rest[len(plan) :]
        small_rows = sources[0].shape[2]
    else:
        table, xhat_out, scale_out, w_out, ext, col, w, sems, out_sem = rest[len(plan) :]

    def copies_in():
        return place(plan, flags[4, 0], flags[4, 1], sources, w, sems)

    def whole_out():
        return pltpu.make_async_copy(w.at[pl.ds(0, KERNEL_TAPS)], w_out, out_sem)

    @pl.when(block == 0)
    def _():
        for copy in copies_in():
            copy.start()
        ext[0:border] = prev[...]
        ext[border : border + x.shape[0]] = x[...]
        ext[border + x.shape[0] :] = nxt[...]

        for copy in copies_in():
            copy.wait()
        whole_out().start()
        if small:
            blocks = width // small_rows
            first_row = lax.broadcasted_iota(jnp.int32, (blocks, width), 0) * small_rows
            pick = (first_row == lax.broadcasted_iota(jnp.int32, (blocks, width), 1)).astype(BF)
            rows = dot(pick, w[KERNEL_TAPS], NN).astype(BF)
            spread_table(small, jnp.concatenate([rows[:, : width // 2], rows[:, width // 2 :]], 0), table)

    @pl.when(block == pl.num_programs(0) - 1)
    def _():
        whole_out().wait()

    def load(start, count):
        return ext[pl.ds(pl.multiple_of(start + border, DILATION_STEP), count), :]

    fill_columns(col, load, flags, block, subs, width)
    total = None
    for k in range(KERNEL_TAPS):
        part = dot(col[:, k * width : (k + 1) * width], w[k], NT)
        total = part if total is None else total + part
    value, slope = gelu_pair(total + table[0:1, :width])
    centered = value - row_mean(value)
    rstd = lax.rsqrt(row_mean(centered * centered) + EPSILON)
    xhat_out[...] = centered * rstd
    scale_out[...] = slope * rstd


def whole_block(shape):
    return pl.BlockSpec(shape, lambda *_: (0,) * len(shape), pipeline_mode=pl.Buffered(1))


def conv_forward(flags, prev, x, nxt, sources, plan, small, table, subs, hidden):
    count, width = x.shape
    rows = subs * SUB
    anywhere = [pl.BlockSpec(memory_space=pl.ANY)] * len(sources)
    out_specs = [pl.BlockSpec((rows, width), lambda j, f: (j, 0))] * 2 + [pl.BlockSpec(memory_space=pltpu.HBM)]
    out_shape = [pltpu.HBM((count, width), F32)] * 2 + [pltpu.HBM((KERNEL_TAPS, width, width), BF)]
    scratch = [
        pltpu.VMEM((count + 2 * prev.shape[0], width), BF),
        pltpu.VMEM((rows, KERNEL_TAPS * width), BF),
        pltpu.VMEM((KERNEL_TAPS + bool(small), width, width), BF),
        pltpu.SemaphoreType.DMA((count_copies(plan),)),
        pltpu.SemaphoreType.DMA,
    ]
    extra_specs, extra = [], []
    if small:
        out_specs = out_specs + [whole_block((8, hidden))]
        out_shape = out_shape + [jax.ShapeDtypeStruct((8, hidden), F32)]
    else:
        extra_specs, extra = [whole_block(table.shape)], [table]
    outs = pl.pallas_call(
        functools.partial(conv_kernel, subs, plan, small),
        grid_spec=pltpu.PrefetchScalarGridSpec(
            num_scalar_prefetch=1,
            grid=(count // rows,),
            in_specs=[whole_block(prev.shape), whole_block(x.shape), whole_block(nxt.shape)] + anywhere + extra_specs,
            out_specs=out_specs,
            scratch_shapes=scratch,
        ),
        out_shape=out_shape,
        compiler_params=pltpu.CompilerParams(vmem_limit_bytes=VMEM_FIRST),
        cost_estimate=pl.CostEstimate(flops=1, bytes_accessed=1, transcendentals=0),
        name="conv_forward",
    )(flags, prev, x, nxt, *sources, *extra)
    return outs if small else (*outs, table)


def ffn_kernel(chunk, fast, plan, flags, x, xhat, scale, og, table, *rest):
    sources, rest = rest[: len(plan)], rest[len(plan) :]
    out, gh_out, gc_out, *rest = rest
    act, slope, dup, ddown, sums, ub_sums, pair, sems = rest[-8:]
    step = pl.program_id(0)
    last = pl.num_programs(0) - 1
    _, hidden, width = pair.shape
    chunks = hidden // chunk
    gain1, shift1, db, gain2, shift2 = (table[i : i + 1, :width] for i in range(1, 6))
    ub = table[6:7, :]

    @pl.when(step == 0)
    def _():
        copies = place(plan, flags[4, 0], flags[4, 1], sources, pair, sems)
        for copy in copies:
            copy.start()
        dup[...] = jnp.zeros_like(dup)
        ddown[...] = jnp.zeros_like(ddown)
        sums[...] = jnp.zeros_like(sums)
        ub_sums[...] = jnp.zeros_like(ub_sums)
        for copy in copies:
            copy.wait()

    one = x[...].astype(F32) + (xhat[...] * gain1 + shift1)
    low = one.astype(BF)
    total = None
    for f in range(chunks):
        cols = slice(f * chunk, (f + 1) * chunk)
        value, s = gelu_pair(dot(low, pair[0, cols, :], NT) + ub[:, cols])
        a = value.astype(BF)
        act[:, cols] = a
        slope[:, cols] = s
        part = dot(a, pair[1, cols, :], NN)
        total = part if total is None else total + part
    d = total + db
    centered = d - row_mean(d)
    rstd = lax.rsqrt(row_mean(centered * centered) + EPSILON)
    hat = centered * rstd
    out[...] = (one + (hat * gain2 + shift2)).astype(BF)
    g = og[...].astype(F32)
    e = g * gain2
    gd = (rstd * (e - row_mean(e) - hat * row_mean(e * hat))).astype(BF)
    sums[0] += fold(g * hat)
    sums[1] += fold(g)
    sums[2] += fold(gd.astype(F32))
    gh = g
    for f in range(chunks):
        cols = slice(f * chunk, (f + 1) * chunk)
        ddown[:, cols] += dot(gd, act[:, cols], TN)
        gu = dot(gd, pair[1, cols, :], NT) * slope[:, cols]
        gul = gu.astype(BF)
        ub_sums[:, cols] += fold(gul.astype(F32))
        dup[:, cols] += dot(low, gul, TN)
        gh = gh + dot(gul, pair[0, cols, :], NN)
    gh_out[...] = gh
    sums[3] += fold(gh * xhat[...])
    sums[4] += fold(gh)
    e = gh * gain1
    gc = (scale[...] * (e - row_mean(e) - xhat[...] * row_mean(e * xhat[...]))).astype(BF)
    gc_out[...] = gc
    if fast:
        edge = rest[0]
        border = edge.shape[0]

        @pl.when((step == 0) & (flags[4, 1] == 1))
        def _():
            edge[...] = gc[:border]

        @pl.when((step == last) & (flags[4, 1] == 0))
        def _():
            edge[...] = gc[gc.shape[0] - border :]

    sums[5] += fold(gc.astype(F32))

    @pl.when(step == last)
    def _():
        if not fast:
            up_out, down_out, sums_out, ub_out = rest[:4]
            up_out[...] = dup[...]
            down_out[...] = ddown[...]
            sums_out[...] = jnp.sum(sums[...], 1)
            ub_out[...] = jnp.sum(ub_sums[...], 0, keepdims=True)
            return
        send, keep = rest[1:3]
        mine = flags[3, 0] == 0
        block = send.shape[-1]
        half = width // 2
        devices = 2 * (hidden // block)

        def own(length):
            each = length // devices
            place = lax.broadcasted_iota(jnp.int32, (devices, length), 1) // each
            return place == lax.broadcasted_iota(jnp.int32, (devices, length), 0)

        def pick(length, start):
            each = length // devices
            place = lax.broadcasted_iota(jnp.int32, (length, 128), 0) % each + start
            return (place == lax.broadcasted_iota(jnp.int32, (length, 128), 1)).astype(BF)

        first = None
        for v in range(6):
            line = jnp.sum(sums[v], 0, keepdims=True)
            part = dot(jnp.where(own(width), line, 0.0).astype(BF), pick(width, v * (width // devices)), NN)
            first = part if first is None else first + part
        line = jnp.sum(ub_sums[...], 0, keepdims=True)
        second = dot(jnp.where(own(hidden), line, 0.0).astype(BF), pick(hidden, 0), NN)
        index = lax.broadcasted_iota(jnp.int32, (16, 128), 0)

        def tail(b, s):
            at = 2 * b + s
            return jnp.where(index == 0, first[at : at + 1], jnp.where(index == 1, second[at : at + 1], 0.0)).astype(BF)

        for b in range(0, hidden // block, 2):
            for s in range(2):
                take = slice(s * half, (s + 1) * half)
                x_bit, z = b // 2 % 2, (b // 4 % 2, b // 8)
                up_at, down_at = (2 * x_bit + s, *z), (2 * s + x_bit, *z)
                for acc, at, start in ((dup, up_at, 0), (ddown, down_at, half + 16)):
                    lo = acc[take, b * block : (b + 1) * block].astype(BF)
                    hi = acc[take, (b + 1) * block : (b + 2) * block].astype(BF)
                    send[(*at, slice(start, start + half))] = jnp.where(mine, hi, lo)
                    keep[(*at, slice(start, start + half))] = jnp.where(mine, lo, hi)
                lo, hi = tail(b, s), tail(b + 1, s)
                send[(*up_at, slice(half, half + 16))] = jnp.where(mine, hi, lo)
                keep[(*up_at, slice(half, half + 16))] = jnp.where(mine, lo, hi)


def ffn(flags, x, xhat, scale, og, table, sources, plan, rows, chunk, batch, fast):
    count, width = x.shape
    hidden = table.shape[1]
    tile = pl.BlockSpec((rows, width), lambda j, f: (j, 0))
    sds = jax.ShapeDtypeStruct
    if fast:
        border = KERNEL_TAPS // 2 * DILATION_STEP
        shapes = [sds((border, width), BF)] + [sds((4, 2, 2, width + 16, hidden // batch), BF)] * 2
    else:
        shapes = [sds(s, F32) for s in ((width, hidden), (width, hidden), (6, width), (1, hidden))]
    anywhere = [pl.BlockSpec(memory_space=pl.ANY)] * len(sources)
    return pl.pallas_call(
        functools.partial(ffn_kernel, chunk, fast, plan),
        grid_spec=pltpu.PrefetchScalarGridSpec(
            num_scalar_prefetch=1,
            grid=(count // rows,),
            in_specs=[tile, tile, tile, tile, whole_block(table.shape)] + anywhere,
            out_specs=[tile, tile, tile] + [whole_block(s.shape) for s in shapes],
            scratch_shapes=[
                pltpu.VMEM((rows, hidden), BF),
                pltpu.VMEM((rows, hidden), F32),
                pltpu.VMEM((width, hidden), F32),
                pltpu.VMEM((width, hidden), F32),
                pltpu.VMEM((6, 8, width), F32),
                pltpu.VMEM((8, hidden), F32),
                pltpu.VMEM((2, hidden, width), BF),
                pltpu.SemaphoreType.DMA((count_copies(plan),)),
            ],
        ),
        out_shape=[pltpu.HBM((count, width), BF), pltpu.HBM((count, width), F32), (pltpu.VMEM if fast else pltpu.HBM)((count, width), BF)] + shapes,
        compiler_params=pltpu.CompilerParams(vmem_limit_bytes=VMEM_FFN if fast else VMEM_PACK),
        cost_estimate=pl.CostEstimate(flops=12 * count * width * hidden // COST, bytes_accessed=2**20, transcendentals=0),
        name="feed_forward",
    )(flags, x, xhat, scale, og, table, *sources)


def conv_weight_kernel(fast, first, flags, prev, x, nxt, g, *rest):
    ext, col = rest[-2:]
    outs = rest[:-2] if first == 0 else rest[2:-2]
    tap = pl.program_id(0) + first
    count, width = g.shape
    border = prev.shape[0]
    subs = count // SUB

    @pl.when(tap == first)
    def _():
        ext[0:border] = prev[...]
        ext[border : border + count] = x[...]
        ext[border + count :] = nxt[...]

    o = (tap - KERNEL_TAPS // 2) * DILATION_STEP
    offset = lax.broadcasted_iota(jnp.int32, (SUB, 1), 0) + o
    for r in range(subs):
        own = flags[2, r].astype(F32)
        before = flags[0, r].astype(F32)
        after = flags[1, r].astype(F32)
        mask = jnp.where(offset < 0, before, jnp.where(offset >= SUB, after, own)).astype(BF)
        rows = ext[pl.ds(pl.multiple_of(r * SUB + o + border, DILATION_STEP), SUB), :]
        col[r * SUB : (r + 1) * SUB, :] = rows * mask

    grad = dot(g[...], col[...], TN)
    if not fast:
        outs[0][0] = grad
        return
    mine = flags[3, 0] == 0
    half = width // 2

    send, keep = outs
    block = send.shape[4]
    early = (tap < (KERNEL_TAPS + 1) // 2).astype(jnp.int32)
    for s in range(2):
        columns = slice(s * half, (s + 1) * half)
        for b in range(0, width // block, 2):
            bit = b // 2 % 2
            at = (early * (2 * bit + s) + (1 - early) * (2 * s + bit), b // 4 % 2, b // 8, 0)
            lo = grad[b * block : (b + 1) * block, columns].astype(BF)
            hi = grad[(b + 1) * block : (b + 2) * block, columns].astype(BF)
            send[at] = jnp.where(mine, hi, lo)
            keep[at] = jnp.where(mine, lo, hi)


def conv_weight_backward(flags, prev, x, nxt, g, batch, fast, first=0, taps=KERNEL_TAPS, into=()):
    count, width = x.shape
    if fast:
        block = (4, 2, 2, 1, width // batch, width // 2)
        specs = [pl.BlockSpec(block, lambda k, f: (0, 0, 0, k + first, 0, 0))] * 2
        shapes = [jax.ShapeDtypeStruct(block[:3] + (KERNEL_TAPS,) + block[4:], BF)] * 2
    else:
        specs = [pl.BlockSpec((1, width, width), lambda k, f: (k, 0, 0))]
        shapes = [jax.ShapeDtypeStruct((KERNEL_TAPS, width, width), F32)]
    return pl.pallas_call(
        functools.partial(conv_weight_kernel, fast, first),
        grid_spec=pltpu.PrefetchScalarGridSpec(
            num_scalar_prefetch=1,
            grid=(taps,),
            in_specs=[whole_block(a.shape) for a in (prev, x, nxt, g)] + [pl.BlockSpec(memory_space=pl.ANY)] * len(into),
            out_specs=specs,
            scratch_shapes=[
                pltpu.VMEM((count + 2 * prev.shape[0], width), BF),
                pltpu.VMEM((count, width), BF),
            ],
        ),
        out_shape=shapes,
        compiler_params=pltpu.CompilerParams(vmem_limit_bytes=VMEM_CONV),
        cost_estimate=conv_cost(count * taps // KERNEL_TAPS, width),
        input_output_aliases={5 + i: i for i in range(len(into))},
        name="conv_weight_backward",
    )(flags, prev, x, nxt, g, *into)


def conv_input_kernel(subs, flags, prev, g, nxt, gh, w, out, ext, col):
    step = pl.program_id(0)
    count, width = g.shape
    border = prev.shape[0]

    @pl.when(step == 0)
    def _():
        ext[0:border] = prev[...]
        ext[border : border + count] = g[...]
        ext[border + count :] = nxt[...]

    def load(start, size):
        return ext[pl.ds(pl.multiple_of(start + border, DILATION_STEP), size), :]

    fill_columns(col, load, flags, step, subs, width)
    total = gh[...]
    for k in range(KERNEL_TAPS):
        total = total + dot(col[:, k * width : (k + 1) * width], w[KERNEL_TAPS - 1 - k], NN)
    out[...] = total


def conv_input_backward(flags, prev, g, nxt, gh, weights, subs):
    count, width = g.shape
    rows = subs * SUB
    tile = pl.BlockSpec((rows, width), lambda j, f: (j, 0))
    return pl.pallas_call(
        functools.partial(conv_input_kernel, subs),
        grid_spec=pltpu.PrefetchScalarGridSpec(
            num_scalar_prefetch=1,
            grid=(count // rows,),
            in_specs=[whole_block(a.shape) for a in (prev, g, nxt)] + [tile, whole_block(weights.shape)],
            out_specs=tile,
            scratch_shapes=[
                pltpu.VMEM((count + 2 * prev.shape[0], width), BF),
                pltpu.VMEM((rows, KERNEL_TAPS * width), BF),
            ],
        ),
        out_shape=jax.ShapeDtypeStruct((count, width), F32),
        compiler_params=pltpu.CompilerParams(vmem_limit_bytes=VMEM_CONV),
        cost_estimate=conv_cost(count, width),
        name="conv_input_backward",
    )(flags, prev, g, nxt, gh, weights)


def pack_kernel(small, slots, count, lengths, first, final, conv, up, down, *rest):
    vectors, (flags, halo, conv_out, pair_out) = rest[: len(small)], rest[len(small) :]
    batch_index = lax.axis_index("z") * 4 + lax.axis_index("x") * 2 + lax.axis_index("core")
    seq_index = lax.axis_index("seq")
    taps, rows, wide = conv.shape
    subs = flags.shape[1]
    conv_out[0, 0:taps] = conv[...]
    line = None
    for v, (start, each) in zip(vectors, small):
        pick = (
            lax.broadcasted_iota(jnp.int32, (each, wide), 0) + start == lax.broadcasted_iota(jnp.int32, (each, wide), 1)
        ).astype(BF)
        part = dot(jnp.broadcast_to(v[...], (rows, each)), pick, NN)
        line = part if line is None else line + part
    conv_out[0, taps] = line.astype(BF)
    pair_out[0, 0] = up[...].T
    pair_out[0, 1] = down[...]
    halo[...] = jnp.where(seq_index == 0, final[...], first[...])
    ends = []
    total = 0
    for i in range(slots):
        total = total + lengths[0, i]
        ends.append(total)
    ids = []
    for j in range(-1, subs + 1):
        start = seq_index * count + j * SUB
        number = 0
        for end in ends:
            number = number + (start >= end).astype(jnp.int32)
        ids.append(jnp.where(start >= 0, number, -1))
    for j in range(subs):
        inside = (ids[j + 1] < slots).astype(jnp.int32)
        flags[0, j] = (ids[j] == ids[j + 1]).astype(jnp.int32) * inside
        flags[1, j] = (ids[j + 2] == ids[j + 1]).astype(jnp.int32) * inside
        flags[2, j] = inside
        flags[3, j] = batch_index % 2
        flags[4, j] = batch_index if j == 0 else seq_index
        bits = (lax.axis_index("x"), seq_index, lax.axis_index("z") % 2, lax.axis_index("z") // 2)
        flags[5, j] = bits[min(j, 3)]


def pack(lengths, x, conv, up, down, vectors, small):
    taps, rows, wide = conv.shape
    count, width = x.shape
    border = KERNEL_TAPS // 2 * DILATION_STEP
    smem = pl.BlockSpec(memory_space=pltpu.SMEM)
    arrays = [conv, up, down] + [v[None] for v in vectors]
    end_rows = pl.BlockSpec((border, width), lambda i: (0, 0))
    final_rows = pl.BlockSpec((border, width), lambda i: (count // border - 1, 0))
    sds = jax.ShapeDtypeStruct
    outs = [
        sds((6, count // SUB), jnp.int32),
        sds((border, width), BF),
        sds((1, taps + 1, rows, wide), BF),
        sds((1, 2) + down.shape, BF),
    ]
    return pl.pallas_call(
        functools.partial(pack_kernel, small, lengths.shape[1], count),
        grid=(1,),
        in_specs=[smem, end_rows, final_rows] + [whole_block(a.shape) for a in arrays],
        out_specs=[smem] + [whole_block(o.shape) for o in outs[1:]],
        out_shape=outs,
        compiler_params=pltpu.CompilerParams(vmem_limit_bytes=VMEM_PACK),
        name="pack",
    )(lengths, x, x, *arrays)


def swap(value, link):
    axis, bit = link
    return lax.ppermute(value, axis, [(i, i ^ bit) for i in range(lax.axis_size(axis))])


def half_of(link):
    return (lax.axis_index(link[0]) // link[1]) % 2


def give_half(value, link, dim):
    return lax.dynamic_index_in_dim(value, 1 - half_of(link), dim, keepdims=False).astype(BF)


def keep_half(value, link, dim):
    return lax.dynamic_index_in_dim(value, half_of(link), dim, keepdims=False).astype(F32)


def after(value, *others):
    return lax.optimization_barrier((value, *others))[0]


def shifted(offsets, b, s):
    return tuple((ob ^ b, os ^ s) for ob, os in offsets)


def both_cores(arrays, plan):
    other = [swap(a, CORE) for a in arrays]
    return arrays + other, tuple(plan) + tuple((shifted(o, 1, 0), first) for o, first in plan)


def gather(own, pair, halo):
    cut = own.shape[1] // 2
    top = lambda value: swap(value[:, :cut], Y)
    bottom = lambda value: swap(value[:, cut:], X)
    own_y, own_x, far = lax.optimization_barrier((swap(own, Y), swap(own, X), swap(own, Z1)))
    column = jnp.concatenate([own, far], 0)
    near, far_x, far_y, own_top, own_bottom = lax.optimization_barrier(
        (swap(column, Z0), swap(far, X), swap(far, Y), top(own_x), bottom(own_y))
    )
    pair = after(pair, near, own_top)
    near_y, near_x, far_top, far_bottom, pair_far = lax.optimization_barrier(
        (swap(near, Y), swap(near, X), top(far_x), bottom(far_y), swap(pair, Z1))
    )
    halo = swap(after(halo, far_top), Y)
    near_top, near_bottom = top(near_x), bottom(near_y)
    pair = jnp.concatenate([pair, pair_far], 0)
    pair = jnp.concatenate([pair, swap(pair, Z0)], 0)
    pair_x, pair_y = swap(pair, X), swap(pair, Y)
    across = lax.ppermute(pair, ("x", "seq"), [(i, i ^ 3) for i in range(4)])
    offsets = ((0, 0), (8, 0), (4, 0), (12, 0))
    pair_plan = [(shifted(offsets, b, s), 0) for b, s in ((0, 0), (2, 0), (0, 1), (2, 1))]
    arrays, plan = [column, near], [(((0, 0), (8, 0)), 0), (((4, 0), (12, 0)), 0)]
    for offsets, members in (
        (((0, 0),), (own_x, own_y, own_top, own_bottom)),
        (((8, 0),), (far_x, far_y, far_top, far_bottom)),
        (((4, 0), (12, 0)), (near_x, near_y, near_top, near_bottom)),
    ):
        arrays += members
        plan += [(shifted(offsets, b, s), first) for b, s, first in ((2, 0, 0), (0, 1, 0), (2, 1, 0), (2, 1, cut))]
    return halo, both_cores(arrays, plan), ([pair, pair_x, pair_y, across], pair_plan)


def stage_kernel(columns, joined, flags, *refs):
    count = len(columns)
    outs = refs[2 * count :]
    at = 0
    for i, column in enumerate(columns):
        keep, got = refs[2 * i], refs[2 * i + 1]
        if joined is None:
            give_out, keep_out, where = outs[2 * i], outs[2 * i + 1], Ellipsis
        else:
            taps = keep.shape[1 + joined]
            give_out, keep_out = outs
            where = (*(slice(None),) * joined, slice(at, at + taps))
            at += taps
        bit = flags[5, column]
        give_out[where] = (keep[1 - bit].astype(F32) + got[1 - bit].astype(F32)).astype(BF)
        keep_out[where] = keep[bit].astype(F32) + got[bit].astype(F32)


def first_stage_kernel(cut, flags, keep, got, *outs):
    for i, taps in enumerate((slice(0, cut), slice(cut, keep.shape[3]))):
        bit = flags[5, i]
        give_out, keep_out = outs[2 * i], outs[2 * i + 1]
        for n in range(2):
            other, own = 2 * (1 - bit) + n, 2 * bit + n
            give_out[n] = (keep[other, :, :, taps].astype(F32) + got[other, :, :, taps].astype(F32)).astype(BF)
            keep_out[n] = keep[own, :, :, taps].astype(F32) + got[own, :, :, taps].astype(F32)


def first_stage(flags, keep, got, cut):
    tail = keep.shape[4:]
    outs = [jax.ShapeDtypeStruct((2, 2, 2, n) + tail, kind) for n in (cut, keep.shape[3] - cut) for kind in (BF, F32)]
    return pl.pallas_call(
        functools.partial(first_stage_kernel, cut),
        grid_spec=pltpu.PrefetchScalarGridSpec(
            num_scalar_prefetch=1,
            grid=(1,),
            in_specs=[whole_block(keep.shape)] * 2,
            out_specs=[whole_block(o.shape) for o in outs],
        ),
        out_shape=outs,
        compiler_params=pltpu.CompilerParams(vmem_limit_bytes=VMEM_SUM),
        name="stage",
    )(flags, keep, got)


def stage(flags, parts, columns, joined=None):
    shapes = [keep.shape[1:] for keep, _ in parts]
    if joined is not None:
        first = list(shapes[0])
        first[joined] = sum(shape[joined] for shape in shapes)
        shapes = [tuple(first)]
    outs = [jax.ShapeDtypeStruct(shape, kind) for shape in shapes for kind in (BF, F32)]
    arrays = [a for part in parts for a in part]
    return pl.pallas_call(
        functools.partial(stage_kernel, columns, joined),
        grid_spec=pltpu.PrefetchScalarGridSpec(
            num_scalar_prefetch=1,
            grid=(1,),
            in_specs=[whole_block(a.shape) for a in arrays],
            out_specs=[whole_block(o.shape) for o in outs],
        ),
        out_shape=outs,
        compiler_params=pltpu.CompilerParams(vmem_limit_bytes=VMEM_SUM),
        name="stage",
    )(flags, *arrays)


def local(inputs, window_lengths, conv_weight, conv_bias, norm1_gain, norm1_bias, up_weight, up_bias, down_weight,
          down_bias, norm2_gain, norm2_bias, out_grad):
    _, count, width = inputs.shape
    batch, seq = lax.axis_size(BATCH), lax.axis_size("seq")
    hidden = up_weight.shape[1] * batch
    border = KERNEL_TAPS // 2 * DILATION_STEP
    x, og = inputs[0], pltpu.with_memory_space_constraint(out_grad[0], pltpu.HBM)
    fast = seq == 2 and batch == 16

    def ends(value):
        first, final = value[:border], value[count - border :]
        if fast:
            other = swap(jnp.where(lax.axis_index("seq") == 0, final, first), Y)
            return other, other
        up = [(i, i + 1) for i in range(seq - 1)]
        return lax.ppermute(final, "seq", up), lax.ppermute(first, "seq", [(j, i) for i, j in up])

    vectors = [conv_bias, norm1_gain, norm1_bias, down_bias, norm2_gain, norm2_bias, up_bias]
    sizes = [v.shape[0] for v in vectors]
    small = tuple((sum(sizes[:i]), n) for i, n in enumerate(sizes))
    conv_own = conv_weight.transpose(0, 2, 1)
    flags, halo, conv_block, pair_block = pack(window_lengths, x, conv_own, up_weight, down_weight, vectors, small)
    if fast:
        halo, (conv_pieces, conv_plan), (pair_pieces, pair_plan) = gather(conv_block, pair_block, halo)
        prev = nxt = halo
        table = None
    else:
        def every(value):
            value = lax.all_gather(value, "seq", axis=2, tiled=True)
            return lax.all_gather(value, BATCH, axis=1, tiled=True)

        prev, nxt = ends(x)
        conv_pieces, conv_plan = [every(conv_own)], ((None, 0),)
        pair_pieces, pair_plan = [every(pair_block[0])], ((None, 0),)
        full = [lax.all_gather(v, (*BATCH, "seq"), axis=0, tiled=True).astype(F32) for v in vectors]
        table = jnp.stack([jnp.pad(v, (0, hidden - v.shape[0])) for v in full + [full[0]]])
        small = ()
    conv_pieces, conv_plan = list(conv_pieces), tuple((None if o is None else tuple(o), f) for o, f in conv_plan)
    xhat, scale, conv_full, table = conv_forward(flags, prev, x, nxt, conv_pieces, conv_plan, small, table, 2, hidden)
    if fast:
        pair_pieces, table = lax.optimization_barrier((pair_pieces, table))
        pair_pieces, pair_plan = both_cores(pair_pieces, pair_plan)
    pair_plan = tuple((None if o is None else tuple(o), f) for o, f in pair_plan)
    block_output, grad_hidden, grad_conv, *ffn_grads = ffn(
        flags, x, xhat, scale, og, table, pair_pieces, pair_plan, 2 * SUB, min(1024, hidden), batch, fast
    )
    grads = (flags, prev, x, nxt, grad_conv, grad_hidden, conv_full)
    if fast:
        input_grad, weight_grads = paired(grads, ffn_grads, batch, width, hidden)
    else:
        grad_prev, grad_next = ends(grad_conv)
        conv_grads = conv_weight_backward(flags, prev, x, nxt, grad_conv, batch, fast)
        input_grad = conv_input_backward(flags, grad_prev, grad_conv, grad_next, grad_hidden, conv_full, 2)
        weight_grads = whole_sums(conv_grads, ffn_grads, batch, seq, width, hidden)
    conv_grad, cb, g1, s1, up_grad, ub_grad, down_grad, db, g2, s2 = weight_grads
    return (block_output[None], input_grad[None], conv_grad, cb, g1, s1, up_grad, ub_grad, down_grad, db, g2, s2)


def paired(grads, ffn_grads, batch, width, hidden):
    flags, prev, x, nxt, grad_conv, grad_hidden, conv_full = grads
    up_rows = width // 2 + 16
    edge, ffn_send, ffn_keep = ffn_grads
    ffn_got, grad_prev = swap(ffn_send, CORE), swap(edge, Y)
    early = 2
    parts = conv_weight_backward(flags, prev, x, prev, grad_conv, batch, True, 0, early)
    ffn_got, grad_prev, parts = lax.optimization_barrier((ffn_got, grad_prev, parts))
    up_give, up_keep, down_give, down_keep = first_stage(flags, ffn_keep, ffn_got, up_rows)
    up_got, down_got = swap(up_give, X), swap(down_give, Y)
    first = after(prev, up_give)
    send, keep = conv_weight_backward(
        flags, first, x, first, grad_conv, batch, True, early, KERNEL_TAPS - early, parts
    )
    up_got, down_got, send = lax.optimization_barrier((up_got, down_got, send))
    got = swap(send, CORE)
    parts = [(up_keep, up_got), (down_keep, down_got)]
    up_give, up_keep, down_give, down_keep = stage(flags, parts, (1, 0))
    up_got, down_got = swap(up_give, Y), swap(down_give, X)
    upper_give, upper_keep, lower_give, lower_keep = first_stage(
        flags, keep, after(got, up_give), (KERNEL_TAPS + 1) // 2
    )
    upper_got, lower_got = swap(upper_give, X), swap(lower_give, Y)
    second = after(grad_prev, upper_give)
    input_grad = conv_input_backward(flags, second, grad_conv, second, grad_hidden, conv_full, 2)
    up_got, down_got, input_grad = lax.optimization_barrier((up_got, down_got, input_grad))
    ffn_give, ffn_keep = stage(flags, [(up_keep, up_got), (down_keep, down_got)], (2, 2), 1)
    ffn_got = swap(ffn_give, Z0)
    upper_got, lower_got, _ = lax.optimization_barrier((upper_got, lower_got, ffn_give))
    parts = [(upper_keep, upper_got), (lower_keep, lower_got)]
    upper_give, upper_keep, lower_give, lower_keep = stage(flags, parts, (1, 0))
    upper_got, lower_got = swap(upper_give, Y), swap(lower_give, X)
    ffn_give, ffn_keep = stage(flags, [(ffn_keep, after(ffn_got, upper_give))], (3,))
    ffn_got = swap(ffn_give, Z1)
    upper_got, lower_got, _ = lax.optimization_barrier((upper_got, lower_got, ffn_give))
    conv_give, conv_keep = stage(flags, [(upper_keep, upper_got), (lower_keep, lower_got)], (2, 2), 1)
    conv_got = swap(conv_give, Z0)
    pair_part = ffn_keep + after(ffn_got, conv_give).astype(F32)
    conv_give, conv_keep = stage(flags, [(conv_keep, conv_got)], (3,))
    conv_got = swap(conv_give, Z1)
    conv_grad = (conv_keep + conv_got.astype(F32)).transpose(0, 2, 1)
    head = width // 2
    up_grad = pair_part[:head]
    down_grad = pair_part[up_rows:].T
    each = width // (batch * 2)
    g2, s2, db, g1, s1, cb = (pair_part[head, i * each : (i + 1) * each] for i in range(6))
    ub_grad = pair_part[head + 1, : hidden // (batch * 2)]
    return input_grad, (conv_grad, cb, g1, s1, up_grad, ub_grad, down_grad, db, g2, s2)


def whole_sums(conv_grads, ffn_grads, batch, seq, width, hidden):
    def total(value, dims):
        value = lax.psum_scatter(value, BATCH, scatter_dimension=dims[1], tiled=True)
        return lax.psum_scatter(value, "seq", scatter_dimension=dims[0], tiled=True)

    conv_grad = total(conv_grads[0], (2, 1)).transpose(0, 2, 1)
    up_grad = total(ffn_grads[0], (0, 1))
    down_grad = total(ffn_grads[1], (0, 1)).T
    vec_grads = total(ffn_grads[2].reshape(6, batch, seq, -1), (2, 1)).reshape(6, -1)
    ub_grad = total(ffn_grads[3].reshape(batch, seq, -1), (1, 0)).reshape(-1)
    g2, s2, db, g1, s1, cb = (vec_grads[i] for i in range(6))
    return conv_grad, cb, g1, s1, up_grad, ub_grad, down_grad, db, g2, s2


def solution(mesh):
    batch, seq = mesh.shape["batch"], mesh.shape["seq"]
    split = Mesh(mesh.devices.reshape(batch // 4, 2, 2, seq), (*BATCH, "seq"))
    both = P((*BATCH, "seq"))
    rows = P(BATCH, "seq", None)
    conv, up, down = P(None, "seq", BATCH), P("seq", BATCH), P(BATCH, "seq")
    in_specs = (rows, P(BATCH, None), conv, both, both, both, up, both, down, both, both, both, rows)
    out_specs = (rows, rows, conv, both, both, both, up, both, down, both, both, both)
    return jax.shard_map(local, mesh=split, in_specs=in_specs, out_specs=out_specs, check_vma=False)
```

```python
import functools
import jax
import jax.numpy as jnp
from jax import lax
from jax.experimental import pallas as pl
from jax.experimental.pallas import tpu as pltpu
from jax.sharding import Mesh, PartitionSpec as P

KERNEL_TAPS = 9
DILATION_STEP = 32
EPSILON = 1e-05
SUB = 256
BF = jnp.bfloat16
F32 = jnp.float32
VMEM_CONV = 28 * 2**20
VMEM_FFN = 50 * 2**20
VMEM_FIRST = 30 * 2**20
VMEM_PACK = 60 * 2**20
VMEM_SUM = 24 * 2**20
COST = 1
BATCH = ("z", "x", "core")
X, Y, Z0, Z1, CORE = ("x", 1), ("seq", 1), ("z", 1), ("z", 2), ("core", 1)
NN = (((1,), (0,)), ((), ()))
NT = (((1,), (1,)), ((), ()))
TN = (((0,), (0,)), ((), ()))


def dot(a, b, dims):
    return lax.dot_general(a, b, dims, preferred_element_type=F32)


def conv_cost(count, width):
    return pl.CostEstimate(flops=2 * count * KERNEL_TAPS * width * width // COST, bytes_accessed=2**20, transcendentals=0)


def gelu_pair(v):
    size = jnp.abs(v)
    t = pl.reciprocal(1.0 + 0.23164189 * size, approx=True)
    poly = t * (0.127414796 + t * (-0.142248368 + t * (0.710706871 + t * (-0.726576013 + t * 0.530702714))))
    bell = jnp.exp2(-0.72134752 * (size * size))
    value = jnp.maximum(v, 0.0) - size * (poly * bell)
    low_side = bell * (poly - 0.39894228 * size)
    return value, jnp.where(v >= 0.0, 1.0 - low_side, low_side)


def row_mean(v):
    return jnp.sum(v, -1, keepdims=True) * (1.0 / v.shape[-1])


def fold(v):
    total = v[0:8]
    for r in range(8, v.shape[0], 8):
        total = total + v[r : r + 8]
    return total


def fill_columns(col, load, flags, block, subs, width):
    for r in range(subs):
        j = block * subs + r
        base = j * SUB
        own = flags[2, j].astype(F32).astype(BF)
        before = flags[0, j].astype(F32).astype(BF)
        after = flags[1, j].astype(F32).astype(BF)
        for k in range(KERNEL_TAPS):
            o = (k - KERNEL_TAPS // 2) * DILATION_STEP
            columns = slice(k * width, (k + 1) * width)
            first = r * SUB
            if o < 0:
                col[first : first - o, columns] = load(base + o, -o) * before
                col[first - o : first + SUB, columns] = load(base, SUB + o) * own
            elif o == 0:
                col[first : first + SUB, columns] = load(base, SUB) * own
            else:
                col[first : first + SUB - o, columns] = load(base + o, SUB - o) * own
                col[first + SUB - o : first + SUB, columns] = load(base + SUB, o) * after


def place(plan, batch_index, seq_index, sources, whole, sems):
    copies = []
    taps = whole.shape[0]
    for source, (offsets, first) in zip(sources, plan):
        if offsets is None:
            copies.append(pltpu.make_async_copy(source, whole, sems.at[len(copies)]))
            continue
        _, span, rows, wide = source.shape
        span = min(span, taps - max(first, 0))
        for n, (db, ds) in enumerate(offsets):
            b, s = (db, ds) if first < 0 else (batch_index ^ db, seq_index ^ ds)
            at_rows = pl.ds(pl.multiple_of(b * rows, rows), rows)
            at_columns = pl.ds(pl.multiple_of(s * wide, wide), wide)
            target = whole.at[pl.ds(max(first, 0), span), at_rows, at_columns]
            copies.append(pltpu.make_async_copy(source.at[n, pl.ds(0, span)], target, sems.at[len(copies)]))
    return copies


def count_copies(plan):
    return sum(1 if offsets is None else len(offsets) for offsets, _ in plan)


def spread_table(small, rows, out):
    devices, wide = rows.shape
    for v, (start, each) in enumerate(small):
        length = devices * each
        place_of = lax.broadcasted_iota(jnp.int32, (wide, length), 1) % each + start
        pick = (place_of == lax.broadcasted_iota(jnp.int32, (wide, length), 0)).astype(BF)
        values = dot(rows, pick, NN)
        owner = lax.broadcasted_iota(jnp.int32, (devices, length), 1) // each
        row = lax.broadcasted_iota(jnp.int32, (devices, length), 0)
        own = owner == 2 * (row % (devices // 2)) + row // (devices // 2)
        out[v : v + 1, :length] = jnp.sum(jnp.where(own, values, 0.0), 0, keepdims=True)


def conv_kernel(subs, plan, small, flags, prev, x, nxt, *rest):
    block = pl.program_id(0)
    width = x.shape[1]
    border = prev.shape[0]
    sources = rest[: len(plan)]
    if small:
        xhat_out, scale_out, w_out, table, ext, col, w, sems, out_sem = rest[len(plan) :]
        small_rows = sources[0].shape[2]
    else:
        table, xhat_out, scale_out, w_out, ext, col, w, sems, out_sem = rest[len(plan) :]

    def copies_in():
        return place(plan, flags[4, 0], flags[4, 1], sources, w, sems)

    def whole_out():
        return pltpu.make_async_copy(w.at[pl.ds(0, KERNEL_TAPS)], w_out, out_sem)

    @pl.when(block == 0)
    def _():
        for copy in copies_in():
            copy.start()
        ext[0:border] = prev[...]
        ext[border : border + x.shape[0]] = x[...]
        ext[border + x.shape[0] :] = nxt[...]

        for copy in copies_in():
            copy.wait()
        whole_out().start()
        if small:
            blocks = width // small_rows
            first_row = lax.broadcasted_iota(jnp.int32, (blocks, width), 0) * small_rows
            pick = (first_row == lax.broadcasted_iota(jnp.int32, (blocks, width), 1)).astype(BF)
            rows = dot(pick, w[KERNEL_TAPS], NN).astype(BF)
            spread_table(small, jnp.concatenate([rows[:, : width // 2], rows[:, width // 2 :]], 0), table)

    @pl.when(block == pl.num_programs(0) - 1)
    def _():
        whole_out().wait()

    def load(start, count):
        return ext[pl.ds(pl.multiple_of(start + border, DILATION_STEP), count), :]

    fill_columns(col, load, flags, block, subs, width)
    total = None
    for k in range(KERNEL_TAPS):
        part = dot(col[:, k * width : (k + 1) * width], w[k], NT)
        total = part if total is None else total + part
    value, slope = gelu_pair(total + table[0:1, :width])
    centered = value - row_mean(value)
    rstd = lax.rsqrt(row_mean(centered * centered) + EPSILON)
    xhat_out[...] = centered * rstd
    scale_out[...] = slope * rstd


def whole_block(shape):
    return pl.BlockSpec(shape, lambda *_: (0,) * len(shape), pipeline_mode=pl.Buffered(1))


def conv_forward(flags, prev, x, nxt, sources, plan, small, table, subs, hidden):
    count, width = x.shape
    rows = subs * SUB
    anywhere = [pl.BlockSpec(memory_space=pl.ANY)] * len(sources)
    out_specs = [pl.BlockSpec((rows, width), lambda j, f: (j, 0))] * 2 + [pl.BlockSpec(memory_space=pltpu.HBM)]
    out_shape = [pltpu.HBM((count, width), F32)] * 2 + [pltpu.HBM((KERNEL_TAPS, width, width), BF)]
    scratch = [
        pltpu.VMEM((count + 2 * prev.shape[0], width), BF),
        pltpu.VMEM((rows, KERNEL_TAPS * width), BF),
        pltpu.VMEM((KERNEL_TAPS + bool(small), width, width), BF),
        pltpu.SemaphoreType.DMA((count_copies(plan),)),
        pltpu.SemaphoreType.DMA,
    ]
    extra_specs, extra = [], []
    if small:
        out_specs = out_specs + [whole_block((8, hidden))]
        out_shape = out_shape + [jax.ShapeDtypeStruct((8, hidden), F32)]
    else:
        extra_specs, extra = [whole_block(table.shape)], [table]
    outs = pl.pallas_call(
        functools.partial(conv_kernel, subs, plan, small),
        grid_spec=pltpu.PrefetchScalarGridSpec(
            num_scalar_prefetch=1,
            grid=(count // rows,),
            in_specs=[whole_block(prev.shape), whole_block(x.shape), whole_block(nxt.shape)] + anywhere + extra_specs,
            out_specs=out_specs,
            scratch_shapes=scratch,
        ),
        out_shape=out_shape,
        compiler_params=pltpu.CompilerParams(vmem_limit_bytes=VMEM_FIRST),
        cost_estimate=pl.CostEstimate(flops=1, bytes_accessed=1, transcendentals=0),
        name="conv_forward",
    )(flags, prev, x, nxt, *sources, *extra)
    return outs if small else (*outs, table)


def ffn_kernel(chunk, fast, plan, flags, x, xhat, scale, og, table, *rest):
    sources, rest = rest[: len(plan)], rest[len(plan) :]
    out, gh_out, gc_out, *rest = rest
    act, slope, dup, ddown, sums, ub_sums, pair, sems = rest[-8:]
    step = pl.program_id(0)
    last = pl.num_programs(0) - 1
    _, hidden, width = pair.shape
    chunks = hidden // chunk
    gain1, shift1, db, gain2, shift2 = (table[i : i + 1, :width] for i in range(1, 6))
    ub = table[6:7, :]

    @pl.when(step == 0)
    def _():
        copies = place(plan, flags[4, 0], flags[4, 1], sources, pair, sems)
        for copy in copies:
            copy.start()
        dup[...] = jnp.zeros_like(dup)
        ddown[...] = jnp.zeros_like(ddown)
        sums[...] = jnp.zeros_like(sums)
        ub_sums[...] = jnp.zeros_like(ub_sums)
        for copy in copies:
            copy.wait()

    one = x[...].astype(F32) + (xhat[...] * gain1 + shift1)
    low = one.astype(BF)
    total = None
    for f in range(chunks):
        cols = slice(f * chunk, (f + 1) * chunk)
        value, s = gelu_pair(dot(low, pair[0, cols, :], NT) + ub[:, cols])
        a = value.astype(BF)
        act[:, cols] = a
        slope[:, cols] = s
        part = dot(a, pair[1, cols, :], NN)
        total = part if total is None else total + part
    d = total + db
    centered = d - row_mean(d)
    rstd = lax.rsqrt(row_mean(centered * centered) + EPSILON)
    hat = centered * rstd
    out[...] = (one + (hat * gain2 + shift2)).astype(BF)
    g = og[...].astype(F32)
    e = g * gain2
    gd = (rstd * (e - row_mean(e) - hat * row_mean(e * hat))).astype(BF)
    sums[0] += fold(g * hat)
    sums[1] += fold(g)
    sums[2] += fold(gd.astype(F32))
    gh = g
    for f in range(chunks):
        cols = slice(f * chunk, (f + 1) * chunk)
        ddown[:, cols] += dot(gd, act[:, cols], TN)
        gu = dot(gd, pair[1, cols, :], NT) * slope[:, cols]
        gul = gu.astype(BF)
        ub_sums[:, cols] += fold(gul.astype(F32))
        dup[:, cols] += dot(low, gul, TN)
        gh = gh + dot(gul, pair[0, cols, :], NN)
    gh_out[...] = gh
    sums[3] += fold(gh * xhat[...])
    sums[4] += fold(gh)
    e = gh * gain1
    gc = (scale[...] * (e - row_mean(e) - xhat[...] * row_mean(e * xhat[...]))).astype(BF)
    gc_out[...] = gc
    if fast:
        edge = rest[0]
        border = edge.shape[0]

        @pl.when((step == 0) & (flags[4, 1] == 1))
        def _():
            edge[...] = gc[:border]

        @pl.when((step == last) & (flags[4, 1] == 0))
        def _():
            edge[...] = gc[gc.shape[0] - border :]

    sums[5] += fold(gc.astype(F32))

    @pl.when(step == last)
    def _():
        if not fast:
            up_out, down_out, sums_out, ub_out = rest[:4]
            up_out[...] = dup[...]
            down_out[...] = ddown[...]
            sums_out[...] = jnp.sum(sums[...], 1)
            ub_out[...] = jnp.sum(ub_sums[...], 0, keepdims=True)
            return
        send, keep = rest[1:3]
        mine = flags[3, 0] == 0
        block = send.shape[-1]
        half = width // 2
        devices = 2 * (hidden // block)

        def own(length):
            each = length // devices
            place = lax.broadcasted_iota(jnp.int32, (devices, length), 1) // each
            return place == lax.broadcasted_iota(jnp.int32, (devices, length), 0)

        def pick(length, start):
            each = length // devices
            place = lax.broadcasted_iota(jnp.int32, (length, 128), 0) % each + start
            return (place == lax.broadcasted_iota(jnp.int32, (length, 128), 1)).astype(BF)

        first = None
        for v in range(6):
            line = jnp.sum(sums[v], 0, keepdims=True)
            part = dot(jnp.where(own(width), line, 0.0).astype(BF), pick(width, v * (width // devices)), NN)
            first = part if first is None else first + part
        line = jnp.sum(ub_sums[...], 0, keepdims=True)
        second = dot(jnp.where(own(hidden), line, 0.0).astype(BF), pick(hidden, 0), NN)
        index = lax.broadcasted_iota(jnp.int32, (16, 128), 0)

        def tail(b, s):
            at = 2 * b + s
            return jnp.where(index == 0, first[at : at + 1], jnp.where(index == 1, second[at : at + 1], 0.0)).astype(BF)

        for b in range(0, hidden // block, 2):
            for s in range(2):
                take = slice(s * half, (s + 1) * half)
                x_bit, z = b // 2 % 2, (b // 4 % 2, b // 8)
                up_at, down_at = (2 * x_bit + s, *z), (2 * s + x_bit, *z)
                for acc, at, start in ((dup, up_at, 0), (ddown, down_at, half + 16)):
                    lo = acc[take, b * block : (b + 1) * block].astype(BF)
                    hi = acc[take, (b + 1) * block : (b + 2) * block].astype(BF)
                    send[(*at, slice(start, start + half))] = jnp.where(mine, hi, lo)
                    keep[(*at, slice(start, start + half))] = jnp.where(mine, lo, hi)
                lo, hi = tail(b, s), tail(b + 1, s)
                send[(*up_at, slice(half, half + 16))] = jnp.where(mine, hi, lo)
                keep[(*up_at, slice(half, half + 16))] = jnp.where(mine, lo, hi)


def ffn(flags, x, xhat, scale, og, table, sources, plan, rows, chunk, batch, fast):
    count, width = x.shape
    hidden = table.shape[1]
    tile = pl.BlockSpec((rows, width), lambda j, f: (j, 0))
    sds = jax.ShapeDtypeStruct
    if fast:
        border = KERNEL_TAPS // 2 * DILATION_STEP
        shapes = [sds((border, width), BF)] + [sds((4, 2, 2, width + 16, hidden // batch), BF)] * 2
    else:
        shapes = [sds(s, F32) for s in ((width, hidden), (width, hidden), (6, width), (1, hidden))]
    anywhere = [pl.BlockSpec(memory_space=pl.ANY)] * len(sources)
    return pl.pallas_call(
        functools.partial(ffn_kernel, chunk, fast, plan),
        grid_spec=pltpu.PrefetchScalarGridSpec(
            num_scalar_prefetch=1,
            grid=(count // rows,),
            in_specs=[tile, tile, tile, tile, whole_block(table.shape)] + anywhere,
            out_specs=[tile, tile, tile] + [whole_block(s.shape) for s in shapes],
            scratch_shapes=[
                pltpu.VMEM((rows, hidden), BF),
                pltpu.VMEM((rows, hidden), F32),
                pltpu.VMEM((width, hidden), F32),
                pltpu.VMEM((width, hidden), F32),
                pltpu.VMEM((6, 8, width), F32),
                pltpu.VMEM((8, hidden), F32),
                pltpu.VMEM((2, hidden, width), BF),
                pltpu.SemaphoreType.DMA((count_copies(plan),)),
            ],
        ),
        out_shape=[pltpu.HBM((count, width), BF), pltpu.HBM((count, width), F32), (pltpu.VMEM if fast else pltpu.HBM)((count, width), BF)] + shapes,
        compiler_params=pltpu.CompilerParams(vmem_limit_bytes=VMEM_FFN if fast else VMEM_PACK),
        cost_estimate=pl.CostEstimate(flops=12 * count * width * hidden // COST, bytes_accessed=2**20, transcendentals=0),
        name="feed_forward",
    )(flags, x, xhat, scale, og, table, *sources)


def conv_weight_kernel(fast, first, flags, prev, x, nxt, g, *rest):
    ext, col = rest[-2:]
    outs = rest[:-2] if first == 0 else rest[2:-2]
    tap = pl.program_id(0) + first
    count, width = g.shape
    border = prev.shape[0]
    subs = count // SUB

    @pl.when(tap == first)
    def _():
        ext[0:border] = prev[...]
        ext[border : border + count] = x[...]
        ext[border + count :] = nxt[...]

    o = (tap - KERNEL_TAPS // 2) * DILATION_STEP
    offset = lax.broadcasted_iota(jnp.int32, (SUB, 1), 0) + o
    for r in range(subs):
        own = flags[2, r].astype(F32)
        before = flags[0, r].astype(F32)
        after = flags[1, r].astype(F32)
        mask = jnp.where(offset < 0, before, jnp.where(offset >= SUB, after, own)).astype(BF)
        rows = ext[pl.ds(pl.multiple_of(r * SUB + o + border, DILATION_STEP), SUB), :]
        col[r * SUB : (r + 1) * SUB, :] = rows * mask

    grad = dot(g[...], col[...], TN)
    if not fast:
        outs[0][0] = grad
        return
    mine = flags[3, 0] == 0
    half = width // 2

    send, keep = outs
    block = send.shape[4]
    early = (tap < (KERNEL_TAPS + 1) // 2).astype(jnp.int32)
    for s in range(2):
        columns = slice(s * half, (s + 1) * half)
        for b in range(0, width // block, 2):
            bit = b // 2 % 2
            at = (early * (2 * bit + s) + (1 - early) * (2 * s + bit), b // 4 % 2, b // 8, 0)
            lo = grad[b * block : (b + 1) * block, columns].astype(BF)
            hi = grad[(b + 1) * block : (b + 2) * block, columns].astype(BF)
            send[at] = jnp.where(mine, hi, lo)
            keep[at] = jnp.where(mine, lo, hi)


def conv_weight_backward(flags, prev, x, nxt, g, batch, fast, first=0, taps=KERNEL_TAPS, into=()):
    count, width = x.shape
    if fast:
        block = (4, 2, 2, 1, width // batch, width // 2)
        specs = [pl.BlockSpec(block, lambda k, f: (0, 0, 0, k + first, 0, 0))] * 2
        shapes = [jax.ShapeDtypeStruct(block[:3] + (KERNEL_TAPS,) + block[4:], BF)] * 2
    else:
        specs = [pl.BlockSpec((1, width, width), lambda k, f: (k, 0, 0))]
        shapes = [jax.ShapeDtypeStruct((KERNEL_TAPS, width, width), F32)]
    return pl.pallas_call(
        functools.partial(conv_weight_kernel, fast, first),
        grid_spec=pltpu.PrefetchScalarGridSpec(
            num_scalar_prefetch=1,
            grid=(taps,),
            in_specs=[whole_block(a.shape) for a in (prev, x, nxt, g)] + [pl.BlockSpec(memory_space=pl.ANY)] * len(into),
            out_specs=specs,
            scratch_shapes=[
                pltpu.VMEM((count + 2 * prev.shape[0], width), BF),
                pltpu.VMEM((count, width), BF),
            ],
        ),
        out_shape=shapes,
        compiler_params=pltpu.CompilerParams(vmem_limit_bytes=VMEM_CONV),
        cost_estimate=conv_cost(count * taps // KERNEL_TAPS, width),
        input_output_aliases={5 + i: i for i in range(len(into))},
        name="conv_weight_backward",
    )(flags, prev, x, nxt, g, *into)


def conv_input_kernel(subs, flags, prev, g, nxt, gh, w, out, ext, col):
    step = pl.program_id(0)
    count, width = g.shape
    border = prev.shape[0]

    @pl.when(step == 0)
    def _():
        ext[0:border] = prev[...]
        ext[border : border + count] = g[...]
        ext[border + count :] = nxt[...]

    def load(start, size):
        return ext[pl.ds(pl.multiple_of(start + border, DILATION_STEP), size), :]

    fill_columns(col, load, flags, step, subs, width)
    total = gh[...]
    for k in range(KERNEL_TAPS):
        total = total + dot(col[:, k * width : (k + 1) * width], w[KERNEL_TAPS - 1 - k], NN)
    out[...] = total


def conv_input_backward(flags, prev, g, nxt, gh, weights, subs):
    count, width = g.shape
    rows = subs * SUB
    tile = pl.BlockSpec((rows, width), lambda j, f: (j, 0))
    return pl.pallas_call(
        functools.partial(conv_input_kernel, subs),
        grid_spec=pltpu.PrefetchScalarGridSpec(
            num_scalar_prefetch=1,
            grid=(count // rows,),
            in_specs=[whole_block(a.shape) for a in (prev, g, nxt)] + [tile, whole_block(weights.shape)],
            out_specs=tile,
            scratch_shapes=[
                pltpu.VMEM((count + 2 * prev.shape[0], width), BF),
                pltpu.VMEM((rows, KERNEL_TAPS * width), BF),
            ],
        ),
        out_shape=jax.ShapeDtypeStruct((count, width), F32),
        compiler_params=pltpu.CompilerParams(vmem_limit_bytes=VMEM_CONV),
        cost_estimate=conv_cost(count, width),
        name="conv_input_backward",
    )(flags, prev, g, nxt, gh, weights)


def pack_kernel(small, slots, count, lengths, first, final, conv, up, down, *rest):
    vectors, (flags, halo, conv_out, pair_out) = rest[: len(small)], rest[len(small) :]
    batch_index = lax.axis_index("z") * 4 + lax.axis_index("x") * 2 + lax.axis_index("core")
    seq_index = lax.axis_index("seq")
    taps, rows, wide = conv.shape
    subs = flags.shape[1]
    conv_out[0, 0:taps] = conv[...]
    line = None
    for v, (start, each) in zip(vectors, small):
        pick = (
            lax.broadcasted_iota(jnp.int32, (each, wide), 0) + start == lax.broadcasted_iota(jnp.int32, (each, wide), 1)
        ).astype(BF)
        part = dot(jnp.broadcast_to(v[...], (rows, each)), pick, NN)
        line = part if line is None else line + part
    conv_out[0, taps] = line.astype(BF)
    pair_out[0, 0] = up[...].T
    pair_out[0, 1] = down[...]
    halo[...] = jnp.where(seq_index == 0, final[...], first[...])
    ends = []
    total = 0
    for i in range(slots):
        total = total + lengths[0, i]
        ends.append(total)
    ids = []
    for j in range(-1, subs + 1):
        start = seq_index * count + j * SUB
        number = 0
        for end in ends:
            number = number + (start >= end).astype(jnp.int32)
        ids.append(jnp.where(start >= 0, number, -1))
    for j in range(subs):
        inside = (ids[j + 1] < slots).astype(jnp.int32)
        flags[0, j] = (ids[j] == ids[j + 1]).astype(jnp.int32) * inside
        flags[1, j] = (ids[j + 2] == ids[j + 1]).astype(jnp.int32) * inside
        flags[2, j] = inside
        flags[3, j] = batch_index % 2
        flags[4, j] = batch_index if j == 0 else seq_index
        bits = (lax.axis_index("x"), seq_index, lax.axis_index("z") % 2, lax.axis_index("z") // 2)
        flags[5, j] = bits[min(j, 3)]


def pack(lengths, x, conv, up, down, vectors, small):
    taps, rows, wide = conv.shape
    count, width = x.shape
    border = KERNEL_TAPS // 2 * DILATION_STEP
    smem = pl.BlockSpec(memory_space=pltpu.SMEM)
    arrays = [conv, up, down] + [v[None] for v in vectors]
    end_rows = pl.BlockSpec((border, width), lambda i: (0, 0))
    final_rows = pl.BlockSpec((border, width), lambda i: (count // border - 1, 0))
    sds = jax.ShapeDtypeStruct
    outs = [
        sds((6, count // SUB), jnp.int32),
        sds((border, width), BF),
        sds((1, taps + 1, rows, wide), BF),
        sds((1, 2) + down.shape, BF),
    ]
    return pl.pallas_call(
        functools.partial(pack_kernel, small, lengths.shape[1], count),
        grid=(1,),
        in_specs=[smem, end_rows, final_rows] + [whole_block(a.shape) for a in arrays],
        out_specs=[smem] + [whole_block(o.shape) for o in outs[1:]],
        out_shape=outs,
        compiler_params=pltpu.CompilerParams(vmem_limit_bytes=VMEM_PACK),
        name="pack",
    )(lengths, x, x, *arrays)


def swap(value, link):
    axis, bit = link
    return lax.ppermute(value, axis, [(i, i ^ bit) for i in range(lax.axis_size(axis))])


def half_of(link):
    return (lax.axis_index(link[0]) // link[1]) % 2


def give_half(value, link, dim):
    return lax.dynamic_index_in_dim(value, 1 - half_of(link), dim, keepdims=False).astype(BF)


def keep_half(value, link, dim):
    return lax.dynamic_index_in_dim(value, half_of(link), dim, keepdims=False).astype(F32)


def after(value, *others):
    return lax.optimization_barrier((value, *others))[0]


def shifted(offsets, b, s):
    return tuple((ob ^ b, os ^ s) for ob, os in offsets)


def both_cores(arrays, plan):
    other = [swap(a, CORE) for a in arrays]
    return arrays + other, tuple(plan) + tuple((shifted(o, 1, 0), first) for o, first in plan)


def gather(own, pair, halo):
    cut = own.shape[1] // 2
    top = lambda value: swap(value[:, :cut], Y)
    bottom = lambda value: swap(value[:, cut:], X)
    own_y, own_x, far = lax.optimization_barrier((swap(own, Y), swap(own, X), swap(own, Z1)))
    column = jnp.concatenate([own, far], 0)
    near, far_x, far_y, own_top, own_bottom = lax.optimization_barrier(
        (swap(column, Z0), swap(far, X), swap(far, Y), top(own_x), bottom(own_y))
    )
    pair = after(pair, near, own_top)
    near_y, near_x, far_top, far_bottom, pair_far = lax.optimization_barrier(
        (swap(near, Y), swap(near, X), top(far_x), bottom(far_y), swap(pair, Z1))
    )
    pair_far, near_x, near_y = lax.optimization_barrier((pair_far, near_x, near_y))
    halo = swap(after(halo, near_x), Y)
    near_top, near_bottom = top(near_x), bottom(near_y)
    pair = jnp.concatenate([pair, pair_far], 0)
    pair = jnp.concatenate([pair, swap(pair, Z0)], 0)
    pair_x, pair_y = swap(pair, X), swap(pair, Y)
    across = lax.ppermute(pair, ("x", "seq"), [(i, i ^ 3) for i in range(4)])
    offsets = ((0, 0), (8, 0), (4, 0), (12, 0))
    pair_plan = [(shifted(offsets, b, s), 0) for b, s in ((0, 0), (2, 0), (0, 1), (2, 1))]
    arrays, plan = [column, near], [(((0, 0), (8, 0)), 0), (((4, 0), (12, 0)), 0)]
    for offsets, members in (
        (((0, 0),), (own_x, own_y, own_top, own_bottom)),
        (((8, 0),), (far_x, far_y, far_top, far_bottom)),
        (((4, 0), (12, 0)), (near_x, near_y, near_top, near_bottom)),
    ):
        arrays += members
        plan += [(shifted(offsets, b, s), first) for b, s, first in ((2, 0, 0), (0, 1, 0), (2, 1, 0), (2, 1, cut))]
    return halo, both_cores(arrays, plan), ([pair, pair_x, pair_y, across], pair_plan)


def stage_kernel(columns, joined, flags, *refs):
    count = len(columns)
    outs = refs[2 * count :]
    at = 0
    for i, column in enumerate(columns):
        keep, got = refs[2 * i], refs[2 * i + 1]
        if joined is None:
            give_out, keep_out, where = outs[2 * i], outs[2 * i + 1], Ellipsis
        else:
            taps = keep.shape[1 + joined]
            give_out, keep_out = outs
            where = (*(slice(None),) * joined, slice(at, at + taps))
            at += taps
        bit = flags[5, column]
        give_out[where] = (keep[1 - bit].astype(F32) + got[1 - bit].astype(F32)).astype(BF)
        keep_out[where] = keep[bit].astype(F32) + got[bit].astype(F32)


def first_stage_kernel(cut, flags, keep, got, *outs):
    for i, taps in enumerate((slice(0, cut), slice(cut, keep.shape[3]))):
        bit = flags[5, i]
        give_out, keep_out = outs[2 * i], outs[2 * i + 1]
        for n in range(2):
            other, own = 2 * (1 - bit) + n, 2 * bit + n
            give_out[n] = (keep[other, :, :, taps].astype(F32) + got[other, :, :, taps].astype(F32)).astype(BF)
            keep_out[n] = keep[own, :, :, taps].astype(F32) + got[own, :, :, taps].astype(F32)


def first_stage(flags, keep, got, cut):
    tail = keep.shape[4:]
    outs = [jax.ShapeDtypeStruct((2, 2, 2, n) + tail, kind) for n in (cut, keep.shape[3] - cut) for kind in (BF, F32)]
    return pl.pallas_call(
        functools.partial(first_stage_kernel, cut),
        grid_spec=pltpu.PrefetchScalarGridSpec(
            num_scalar_prefetch=1,
            grid=(1,),
            in_specs=[whole_block(keep.shape)] * 2,
            out_specs=[whole_block(o.shape) for o in outs],
        ),
        out_shape=outs,
        compiler_params=pltpu.CompilerParams(vmem_limit_bytes=VMEM_SUM),
        name="stage",
    )(flags, keep, got)


def stage(flags, parts, columns, joined=None):
    shapes = [keep.shape[1:] for keep, _ in parts]
    if joined is not None:
        first = list(shapes[0])
        first[joined] = sum(shape[joined] for shape in shapes)
        shapes = [tuple(first)]
    outs = [jax.ShapeDtypeStruct(shape, kind) for shape in shapes for kind in (BF, F32)]
    arrays = [a for part in parts for a in part]
    return pl.pallas_call(
        functools.partial(stage_kernel, columns, joined),
        grid_spec=pltpu.PrefetchScalarGridSpec(
            num_scalar_prefetch=1,
            grid=(1,),
            in_specs=[whole_block(a.shape) for a in arrays],
            out_specs=[whole_block(o.shape) for o in outs],
        ),
        out_shape=outs,
        compiler_params=pltpu.CompilerParams(vmem_limit_bytes=VMEM_SUM),
        name="stage",
    )(flags, *arrays)


def local(inputs, window_lengths, conv_weight, conv_bias, norm1_gain, norm1_bias, up_weight, up_bias, down_weight,
          down_bias, norm2_gain, norm2_bias, out_grad):
    _, count, width = inputs.shape
    batch, seq = lax.axis_size(BATCH), lax.axis_size("seq")
    hidden = up_weight.shape[1] * batch
    border = KERNEL_TAPS // 2 * DILATION_STEP
    x, og = inputs[0], pltpu.with_memory_space_constraint(out_grad[0], pltpu.HBM)
    fast = seq == 2 and batch == 16

    def ends(value):
        first, final = value[:border], value[count - border :]
        if fast:
            other = swap(jnp.where(lax.axis_index("seq") == 0, final, first), Y)
            return other, other
        up = [(i, i + 1) for i in range(seq - 1)]
        return lax.ppermute(final, "seq", up), lax.ppermute(first, "seq", [(j, i) for i, j in up])

    vectors = [conv_bias, norm1_gain, norm1_bias, down_bias, norm2_gain, norm2_bias, up_bias]
    sizes = [v.shape[0] for v in vectors]
    small = tuple((sum(sizes[:i]), n) for i, n in enumerate(sizes))
    conv_own = conv_weight.transpose(0, 2, 1)
    flags, halo, conv_block, pair_block = pack(window_lengths, x, conv_own, up_weight, down_weight, vectors, small)
    if fast:
        halo, (conv_pieces, conv_plan), (pair_pieces, pair_plan) = gather(conv_block, pair_block, halo)
        prev = nxt = halo
        table = None
    else:
        def every(value):
            value = lax.all_gather(value, "seq", axis=2, tiled=True)
            return lax.all_gather(value, BATCH, axis=1, tiled=True)

        prev, nxt = ends(x)
        conv_pieces, conv_plan = [every(conv_own)], ((None, 0),)
        pair_pieces, pair_plan = [every(pair_block[0])], ((None, 0),)
        full = [lax.all_gather(v, (*BATCH, "seq"), axis=0, tiled=True).astype(F32) for v in vectors]
        table = jnp.stack([jnp.pad(v, (0, hidden - v.shape[0])) for v in full + [full[0]]])
        small = ()
    conv_pieces, conv_plan = list(conv_pieces), tuple((None if o is None else tuple(o), f) for o, f in conv_plan)
    xhat, scale, conv_full, table = conv_forward(flags, prev, x, nxt, conv_pieces, conv_plan, small, table, 2, hidden)
    if fast:
        pair_pieces, table = lax.optimization_barrier((pair_pieces, table))
        pair_pieces, pair_plan = both_cores(pair_pieces, pair_plan)
    pair_plan = tuple((None if o is None else tuple(o), f) for o, f in pair_plan)
    block_output, grad_hidden, grad_conv, *ffn_grads = ffn(
        flags, x, xhat, scale, og, table, pair_pieces, pair_plan, 2 * SUB, min(1024, hidden), batch, fast
    )
    grads = (flags, prev, x, nxt, grad_conv, grad_hidden, conv_full)
    if fast:
        input_grad, weight_grads = paired(grads, ffn_grads, batch, width, hidden)
    else:
        grad_prev, grad_next = ends(grad_conv)
        conv_grads = conv_weight_backward(flags, prev, x, nxt, grad_conv, batch, fast)
        input_grad = conv_input_backward(flags, grad_prev, grad_conv, grad_next, grad_hidden, conv_full, 2)
        weight_grads = whole_sums(conv_grads, ffn_grads, batch, seq, width, hidden)
    conv_grad, cb, g1, s1, up_grad, ub_grad, down_grad, db, g2, s2 = weight_grads
    return (block_output[None], input_grad[None], conv_grad, cb, g1, s1, up_grad, ub_grad, down_grad, db, g2, s2)


def paired(grads, ffn_grads, batch, width, hidden):
    flags, prev, x, nxt, grad_conv, grad_hidden, conv_full = grads
    up_rows = width // 2 + 16
    edge, ffn_send, ffn_keep = ffn_grads
    ffn_got, grad_prev = swap(ffn_send, CORE), swap(edge, Y)
    early = 2
    parts = conv_weight_backward(flags, prev, x, prev, grad_conv, batch, True, 0, early)
    ffn_got, grad_prev, parts = lax.optimization_barrier((ffn_got, grad_prev, parts))
    up_give, up_keep, down_give, down_keep = first_stage(flags, ffn_keep, ffn_got, up_rows)
    up_got, down_got = swap(up_give, X), swap(down_give, Y)
    first = after(prev, up_give)
    send, keep = conv_weight_backward(
        flags, first, x, first, grad_conv, batch, True, early, KERNEL_TAPS - early, parts
    )
    up_got, down_got, send = lax.optimization_barrier((up_got, down_got, send))
    got = swap(send, CORE)
    parts = [(up_keep, up_got), (down_keep, down_got)]
    up_give, up_keep, down_give, down_keep = stage(flags, parts, (1, 0))
    up_got, down_got = swap(up_give, Y), swap(down_give, X)
    upper_give, upper_keep, lower_give, lower_keep = first_stage(
        flags, keep, after(got, up_give), (KERNEL_TAPS + 1) // 2
    )
    upper_got, lower_got = swap(upper_give, X), swap(lower_give, Y)
    second = after(grad_prev, upper_give)
    input_grad = conv_input_backward(flags, second, grad_conv, second, grad_hidden, conv_full, 2)
    up_got, down_got, input_grad = lax.optimization_barrier((up_got, down_got, input_grad))
    ffn_give, ffn_keep = stage(flags, [(up_keep, up_got), (down_keep, down_got)], (2, 2), 1)
    ffn_got = swap(ffn_give, Z0)
    upper_got, lower_got, _ = lax.optimization_barrier((upper_got, lower_got, ffn_give))
    parts = [(upper_keep, upper_got), (lower_keep, lower_got)]
    upper_give, upper_keep, lower_give, lower_keep = stage(flags, parts, (1, 0))
    upper_got, lower_got = swap(upper_give, Y), swap(lower_give, X)
    ffn_give, ffn_keep = stage(flags, [(ffn_keep, after(ffn_got, upper_give))], (3,))
    ffn_got = swap(ffn_give, Z1)
    upper_got, lower_got, _ = lax.optimization_barrier((upper_got, lower_got, ffn_give))
    conv_give, conv_keep = stage(flags, [(upper_keep, upper_got), (lower_keep, lower_got)], (2, 2), 1)
    conv_got = swap(conv_give, Z0)
    pair_part = ffn_keep + after(ffn_got, conv_give).astype(F32)
    conv_give, conv_keep = stage(flags, [(conv_keep, conv_got)], (3,))
    conv_got = swap(conv_give, Z1)
    conv_grad = (conv_keep + conv_got.astype(F32)).transpose(0, 2, 1)
    head = width // 2
    up_grad = pair_part[:head]
    down_grad = pair_part[up_rows:].T
    each = width // (batch * 2)
    g2, s2, db, g1, s1, cb = (pair_part[head, i * each : (i + 1) * each] for i in range(6))
    ub_grad = pair_part[head + 1, : hidden // (batch * 2)]
    return input_grad, (conv_grad, cb, g1, s1, up_grad, ub_grad, down_grad, db, g2, s2)


def whole_sums(conv_grads, ffn_grads, batch, seq, width, hidden):
    def total(value, dims):
        value = lax.psum_scatter(value, BATCH, scatter_dimension=dims[1], tiled=True)
        return lax.psum_scatter(value, "seq", scatter_dimension=dims[0], tiled=True)

    conv_grad = total(conv_grads[0], (2, 1)).transpose(0, 2, 1)
    up_grad = total(ffn_grads[0], (0, 1))
    down_grad = total(ffn_grads[1], (0, 1)).T
    vec_grads = total(ffn_grads[2].reshape(6, batch, seq, -1), (2, 1)).reshape(6, -1)
    ub_grad = total(ffn_grads[3].reshape(batch, seq, -1), (1, 0)).reshape(-1)
    g2, s2, db, g1, s1, cb = (vec_grads[i] for i in range(6))
    return conv_grad, cb, g1, s1, up_grad, ub_grad, down_grad, db, g2, s2


def solution(mesh):
    batch, seq = mesh.shape["batch"], mesh.shape["seq"]
    split = Mesh(mesh.devices.reshape(batch // 4, 2, 2, seq), (*BATCH, "seq"))
    both = P((*BATCH, "seq"))
    rows = P(BATCH, "seq", None)
    conv, up, down = P(None, "seq", BATCH), P("seq", BATCH), P(BATCH, "seq")
    in_specs = (rows, P(BATCH, None), conv, both, both, both, up, both, down, both, both, both, rows)
    out_specs = (rows, rows, conv, both, both, both, up, both, down, both, both, both)
    return jax.shard_map(local, mesh=split, in_specs=in_specs, out_specs=out_specs, check_vma=False)
```

```python
import functools
import jax
import jax.numpy as jnp
from jax import lax
from jax.experimental import pallas as pl
from jax.experimental.pallas import tpu as pltpu
from jax.sharding import Mesh, PartitionSpec as P

KERNEL_TAPS = 9
DILATION_STEP = 32
EPSILON = 1e-05
SUB = 256
BF = jnp.bfloat16
F32 = jnp.float32
VMEM_CONV = 28 * 2**20
VMEM_FFN = 50 * 2**20
VMEM_FIRST = 30 * 2**20
VMEM_PACK = 60 * 2**20
VMEM_SUM = 24 * 2**20
COST = 1
BATCH = ("z", "x", "core")
X, Y, Z0, Z1, CORE = ("x", 1), ("seq", 1), ("z", 1), ("z", 2), ("core", 1)
NN = (((1,), (0,)), ((), ()))
NT = (((1,), (1,)), ((), ()))
TN = (((0,), (0,)), ((), ()))


def dot(a, b, dims):
    return lax.dot_general(a, b, dims, preferred_element_type=F32)


def conv_cost(count, width):
    return pl.CostEstimate(flops=2 * count * KERNEL_TAPS * width * width // COST, bytes_accessed=2**20, transcendentals=0)


def gelu_pair(v):
    size = jnp.abs(v)
    t = pl.reciprocal(1.0 + 0.23164189 * size, approx=True)
    poly = t * (0.127414796 + t * (-0.142248368 + t * (0.710706871 + t * (-0.726576013 + t * 0.530702714))))
    bell = jnp.exp2(-0.72134752 * (size * size))
    value = jnp.maximum(v, 0.0) - size * (poly * bell)
    low_side = bell * (poly - 0.39894228 * size)
    return value, jnp.where(v >= 0.0, 1.0 - low_side, low_side)


def row_mean(v):
    return jnp.sum(v, -1, keepdims=True) * (1.0 / v.shape[-1])


def fold(v):
    total = v[0:8]
    for r in range(8, v.shape[0], 8):
        total = total + v[r : r + 8]
    return total


def fill_columns(col, load, flags, block, subs, width):
    for r in range(subs):
        j = block * subs + r
        base = j * SUB
        own = flags[2, j].astype(F32).astype(BF)
        before = flags[0, j].astype(F32).astype(BF)
        after = flags[1, j].astype(F32).astype(BF)
        for k in range(KERNEL_TAPS):
            o = (k - KERNEL_TAPS // 2) * DILATION_STEP
            columns = slice(k * width, (k + 1) * width)
            first = r * SUB
            if o < 0:
                col[first : first - o, columns] = load(base + o, -o) * before
                col[first - o : first + SUB, columns] = load(base, SUB + o) * own
            elif o == 0:
                col[first : first + SUB, columns] = load(base, SUB) * own
            else:
                col[first : first + SUB - o, columns] = load(base + o, SUB - o) * own
                col[first + SUB - o : first + SUB, columns] = load(base + SUB, o) * after


def place(plan, batch_index, seq_index, sources, whole, sems):
    copies = []
    taps = whole.shape[0]
    for source, (offsets, first) in zip(sources, plan):
        if offsets is None:
            copies.append(pltpu.make_async_copy(source, whole, sems.at[len(copies)]))
            continue
        _, span, rows, wide = source.shape
        span = min(span, taps - max(first, 0))
        for n, (db, ds) in enumerate(offsets):
            b, s = (db, ds) if first < 0 else (batch_index ^ db, seq_index ^ ds)
            at_rows = pl.ds(pl.multiple_of(b * rows, rows), rows)
            at_columns = pl.ds(pl.multiple_of(s * wide, wide), wide)
            target = whole.at[pl.ds(max(first, 0), span), at_rows, at_columns]
            copies.append(pltpu.make_async_copy(source.at[n, pl.ds(0, span)], target, sems.at[len(copies)]))
    return copies


def count_copies(plan):
    return sum(1 if offsets is None else len(offsets) for offsets, _ in plan)


def spread_table(small, rows, out):
    devices, wide = rows.shape
    for v, (start, each) in enumerate(small):
        length = devices * each
        place_of = lax.broadcasted_iota(jnp.int32, (wide, length), 1) % each + start
        pick = (place_of == lax.broadcasted_iota(jnp.int32, (wide, length), 0)).astype(BF)
        values = dot(rows, pick, NN)
        owner = lax.broadcasted_iota(jnp.int32, (devices, length), 1) // each
        row = lax.broadcasted_iota(jnp.int32, (devices, length), 0)
        own = owner == 2 * (row % (devices // 2)) + row // (devices // 2)
        out[v : v + 1, :length] = jnp.sum(jnp.where(own, values, 0.0), 0, keepdims=True)


def conv_kernel(subs, plan, small, flags, prev, x, nxt, *rest):
    block = pl.program_id(0)
    width = x.shape[1]
    border = prev.shape[0]
    sources = rest[: len(plan)]
    if small:
        xhat_out, scale_out, w_out, table, ext, col, w, sems, out_sem = rest[len(plan) :]
        small_rows = sources[0].shape[2]
    else:
        table, xhat_out, scale_out, w_out, ext, col, w, sems, out_sem = rest[len(plan) :]

    def copies_in():
        return place(plan, flags[4, 0], flags[4, 1], sources, w, sems)

    def whole_out():
        return pltpu.make_async_copy(w.at[pl.ds(0, KERNEL_TAPS)], w_out, out_sem)

    @pl.when(block == 0)
    def _():
        for copy in copies_in():
            copy.start()
        ext[0:border] = prev[...]
        ext[border : border + x.shape[0]] = x[...]
        ext[border + x.shape[0] :] = nxt[...]

        for copy in copies_in():
            copy.wait()
        whole_out().start()
        if small:
            blocks = width // small_rows
            first_row = lax.broadcasted_iota(jnp.int32, (blocks, width), 0) * small_rows
            pick = (first_row == lax.broadcasted_iota(jnp.int32, (blocks, width), 1)).astype(BF)
            rows = dot(pick, w[KERNEL_TAPS], NN).astype(BF)
            spread_table(small, jnp.concatenate([rows[:, : width // 2], rows[:, width // 2 :]], 0), table)

    @pl.when(block == pl.num_programs(0) - 1)
    def _():
        whole_out().wait()

    def load(start, count):
        return ext[pl.ds(pl.multiple_of(start + border, DILATION_STEP), count), :]

    fill_columns(col, load, flags, block, subs, width)
    total = None
    for k in range(KERNEL_TAPS):
        part = dot(col[:, k * width : (k + 1) * width], w[k], NT)
        total = part if total is None else total + part
    value, slope = gelu_pair(total + table[0:1, :width])
    centered = value - row_mean(value)
    rstd = lax.rsqrt(row_mean(centered * centered) + EPSILON)
    xhat_out[...] = centered * rstd
    scale_out[...] = slope * rstd


def whole_block(shape):
    return pl.BlockSpec(shape, lambda *_: (0,) * len(shape), pipeline_mode=pl.Buffered(1))


def conv_forward(flags, prev, x, nxt, sources, plan, small, table, subs, hidden):
    count, width = x.shape
    rows = subs * SUB
    anywhere = [pl.BlockSpec(memory_space=pl.ANY)] * len(sources)
    out_specs = [pl.BlockSpec((rows, width), lambda j, f: (j, 0))] * 2 + [pl.BlockSpec(memory_space=pltpu.HBM)]
    out_shape = [pltpu.HBM((count, width), F32)] * 2 + [pltpu.HBM((KERNEL_TAPS, width, width), BF)]
    scratch = [
        pltpu.VMEM((count + 2 * prev.shape[0], width), BF),
        pltpu.VMEM((rows, KERNEL_TAPS * width), BF),
        pltpu.VMEM((KERNEL_TAPS + bool(small), width, width), BF),
        pltpu.SemaphoreType.DMA((count_copies(plan),)),
        pltpu.SemaphoreType.DMA,
    ]
    extra_specs, extra = [], []
    if small:
        out_specs = out_specs + [whole_block((8, hidden))]
        out_shape = out_shape + [jax.ShapeDtypeStruct((8, hidden), F32)]
    else:
        extra_specs, extra = [whole_block(table.shape)], [table]
    outs = pl.pallas_call(
        functools.partial(conv_kernel, subs, plan, small),
        grid_spec=pltpu.PrefetchScalarGridSpec(
            num_scalar_prefetch=1,
            grid=(count // rows,),
            in_specs=[whole_block(prev.shape), whole_block(x.shape), whole_block(nxt.shape)] + anywhere + extra_specs,
            out_specs=out_specs,
            scratch_shapes=scratch,
        ),
        out_shape=out_shape,
        compiler_params=pltpu.CompilerParams(vmem_limit_bytes=VMEM_FIRST),
        cost_estimate=pl.CostEstimate(flops=1, bytes_accessed=1, transcendentals=0),
        name="conv_forward",
    )(flags, prev, x, nxt, *sources, *extra)
    return outs if small else (*outs, table)


def ffn_kernel(chunk, fast, plan, flags, x, xhat, scale, og, table, *rest):
    sources, rest = rest[: len(plan)], rest[len(plan) :]
    out, gh_out, gc_out, *rest = rest
    act, slope, dup, ddown, sums, ub_sums, pair, sems = rest[-8:]
    step = pl.program_id(0)
    last = pl.num_programs(0) - 1
    _, hidden, width = pair.shape
    chunks = hidden // chunk
    gain1, shift1, db, gain2, shift2 = (table[i : i + 1, :width] for i in range(1, 6))
    ub = table[6:7, :]

    @pl.when(step == 0)
    def _():
        copies = place(plan, flags[4, 0], flags[4, 1], sources, pair, sems)
        for copy in copies:
            copy.start()
        dup[...] = jnp.zeros_like(dup)
        ddown[...] = jnp.zeros_like(ddown)
        sums[...] = jnp.zeros_like(sums)
        ub_sums[...] = jnp.zeros_like(ub_sums)
        for copy in copies:
            copy.wait()

    one = x[...].astype(F32) + (xhat[...] * gain1 + shift1)
    low = one.astype(BF)
    total = None
    for f in range(chunks):
        cols = slice(f * chunk, (f + 1) * chunk)
        value, s = gelu_pair(dot(low, pair[0, cols, :], NT) + ub[:, cols])
        a = value.astype(BF)
        act[:, cols] = a
        slope[:, cols] = s
        part = dot(a, pair[1, cols, :], NN)
        total = part if total is None else total + part
    d = total + db
    centered = d - row_mean(d)
    rstd = lax.rsqrt(row_mean(centered * centered) + EPSILON)
    hat = centered * rstd
    out[...] = (one + (hat * gain2 + shift2)).astype(BF)
    g = og[...].astype(F32)
    e = g * gain2
    gd = (rstd * (e - row_mean(e) - hat * row_mean(e * hat))).astype(BF)
    sums[0] += fold(g * hat)
    sums[1] += fold(g)
    sums[2] += fold(gd.astype(F32))
    gh = g
    for f in range(chunks):
        cols = slice(f * chunk, (f + 1) * chunk)
        ddown[:, cols] += dot(gd, act[:, cols], TN)
        gu = dot(gd, pair[1, cols, :], NT) * slope[:, cols]
        gul = gu.astype(BF)
        ub_sums[:, cols] += fold(gul.astype(F32))
        dup[:, cols] += dot(low, gul, TN)
        gh = gh + dot(gul, pair[0, cols, :], NN)
    gh_out[...] = gh
    sums[3] += fold(gh * xhat[...])
    sums[4] += fold(gh)
    e = gh * gain1
    gc = (scale[...] * (e - row_mean(e) - xhat[...] * row_mean(e * xhat[...]))).astype(BF)
    gc_out[...] = gc
    if fast:
        edge = rest[0]
        border = edge.shape[0]

        @pl.when((step == 0) & (flags[4, 1] == 1))
        def _():
            edge[...] = gc[:border]

        @pl.when((step == last) & (flags[4, 1] == 0))
        def _():
            edge[...] = gc[gc.shape[0] - border :]

    sums[5] += fold(gc.astype(F32))

    @pl.when(step == last)
    def _():
        if not fast:
            up_out, down_out, sums_out, ub_out = rest[:4]
            up_out[...] = dup[...]
            down_out[...] = ddown[...]
            sums_out[...] = jnp.sum(sums[...], 1)
            ub_out[...] = jnp.sum(ub_sums[...], 0, keepdims=True)
            return
        send, keep = rest[1:3]
        mine = flags[3, 0] == 0
        block = send.shape[-1]
        half = width // 2
        devices = 2 * (hidden // block)

        def own(length):
            each = length // devices
            place = lax.broadcasted_iota(jnp.int32, (devices, length), 1) // each
            return place == lax.broadcasted_iota(jnp.int32, (devices, length), 0)

        def pick(length, start):
            each = length // devices
            place = lax.broadcasted_iota(jnp.int32, (length, 128), 0) % each + start
            return (place == lax.broadcasted_iota(jnp.int32, (length, 128), 1)).astype(BF)

        first = None
        for v in range(6):
            line = jnp.sum(sums[v], 0, keepdims=True)
            part = dot(jnp.where(own(width), line, 0.0).astype(BF), pick(width, v * (width // devices)), NN)
            first = part if first is None else first + part
        line = jnp.sum(ub_sums[...], 0, keepdims=True)
        second = dot(jnp.where(own(hidden), line, 0.0).astype(BF), pick(hidden, 0), NN)
        index = lax.broadcasted_iota(jnp.int32, (16, 128), 0)

        def tail(b, s):
            at = 2 * b + s
            return jnp.where(index == 0, first[at : at + 1], jnp.where(index == 1, second[at : at + 1], 0.0)).astype(BF)

        for b in range(0, hidden // block, 2):
            for s in range(2):
                take = slice(s * half, (s + 1) * half)
                x_bit, z = b // 2 % 2, (b // 4 % 2, b // 8)
                up_at, down_at = (2 * x_bit + s, *z), (2 * s + x_bit, *z)
                for acc, at, start in ((dup, up_at, 0), (ddown, down_at, half + 16)):
                    lo = acc[take, b * block : (b + 1) * block].astype(BF)
                    hi = acc[take, (b + 1) * block : (b + 2) * block].astype(BF)
                    send[(*at, slice(start, start + half))] = jnp.where(mine, hi, lo)
                    keep[(*at, slice(start, start + half))] = jnp.where(mine, lo, hi)
                lo, hi = tail(b, s), tail(b + 1, s)
                send[(*up_at, slice(half, half + 16))] = jnp.where(mine, hi, lo)
                keep[(*up_at, slice(half, half + 16))] = jnp.where(mine, lo, hi)


def ffn(flags, x, xhat, scale, og, table, sources, plan, rows, chunk, batch, fast):
    count, width = x.shape
    hidden = table.shape[1]
    tile = pl.BlockSpec((rows, width), lambda j, f: (j, 0))
    sds = jax.ShapeDtypeStruct
    if fast:
        border = KERNEL_TAPS // 2 * DILATION_STEP
        shapes = [sds((border, width), BF)] + [sds((4, 2, 2, width + 16, hidden // batch), BF)] * 2
    else:
        shapes = [sds(s, F32) for s in ((width, hidden), (width, hidden), (6, width), (1, hidden))]
    anywhere = [pl.BlockSpec(memory_space=pl.ANY)] * len(sources)
    return pl.pallas_call(
        functools.partial(ffn_kernel, chunk, fast, plan),
        grid_spec=pltpu.PrefetchScalarGridSpec(
            num_scalar_prefetch=1,
            grid=(count // rows,),
            in_specs=[tile, tile, tile, tile, whole_block(table.shape)] + anywhere,
            out_specs=[tile, tile, tile] + [whole_block(s.shape) for s in shapes],
            scratch_shapes=[
                pltpu.VMEM((rows, hidden), BF),
                pltpu.VMEM((rows, hidden), F32),
                pltpu.VMEM((width, hidden), F32),
                pltpu.VMEM((width, hidden), F32),
                pltpu.VMEM((6, 8, width), F32),
                pltpu.VMEM((8, hidden), F32),
                pltpu.VMEM((2, hidden, width), BF),
                pltpu.SemaphoreType.DMA((count_copies(plan),)),
            ],
        ),
        out_shape=[pltpu.HBM((count, width), BF), pltpu.HBM((count, width), F32), (pltpu.VMEM if fast else pltpu.HBM)((count, width), BF)] + shapes,
        compiler_params=pltpu.CompilerParams(vmem_limit_bytes=VMEM_FFN if fast else VMEM_PACK),
        cost_estimate=pl.CostEstimate(flops=12 * count * width * hidden // COST, bytes_accessed=2**20, transcendentals=0),
        name="feed_forward",
    )(flags, x, xhat, scale, og, table, *sources)


def conv_weight_kernel(fast, first, flags, prev, x, nxt, g, *rest):
    ext, col = rest[-2:]
    outs = rest[:-2] if first == 0 else rest[2:-2]
    tap = pl.program_id(0) + first
    count, width = g.shape
    border = prev.shape[0]
    subs = count // SUB

    @pl.when(tap == first)
    def _():
        ext[0:border] = prev[...]
        ext[border : border + count] = x[...]
        ext[border + count :] = nxt[...]

    o = (tap - KERNEL_TAPS // 2) * DILATION_STEP
    offset = lax.broadcasted_iota(jnp.int32, (SUB, 1), 0) + o
    for r in range(subs):
        own = flags[2, r].astype(F32)
        before = flags[0, r].astype(F32)
        after = flags[1, r].astype(F32)
        mask = jnp.where(offset < 0, before, jnp.where(offset >= SUB, after, own)).astype(BF)
        rows = ext[pl.ds(pl.multiple_of(r * SUB + o + border, DILATION_STEP), SUB), :]
        col[r * SUB : (r + 1) * SUB, :] = rows * mask

    grad = dot(g[...], col[...], TN)
    if not fast:
        outs[0][0] = grad
        return
    mine = flags[3, 0] == 0
    half = width // 2

    send, keep = outs
    block = send.shape[4]
    early = (tap < (KERNEL_TAPS + 1) // 2).astype(jnp.int32)
    for s in range(2):
        columns = slice(s * half, (s + 1) * half)
        for b in range(0, width // block, 2):
            bit = b // 2 % 2
            at = (early * (2 * bit + s) + (1 - early) * (2 * s + bit), b // 4 % 2, b // 8, 0)
            lo = grad[b * block : (b + 1) * block, columns].astype(BF)
            hi = grad[(b + 1) * block : (b + 2) * block, columns].astype(BF)
            send[at] = jnp.where(mine, hi, lo)
            keep[at] = jnp.where(mine, lo, hi)


def conv_weight_backward(flags, prev, x, nxt, g, batch, fast, first=0, taps=KERNEL_TAPS, into=()):
    count, width = x.shape
    if fast:
        block = (4, 2, 2, 1, width // batch, width // 2)
        specs = [pl.BlockSpec(block, lambda k, f: (0, 0, 0, k + first, 0, 0))] * 2
        shapes = [jax.ShapeDtypeStruct(block[:3] + (KERNEL_TAPS,) + block[4:], BF)] * 2
    else:
        specs = [pl.BlockSpec((1, width, width), lambda k, f: (k, 0, 0))]
        shapes = [jax.ShapeDtypeStruct((KERNEL_TAPS, width, width), F32)]
    return pl.pallas_call(
        functools.partial(conv_weight_kernel, fast, first),
        grid_spec=pltpu.PrefetchScalarGridSpec(
            num_scalar_prefetch=1,
            grid=(taps,),
            in_specs=[whole_block(a.shape) for a in (prev, x, nxt, g)] + [pl.BlockSpec(memory_space=pl.ANY)] * len(into),
            out_specs=specs,
            scratch_shapes=[
                pltpu.VMEM((count + 2 * prev.shape[0], width), BF),
                pltpu.VMEM((count, width), BF),
            ],
        ),
        out_shape=shapes,
        compiler_params=pltpu.CompilerParams(vmem_limit_bytes=VMEM_CONV),
        cost_estimate=conv_cost(count * taps // KERNEL_TAPS, width),
        input_output_aliases={5 + i: i for i in range(len(into))},
        name="conv_weight_backward",
    )(flags, prev, x, nxt, g, *into)


def conv_input_kernel(subs, flags, prev, g, nxt, gh, w, out, ext, col):
    step = pl.program_id(0)
    count, width = g.shape
    border = prev.shape[0]

    @pl.when(step == 0)
    def _():
        ext[0:border] = prev[...]
        ext[border : border + count] = g[...]
        ext[border + count :] = nxt[...]

    def load(start, size):
        return ext[pl.ds(pl.multiple_of(start + border, DILATION_STEP), size), :]

    fill_columns(col, load, flags, step, subs, width)
    total = gh[...]
    for k in range(KERNEL_TAPS):
        total = total + dot(col[:, k * width : (k + 1) * width], w[KERNEL_TAPS - 1 - k], NN)
    out[...] = total


def conv_input_backward(flags, prev, g, nxt, gh, weights, subs):
    count, width = g.shape
    rows = subs * SUB
    tile = pl.BlockSpec((rows, width), lambda j, f: (j, 0))
    return pl.pallas_call(
        functools.partial(conv_input_kernel, subs),
        grid_spec=pltpu.PrefetchScalarGridSpec(
            num_scalar_prefetch=1,
            grid=(count // rows,),
            in_specs=[whole_block(a.shape) for a in (prev, g, nxt)] + [tile, whole_block(weights.shape)],
            out_specs=tile,
            scratch_shapes=[
                pltpu.VMEM((count + 2 * prev.shape[0], width), BF),
                pltpu.VMEM((rows, KERNEL_TAPS * width), BF),
            ],
        ),
        out_shape=jax.ShapeDtypeStruct((count, width), F32),
        compiler_params=pltpu.CompilerParams(vmem_limit_bytes=VMEM_CONV),
        cost_estimate=conv_cost(count, width),
        name="conv_input_backward",
    )(flags, prev, g, nxt, gh, weights)


def pack_kernel(small, slots, count, lengths, first, final, conv, up, down, *rest):
    vectors, (flags, halo, conv_out, pair_out) = rest[: len(small)], rest[len(small) :]
    batch_index = lax.axis_index("z") * 4 + lax.axis_index("x") * 2 + lax.axis_index("core")
    seq_index = lax.axis_index("seq")
    taps, rows, wide = conv.shape
    subs = flags.shape[1]
    conv_out[0, 0:taps] = conv[...]
    line = None
    for v, (start, each) in zip(vectors, small):
        pick = (
            lax.broadcasted_iota(jnp.int32, (each, wide), 0) + start == lax.broadcasted_iota(jnp.int32, (each, wide), 1)
        ).astype(BF)
        part = dot(jnp.broadcast_to(v[...], (rows, each)), pick, NN)
        line = part if line is None else line + part
    conv_out[0, taps] = line.astype(BF)
    pair_out[0, 0] = up[...].T
    pair_out[0, 1] = down[...]
    halo[...] = jnp.where(seq_index == 0, final[...], first[...])
    ends = []
    total = 0
    for i in range(slots):
        total = total + lengths[0, i]
        ends.append(total)
    ids = []
    for j in range(-1, subs + 1):
        start = seq_index * count + j * SUB
        number = 0
        for end in ends:
            number = number + (start >= end).astype(jnp.int32)
        ids.append(jnp.where(start >= 0, number, -1))
    for j in range(subs):
        inside = (ids[j + 1] < slots).astype(jnp.int32)
        flags[0, j] = (ids[j] == ids[j + 1]).astype(jnp.int32) * inside
        flags[1, j] = (ids[j + 2] == ids[j + 1]).astype(jnp.int32) * inside
        flags[2, j] = inside
        flags[3, j] = batch_index % 2
        flags[4, j] = batch_index if j == 0 else seq_index
        bits = (lax.axis_index("x"), seq_index, lax.axis_index("z") % 2, lax.axis_index("z") // 2)
        flags[5, j] = bits[min(j, 3)]


def pack(lengths, x, conv, up, down, vectors, small):
    taps, rows, wide = conv.shape
    count, width = x.shape
    border = KERNEL_TAPS // 2 * DILATION_STEP
    smem = pl.BlockSpec(memory_space=pltpu.SMEM)
    arrays = [conv, up, down] + [v[None] for v in vectors]
    end_rows = pl.BlockSpec((border, width), lambda i: (0, 0))
    final_rows = pl.BlockSpec((border, width), lambda i: (count // border - 1, 0))
    sds = jax.ShapeDtypeStruct
    outs = [
        sds((6, count // SUB), jnp.int32),
        sds((border, width), BF),
        pltpu.VMEM((1, taps + 1, rows, wide), BF),
        sds((1, 2) + down.shape, BF),
    ]
    return pl.pallas_call(
        functools.partial(pack_kernel, small, lengths.shape[1], count),
        grid=(1,),
        in_specs=[smem, end_rows, final_rows] + [whole_block(a.shape) for a in arrays],
        out_specs=[smem] + [whole_block(o.shape) for o in outs[1:]],
        out_shape=outs,
        compiler_params=pltpu.CompilerParams(vmem_limit_bytes=VMEM_PACK),
        name="pack",
    )(lengths, x, x, *arrays)


def swap(value, link):
    axis, bit = link
    return lax.ppermute(value, axis, [(i, i ^ bit) for i in range(lax.axis_size(axis))])


def half_of(link):
    return (lax.axis_index(link[0]) // link[1]) % 2


def give_half(value, link, dim):
    return lax.dynamic_index_in_dim(value, 1 - half_of(link), dim, keepdims=False).astype(BF)


def keep_half(value, link, dim):
    return lax.dynamic_index_in_dim(value, half_of(link), dim, keepdims=False).astype(F32)


def after(value, *others):
    return lax.optimization_barrier((value, *others))[0]


def shifted(offsets, b, s):
    return tuple((ob ^ b, os ^ s) for ob, os in offsets)


def both_cores(arrays, plan):
    other = [swap(a, CORE) for a in arrays]
    return arrays + other, tuple(plan) + tuple((shifted(o, 1, 0), first) for o, first in plan)


def gather(own, pair, halo):
    cut = own.shape[1] // 2
    top = lambda value: swap(value[:, :cut], Y)
    bottom = lambda value: swap(value[:, cut:], X)
    own_y, own_x, far = lax.optimization_barrier((swap(own, Y), swap(own, X), swap(own, Z1)))
    column = jnp.concatenate([own, far], 0)
    near, far_x, far_y, own_top, own_bottom = lax.optimization_barrier(
        (swap(column, Z0), swap(far, X), swap(far, Y), top(own_x), bottom(own_y))
    )
    pair = after(pair, near, own_top)
    near_y, near_x, far_top, far_bottom, pair_far = lax.optimization_barrier(
        (swap(near, Y), swap(near, X), top(far_x), bottom(far_y), swap(pair, Z1))
    )
    pair_far, near_x, near_y = lax.optimization_barrier((pair_far, near_x, near_y))
    halo = swap(after(halo, near_x), Y)
    near_top, near_bottom = top(near_x), bottom(near_y)
    pair = jnp.concatenate([pair, pair_far], 0)
    pair = jnp.concatenate([pair, swap(pair, Z0)], 0)
    pair_x, pair_y = swap(pair, X), swap(pair, Y)
    across = lax.ppermute(pair, ("x", "seq"), [(i, i ^ 3) for i in range(4)])
    offsets = ((0, 0), (8, 0), (4, 0), (12, 0))
    pair_plan = [(shifted(offsets, b, s), 0) for b, s in ((0, 0), (2, 0), (0, 1), (2, 1))]
    arrays, plan = [column, near], [(((0, 0), (8, 0)), 0), (((4, 0), (12, 0)), 0)]
    for offsets, members in (
        (((0, 0),), (own_x, own_y, own_top, own_bottom)),
        (((8, 0),), (far_x, far_y, far_top, far_bottom)),
        (((4, 0), (12, 0)), (near_x, near_y, near_top, near_bottom)),
    ):
        arrays += members
        plan += [(shifted(offsets, b, s), first) for b, s, first in ((2, 0, 0), (0, 1, 0), (2, 1, 0), (2, 1, cut))]
    return halo, both_cores(arrays, plan), ([pair, pair_x, pair_y, across], pair_plan)


def stage_kernel(columns, joined, flags, *refs):
    count = len(columns)
    outs = refs[2 * count :]
    at = 0
    for i, column in enumerate(columns):
        keep, got = refs[2 * i], refs[2 * i + 1]
        if joined is None:
            give_out, keep_out, where = outs[2 * i], outs[2 * i + 1], Ellipsis
        else:
            taps = keep.shape[1 + joined]
            give_out, keep_out = outs
            where = (*(slice(None),) * joined, slice(at, at + taps))
            at += taps
        bit = flags[5, column]
        give_out[where] = (keep[1 - bit].astype(F32) + got[1 - bit].astype(F32)).astype(BF)
        keep_out[where] = keep[bit].astype(F32) + got[bit].astype(F32)


def first_stage_kernel(cut, flags, keep, got, *outs):
    for i, taps in enumerate((slice(0, cut), slice(cut, keep.shape[3]))):
        bit = flags[5, i]
        give_out, keep_out = outs[2 * i], outs[2 * i + 1]
        for n in range(2):
            other, own = 2 * (1 - bit) + n, 2 * bit + n
            give_out[n] = (keep[other, :, :, taps].astype(F32) + got[other, :, :, taps].astype(F32)).astype(BF)
            keep_out[n] = keep[own, :, :, taps].astype(F32) + got[own, :, :, taps].astype(F32)


def first_stage(flags, keep, got, cut):
    tail = keep.shape[4:]
    outs = [jax.ShapeDtypeStruct((2, 2, 2, n) + tail, kind) for n in (cut, keep.shape[3] - cut) for kind in (BF, F32)]
    return pl.pallas_call(
        functools.partial(first_stage_kernel, cut),
        grid_spec=pltpu.PrefetchScalarGridSpec(
            num_scalar_prefetch=1,
            grid=(1,),
            in_specs=[whole_block(keep.shape)] * 2,
            out_specs=[whole_block(o.shape) for o in outs],
        ),
        out_shape=outs,
        compiler_params=pltpu.CompilerParams(vmem_limit_bytes=VMEM_SUM),
        name="stage",
    )(flags, keep, got)


def stage(flags, parts, columns, joined=None):
    shapes = [keep.shape[1:] for keep, _ in parts]
    if joined is not None:
        first = list(shapes[0])
        first[joined] = sum(shape[joined] for shape in shapes)
        shapes = [tuple(first)]
    outs = [jax.ShapeDtypeStruct(shape, kind) for shape in shapes for kind in (BF, F32)]
    arrays = [a for part in parts for a in part]
    return pl.pallas_call(
        functools.partial(stage_kernel, columns, joined),
        grid_spec=pltpu.PrefetchScalarGridSpec(
            num_scalar_prefetch=1,
            grid=(1,),
            in_specs=[whole_block(a.shape) for a in arrays],
            out_specs=[whole_block(o.shape) for o in outs],
        ),
        out_shape=outs,
        compiler_params=pltpu.CompilerParams(vmem_limit_bytes=VMEM_SUM),
        name="stage",
    )(flags, *arrays)


def local(inputs, window_lengths, conv_weight, conv_bias, norm1_gain, norm1_bias, up_weight, up_bias, down_weight,
          down_bias, norm2_gain, norm2_bias, out_grad):
    _, count, width = inputs.shape
    batch, seq = lax.axis_size(BATCH), lax.axis_size("seq")
    hidden = up_weight.shape[1] * batch
    border = KERNEL_TAPS // 2 * DILATION_STEP
    x, og = inputs[0], pltpu.with_memory_space_constraint(out_grad[0], pltpu.HBM)
    fast = seq == 2 and batch == 16

    def ends(value):
        first, final = value[:border], value[count - border :]
        if fast:
            other = swap(jnp.where(lax.axis_index("seq") == 0, final, first), Y)
            return other, other
        up = [(i, i + 1) for i in range(seq - 1)]
        return lax.ppermute(final, "seq", up), lax.ppermute(first, "seq", [(j, i) for i, j in up])

    vectors = [conv_bias, norm1_gain, norm1_bias, down_bias, norm2_gain, norm2_bias, up_bias]
    sizes = [v.shape[0] for v in vectors]
    small = tuple((sum(sizes[:i]), n) for i, n in enumerate(sizes))
    conv_own = conv_weight.transpose(0, 2, 1)
    flags, halo, conv_block, pair_block = pack(window_lengths, x, conv_own, up_weight, down_weight, vectors, small)
    if fast:
        halo, (conv_pieces, conv_plan), (pair_pieces, pair_plan) = gather(conv_block, pair_block, halo)
        prev = nxt = halo
        table = None
    else:
        def every(value):
            value = lax.all_gather(value, "seq", axis=2, tiled=True)
            return lax.all_gather(value, BATCH, axis=1, tiled=True)

        prev, nxt = ends(x)
        conv_pieces, conv_plan = [every(conv_own)], ((None, 0),)
        pair_pieces, pair_plan = [every(pair_block[0])], ((None, 0),)
        full = [lax.all_gather(v, (*BATCH, "seq"), axis=0, tiled=True).astype(F32) for v in vectors]
        table = jnp.stack([jnp.pad(v, (0, hidden - v.shape[0])) for v in full + [full[0]]])
        small = ()
    conv_pieces, conv_plan = list(conv_pieces), tuple((None if o is None else tuple(o), f) for o, f in conv_plan)
    xhat, scale, conv_full, table = conv_forward(flags, prev, x, nxt, conv_pieces, conv_plan, small, table, 2, hidden)
    if fast:
        pair_pieces, table = lax.optimization_barrier((pair_pieces, table))
        pair_pieces, pair_plan = both_cores(pair_pieces, pair_plan)
    pair_plan = tuple((None if o is None else tuple(o), f) for o, f in pair_plan)
    block_output, grad_hidden, grad_conv, *ffn_grads = ffn(
        flags, x, xhat, scale, og, table, pair_pieces, pair_plan, 2 * SUB, min(1024, hidden), batch, fast
    )
    grads = (flags, prev, x, nxt, grad_conv, grad_hidden, conv_full)
    if fast:
        input_grad, weight_grads = paired(grads, ffn_grads, batch, width, hidden)
    else:
        grad_prev, grad_next = ends(grad_conv)
        conv_grads = conv_weight_backward(flags, prev, x, nxt, grad_conv, batch, fast)
        input_grad = conv_input_backward(flags, grad_prev, grad_conv, grad_next, grad_hidden, conv_full, 2)
        weight_grads = whole_sums(conv_grads, ffn_grads, batch, seq, width, hidden)
    conv_grad, cb, g1, s1, up_grad, ub_grad, down_grad, db, g2, s2 = weight_grads
    return (block_output[None], input_grad[None], conv_grad, cb, g1, s1, up_grad, ub_grad, down_grad, db, g2, s2)


def paired(grads, ffn_grads, batch, width, hidden):
    flags, prev, x, nxt, grad_conv, grad_hidden, conv_full = grads
    up_rows = width // 2 + 16
    edge, ffn_send, ffn_keep = ffn_grads
    ffn_got, grad_prev = swap(ffn_send, CORE), swap(edge, Y)
    early = 2
    parts = conv_weight_backward(flags, prev, x, prev, grad_conv, batch, True, 0, early)
    ffn_got, grad_prev, parts = lax.optimization_barrier((ffn_got, grad_prev, parts))
    up_give, up_keep, down_give, down_keep = first_stage(flags, ffn_keep, ffn_got, up_rows)
    up_got, down_got = swap(up_give, X), swap(down_give, Y)
    first = after(prev, up_give)
    send, keep = conv_weight_backward(
        flags, first, x, first, grad_conv, batch, True, early, KERNEL_TAPS - early, parts
    )
    up_got, down_got, send = lax.optimization_barrier((up_got, down_got, send))
    got = swap(send, CORE)
    parts = [(up_keep, up_got), (down_keep, down_got)]
    up_give, up_keep, down_give, down_keep = stage(flags, parts, (1, 0))
    up_got, down_got = swap(up_give, Y), swap(down_give, X)
    upper_give, upper_keep, lower_give, lower_keep = first_stage(
        flags, keep, after(got, up_give), (KERNEL_TAPS + 1) // 2
    )
    upper_got, lower_got = swap(upper_give, X), swap(lower_give, Y)
    second = after(grad_prev, upper_give)
    input_grad = conv_input_backward(flags, second, grad_conv, second, grad_hidden, conv_full, 2)
    up_got, down_got, input_grad = lax.optimization_barrier((up_got, down_got, input_grad))
    ffn_give, ffn_keep = stage(flags, [(up_keep, up_got), (down_keep, down_got)], (2, 2), 1)
    ffn_got = swap(ffn_give, Z0)
    upper_got, lower_got, _ = lax.optimization_barrier((upper_got, lower_got, ffn_give))
    parts = [(upper_keep, upper_got), (lower_keep, lower_got)]
    upper_give, upper_keep, lower_give, lower_keep = stage(flags, parts, (1, 0))
    upper_got, lower_got = swap(upper_give, Y), swap(lower_give, X)
    ffn_give, ffn_keep = stage(flags, [(ffn_keep, after(ffn_got, upper_give))], (3,))
    ffn_got = swap(ffn_give, Z1)
    upper_got, lower_got, _ = lax.optimization_barrier((upper_got, lower_got, ffn_give))
    conv_give, conv_keep = stage(flags, [(upper_keep, upper_got), (lower_keep, lower_got)], (2, 2), 1)
    conv_got = swap(conv_give, Z0)
    pair_part = ffn_keep + after(ffn_got, conv_give).astype(F32)
    conv_give, conv_keep = stage(flags, [(conv_keep, conv_got)], (3,))
    conv_got = swap(conv_give, Z1)
    conv_grad = (conv_keep + conv_got.astype(F32)).transpose(0, 2, 1)
    head = width // 2
    up_grad = pair_part[:head]
    down_grad = pair_part[up_rows:].T
    each = width // (batch * 2)
    g2, s2, db, g1, s1, cb = (pair_part[head, i * each : (i + 1) * each] for i in range(6))
    ub_grad = pair_part[head + 1, : hidden // (batch * 2)]
    return input_grad, (conv_grad, cb, g1, s1, up_grad, ub_grad, down_grad, db, g2, s2)


def whole_sums(conv_grads, ffn_grads, batch, seq, width, hidden):
    def total(value, dims):
        value = lax.psum_scatter(value, BATCH, scatter_dimension=dims[1], tiled=True)
        return lax.psum_scatter(value, "seq", scatter_dimension=dims[0], tiled=True)

    conv_grad = total(conv_grads[0], (2, 1)).transpose(0, 2, 1)
    up_grad = total(ffn_grads[0], (0, 1))
    down_grad = total(ffn_grads[1], (0, 1)).T
    vec_grads = total(ffn_grads[2].reshape(6, batch, seq, -1), (2, 1)).reshape(6, -1)
    ub_grad = total(ffn_grads[3].reshape(batch, seq, -1), (1, 0)).reshape(-1)
    g2, s2, db, g1, s1, cb = (vec_grads[i] for i in range(6))
    return conv_grad, cb, g1, s1, up_grad, ub_grad, down_grad, db, g2, s2


def solution(mesh):
    batch, seq = mesh.shape["batch"], mesh.shape["seq"]
    split = Mesh(mesh.devices.reshape(batch // 4, 2, 2, seq), (*BATCH, "seq"))
    both = P((*BATCH, "seq"))
    rows = P(BATCH, "seq", None)
    conv, up, down = P(None, "seq", BATCH), P("seq", BATCH), P(BATCH, "seq")
    in_specs = (rows, P(BATCH, None), conv, both, both, both, up, both, down, both, both, both, rows)
    out_specs = (rows, rows, conv, both, both, both, up, both, down, both, both, both)
    return jax.shard_map(local, mesh=split, in_specs=in_specs, out_specs=out_specs, check_vma=False)
```
